32 devices in a mesh: set: 1, kb: 32 (over z, y, x, core).
Axes of the slice: x: 2, y: 2, z: 4, core: 2. Of those that a mesh axis runs over, the one named last changes fastest.
Arguments:
- green_momentum_grid: float32 [2, 4, 4096, 512], P('set', None, 'kb'), may hold values from -6 to 6
- pair_table: int32 [8, 2], replicated, may hold values from 0 to 3, as said below
- mirror_map: int32 [3, 16], P('set'), may hold values from 0 to 15, as said below
Outputs:
- chi_out: float32 [2, 8, 4096, 512], P('set', None, 'kb')
The draws below stay inside these ranges and needn't reach their ends.
Inputs may be any that keep to these rules, and one draw needn't show every extreme that they name: `pair_table`: each of the two columns names every entry number 0 to 3 at least once. Each row d is a reflection: mirror_map[d,x] = (c_d - x) mod 16 for a centre c_d of that row.
All inputs are finite; a program needn't handle non-finite values.
Results may differ from the reference program's by a relative error of at most 0.0003.
Values sent between devices are 32-bit elements; how exact they have to be, the bound alone decides.
A program may use at most 128 MiB of HBM per device.

```python
import math
import jax
import jax.numpy as jnp
from jax import lax

SIDE = 16
KPTS = 4096
NFREQ = 512
NENT = 4
NCHI = 8


def draw_pair_table(key, part):
    column_one = jax.random.permutation(jax.random.fold_in(key, 11), jnp.arange(NCHI, dtype=jnp.int32) % NENT)
    column_two = jax.random.permutation(jax.random.fold_in(key, 12), jnp.arange(NCHI, dtype=jnp.int32) % NENT)
    return jnp.stack([column_one, column_two], axis=1).astype(jnp.int32)


def draw_mirror_map(key, part):
    centres = jax.random.randint(jax.random.fold_in(key, 21), (3,), 0, SIDE, dtype=jnp.int32)
    coords = jnp.arange(SIDE, dtype=jnp.int32)
    return ((centres[:, None] - coords[None, :]) % SIDE).astype(jnp.int32)


def steps_of(stream_key, shape, pieces, least, high):
    gain = 1.0
    for dim, shards_of in pieces:
        steps = jax.random.uniform(jax.random.fold_in(jax.random.fold_in(stream_key, 6), dim), (shards_of,), jnp.float32, least / len(pieces), high / len(pieces))
        gain = gain * jnp.repeat(jnp.exp(steps), shape[dim] // shards_of).reshape((-1,) + (1,) * (len(shape) - 1 - dim))
    return gain


def gaussian(rng, shape, width, limit, cuts=(), kind=jnp.bfloat16):
    result = jax.random.normal(rng, shape, jnp.float32) * width
    if len(cuts) > 0:
        result = steps_of(rng, shape, cuts, -0.22, 0.18) * result
    return jnp.clip(result, min=-limit, max=limit).astype(kind)


def setup_inputs(seed: int = 0, part: int = 0) -> dict:
    key_of = jax.random.split(jax.random.key(seed), 4)
    own_keys = jax.random.split(jax.random.fold_in(key_of[3], part), 4)
    green_momentum_grid = gaussian(own_keys[0], (2, NENT, KPTS, NFREQ), 1.0, 6.0, ((2, 32),), jnp.float32)
    pair_table = draw_pair_table(jax.random.fold_in(key_of[3], 71), part)
    mirror_map = draw_mirror_map(jax.random.fold_in(jax.random.fold_in(key_of[3], part), 71), part)
    return {"green_momentum_grid": green_momentum_grid, "pair_table": pair_table, "mirror_map": mirror_map}


def trig_pair(angle_int, period, scale):
    angle = (2.0 * math.pi / period) * angle_int.astype(jnp.float32)
    return scale * jnp.cos(angle), scale * jnp.sin(angle)


def complex_combine(formula, cosine, sine, real_part, imag_part):
    first_term = jnp.einsum(formula, cosine, real_part + imag_part, precision=lax.Precision.HIGHEST)
    second_term = jnp.einsum(formula, cosine + sine, imag_part, precision=lax.Precision.HIGHEST)
    third_term = jnp.einsum(formula, sine - cosine, real_part, precision=lax.Precision.HIGHEST)
    return first_term - second_term, first_term + third_term


def forward_imaginary_time(tau_rows, frequency_count):
    freq_index = jnp.arange(frequency_count, dtype=jnp.int32)
    angle_int = ((2 * freq_index[None, :] - frequency_count + 1) * (2 * tau_rows[:, None] + 1)) % (4 * frequency_count)
    cosine, sine = trig_pair(angle_int, 4 * frequency_count, frequency_count ** -0.5)
    return cosine, -sine


def tau_backward(tau_rows, frequency_count):
    freq_index = jnp.arange(frequency_count, dtype=jnp.int32)
    angle_int = ((freq_index[:, None] - frequency_count // 2) * (2 * tau_rows[None, :] + 1)) % (2 * frequency_count)
    return trig_pair(angle_int, 2 * frequency_count, frequency_count ** -0.5)


def grid_transform(real_part, imag_part, grid_side, direction):
    shape = real_part.shape
    plane = jnp.arange(grid_side * grid_side, dtype=jnp.int32)
    upper = plane // grid_side
    lower = plane % grid_side
    plane_int = (upper[:, None] * upper[None, :] + lower[:, None] * lower[None, :]) % grid_side
    plane_cos, plane_sin = trig_pair(plane_int, grid_side, 1.0 / grid_side)
    line = jnp.arange(grid_side, dtype=jnp.int32)
    line_cos, line_sin = trig_pair((line[:, None] * line[None, :]) % grid_side, grid_side, grid_side ** -0.5)
    real_part = real_part.reshape(shape[:-1] + (grid_side, grid_side * grid_side))
    imag_part = imag_part.reshape(shape[:-1] + (grid_side, grid_side * grid_side))
    real_part, imag_part = complex_combine('pq,...xq->...xp', plane_cos, direction * plane_sin, real_part, imag_part)
    real_part, imag_part = complex_combine('ax,...xp->...ap', line_cos, direction * line_sin, real_part, imag_part)
    return real_part.reshape(shape), imag_part.reshape(shape)


def mirror_index(mirror_map, grid_side):
    index_x = mirror_map[0][:, None, None]
    index_y = mirror_map[1][None, :, None]
    index_z = mirror_map[2][None, None, :]
    return (index_x * grid_side * grid_side + index_y * grid_side + index_z).reshape(-1).astype(jnp.int32)


def bubble(gr_re, gr_im, mirror_re, mirror_im, pair_table, entries):
    entry_ids = jnp.arange(entries, dtype=jnp.int32)
    pick_left = (pair_table[:, 0][:, None] == entry_ids[None, :]).astype(jnp.float32)
    pick_right = (pair_table[:, 1][:, None] == entry_ids[None, :]).astype(jnp.float32)
    left_re = jnp.einsum('me,e...->m...', pick_left, gr_re, precision=lax.Precision.HIGHEST)
    left_im = jnp.einsum('me,e...->m...', pick_left, gr_im, precision=lax.Precision.HIGHEST)
    right_re = jnp.einsum('me,e...->m...', pick_right, mirror_re, precision=lax.Precision.HIGHEST)
    right_im = jnp.einsum('me,e...->m...', pick_right, mirror_im, precision=lax.Precision.HIGHEST)
    return left_re * right_re - left_im * right_im, left_re * right_im + left_im * right_re


def reference(green_momentum_grid, pair_table, mirror_map):
    tau_rows = jnp.arange(NFREQ, dtype=jnp.int32)
    fwd_cos, fwd_sin = forward_imaginary_time(tau_rows, NFREQ)
    tau_re, tau_im = complex_combine('qa,fsa->fqs', fwd_cos, fwd_sin, green_momentum_grid[0], green_momentum_grid[1])
    mirror_flat = mirror_index(mirror_map, SIDE)

    def one_time(time_index):
        other_index = (NFREQ - 1 - time_index).astype(jnp.int32)
        here_re = lax.dynamic_index_in_dim(tau_re, time_index, 1, keepdims=False)
        here_im = lax.dynamic_index_in_dim(tau_im, time_index, 1, keepdims=False)
        there_re = lax.dynamic_index_in_dim(tau_re, other_index, 1, keepdims=False)
        there_im = lax.dynamic_index_in_dim(tau_im, other_index, 1, keepdims=False)
        here_re, here_im = grid_transform(here_re, here_im, SIDE, 1.0)
        there_re, there_im = grid_transform(there_re, there_im, SIDE, 1.0)
        there_re = jnp.take(there_re, mirror_flat, axis=1)
        there_im = jnp.take(there_im, mirror_flat, axis=1)
        chi_re, chi_im = bubble(here_re, here_im, there_re, there_im, pair_table, NENT)
        chi_re, chi_im = grid_transform(chi_re, chi_im, SIDE, -1.0)
        return jnp.stack([chi_re, chi_im])

    momenta = lax.map(one_time, jnp.arange(NFREQ, dtype=jnp.int32))
    momenta = jnp.transpose(momenta, (1, 2, 0, 3))
    back_cos, back_sin = tau_backward(tau_rows, NFREQ)
    out_re, out_im = complex_combine('vj,ejk->ekv', back_cos, back_sin, momenta[0], momenta[1])
    return jnp.stack([out_re, out_im])
```

```python
import functools

import numpy as np
import ml_dtypes
import jax
import jax.numpy as jnp
from jax import lax
from jax.experimental import pallas as pl
from jax.experimental.pallas import tpu as pltpu
from jax.sharding import PartitionSpec as P

CHUNKS = 2
SMEM = pl.BlockSpec(memory_space=pltpu.SMEM)


def split_np(table):
    table = table.astype(np.float32)
    high = table.astype(ml_dtypes.bfloat16)
    low = (table - high.astype(np.float32)).astype(ml_dtypes.bfloat16)
    return high, low


def split(x):
    high = x.astype(jnp.bfloat16)
    return high, (x - high.astype(jnp.float32)).astype(jnp.bfloat16)


def mm(a, b, dims):
    return lax.dot_general(a, b, (dims, ((), ())), preferred_element_type=jnp.float32)


def mm3(a, b, dims=((1,), (0,))):
    return mm(a[0], b[0], dims) + mm(a[1], b[0], dims) + mm(a[0], b[1], dims)


def owned_times(devices, freqs, chunk):
    per = freqs // (2 * CHUNKS * devices)
    first = chunk * (freqs // (2 * CHUNKS)) + np.arange(devices)[:, None] * per + np.arange(per)[None, :]
    return np.stack([first, freqs - 1 - first], axis=1).reshape(-1)


def time_tables(times, freqs):
    angle = ((2 * np.arange(freqs)[None, :] - freqs + 1) * (2 * times[:, None] + 1)) % (4 * freqs)
    angle = angle * (2 * np.pi / (4 * freqs))
    scale = freqs**-0.5
    return split_np(scale * np.cos(angle)) + split_np(scale * np.sin(angle))


def frequency_tables(times, freqs):
    angle = ((np.arange(freqs)[None, :] - freqs // 2) * (2 * times[:, None] + 1)) % (2 * freqs)
    angle = angle * (2 * np.pi / (2 * freqs))
    cos, sin = np.cos(angle) * freqs**-0.5, np.sin(angle) * freqs**-0.5
    return split_np(np.block([[cos, sin], [-sin, cos]]))


def plane_table(side, sign):
    index = np.arange(side * side)
    upper, lower = index // side, index % side
    angle = (upper[:, None] * upper[None, :] + lower[:, None] * lower[None, :]) % side * (2 * np.pi / side)
    scale = (side**3) ** -0.5
    cos, sin = scale * np.cos(angle), sign * scale * np.sin(angle)
    return split_np(np.block([[cos, sin], [-sin, cos]]))


def cadd(a, b):
    return a[0] + b[0], a[1] + b[1]


def csub(a, b):
    return a[0] - b[0], a[1] - b[1]


def dft4(a, sign):
    s02, d02 = cadd(a[0], a[2]), csub(a[0], a[2])
    s13, d13 = cadd(a[1], a[3]), csub(a[1], a[3])
    turned = (-d13[1], d13[0]) if sign > 0 else (d13[1], -d13[0])
    return [cadd(s02, s13), cadd(d02, turned), csub(s02, s13), csub(d02, turned)]


def twiddle(a, power, sign):
    if power == 0:
        return a
    if power == 4:
        return (-a[1], a[0]) if sign > 0 else (a[1], -a[0])
    if power in (2, 6):
        r = np.float32(np.sqrt(0.5))
        plus, minus = (a[0] + a[1]) * r, (a[0] - a[1]) * r
        if power == 2:
            return (minus, plus) if sign > 0 else (plus, -minus)
        return (-plus, minus) if sign > 0 else (-minus, -plus)
    c = np.float32(np.cos(2 * np.pi * power / 16))
    s = np.float32(sign * np.sin(2 * np.pi * power / 16))
    return a[0] * c - a[1] * s, a[0] * s + a[1] * c


def dft16(x, sign):
    columns = [dft4([x[4 * n1 + n2] for n1 in range(4)], sign) for n2 in range(4)]
    out = [None] * 16
    for k1 in range(4):
        row = dft4([twiddle(columns[n2][k1], n2 * k1, sign) for n2 in range(4)], sign)
        for k2 in range(4):
            out[k1 + 4 * k2] = row[k2]
    return out


def to_time(g_ref, table, o_ref, p):
    devices, _, entries, slots, points = o_ref.shape[1:]
    freqs = g_ref.shape[-1]
    cos, sin = (table[p, 0], table[p, 1]), (table[p, 2], table[p, 3])
    dims = ((1,), (1,))
    re = split(g_ref[0].reshape(entries * points, freqs))
    im = split(g_ref[1].reshape(entries * points, freqs))
    tau = (mm3(cos, re, dims) + mm3(sin, im, dims), mm3(cos, im, dims) - mm3(sin, re, dims))
    for part in range(2):
        for e in range(entries):
            o_ref[p, :, part, e] = tau[part][:, e * points:(e + 1) * points].reshape(devices, slots, points)


def bubble(pair_ref, mirror_ref, x_ref, ahead, mirrored, inverse, o_ref, y, g, gm, chi, p):
    devices, _, entries, slots, points = x_ref.shape[1:]
    side = y.shape[0]
    plane = side * side
    halves = devices // side
    comps = o_ref.shape[3]

    def forth(e, carry):
        for h in range(halves):
            cells = [(x_ref[p, k * halves + h, 0, e], x_ref[p, k * halves + h, 1, e]) for k in range(side)]
            for k, (re, im) in enumerate(dft16(cells, 1)):
                y[k, e, :, h * points:(h + 1) * points] = re
                y[k, e, :, plane + h * points:plane + (h + 1) * points] = im
        return carry

    lax.fori_loop(0, entries, forth, 0)
    rows = split(y[...].reshape(side * entries * slots, 2 * plane))
    g[...] = mm3(rows, (ahead[0], ahead[1])).reshape(g.shape)
    other = mm3(rows, (mirrored[0], mirrored[1])).reshape(side * entries, slots, 2 * plane)
    other = jnp.concatenate([other[:, slots // 2:], other[:, :slots // 2]], axis=1)
    gm[...] = other.reshape(gm.shape)

    def one(c, carry):
        left, right = pair_ref[0, c], pair_ref[1, c]
        for r in range(side):
            a = g[r, left]
            b = gm[mirror_ref[0, r], right]
            ar, ai, br, bi = a[:, :plane], a[:, plane:], b[:, :plane], b[:, plane:]
            chi[c, r, :, :plane] = ar * br - ai * bi
            chi[c, r, :, plane:] = ar * bi + ai * br
        return carry

    lax.fori_loop(0, comps, one, 0)
    rows = split(chi[...].reshape(comps * side * slots, 2 * plane))
    chi[...] = mm3(rows, (inverse[0], inverse[1])).reshape(chi.shape)

    def back(c, carry):
        for h in range(halves):
            lanes = slice(h * points, (h + 1) * points)
            high = slice(plane + h * points, plane + (h + 1) * points)
            cells = [(chi[c, r, :, lanes], chi[c, r, :, high]) for r in range(side)]
            for q, (re, im) in enumerate(dft16(cells, -1)):
                o_ref[p, q * halves + h, 0, c] = re
                o_ref[p, q * halves + h, 1, c] = im
        return carry

    lax.fori_loop(0, comps, back, 0)


def main_kernel(pair_ref, mirror_ref, green_hbm, time_hbm, plane_hbm, back_hbm, half_hbm, last,
                green, table, planes, back, mirrored, tau, x, y, g, gm, chi, sent, got, acc,
                load, own, send, recv):
    devices = tau.shape[1]
    side = y.shape[0]
    plane = side * side
    me = lax.axis_index("kb")
    loads = [pltpu.make_async_copy(src, dst, load.at[i])
             for i, (src, dst) in enumerate([(time_hbm, table), (plane_hbm, planes), (back_hbm, back),
                                       (green_hbm, green)])]
    for i in (3, 0, 1, 2):
        loads[i].start()
    barrier = pltpu.get_barrier_semaphore()

    def greet(s, carry):
        pl.semaphore_signal(barrier, inc=1, device_id={"kb": lax.rem(me + s, devices)},
                            device_id_type=pl.DeviceIdType.MESH)
        return carry

    lax.fori_loop(1, devices, greet, 0)

    def partner(shift):
        total, bit = 0, 1
        while bit < devices:
            total += bit * lax.rem(me // bit + shift // bit, 2)
            bit *= 2
        return total

    def exchange(src, dst, n):
        pltpu.make_async_copy(src.at[me], dst.at[me], own.at[n]).start()

        def one(i, carry):
            other = partner(i // 4 + devices // 4 * lax.rem(i + 2, 4))
            pltpu.make_async_remote_copy(
                src_ref=src.at[other], dst_ref=dst.at[me], send_sem=send.at[n], recv_sem=recv.at[n],
                device_id={"kb": other}, device_id_type=pl.DeviceIdType.MESH,
            ).start()
            return carry

        lax.fori_loop(0, 2, one, 0)
        lax.fori_loop(3, devices, one, 0)

    def finish(ref, sem):
        part = ref.at[pl.ds(0, devices - 1)]
        pltpu.make_async_copy(part, part, sem).wait()

    loads[3].wait()
    loads[0].wait()
    for p in range(CHUNKS):
        to_time(green, table, tau, p)
        if p == 0:
            pl.semaphore_wait(barrier, devices - 1)
        exchange(tau.at[p], x.at[p], p)
    loads[1].wait()
    lane = lax.broadcasted_iota(jnp.int32, (plane, plane), 1)
    ry, rz = lane // side, lane % side
    target = (mirror_ref[1, 0] + side - ry) % side * side + (mirror_ref[2, 0] + side - rz) % side
    pick = (lax.broadcasted_iota(jnp.int32, (plane, plane), 0) == target).astype(jnp.float32).astype(jnp.bfloat16)
    for i in range(2):
        for part in range(2):
            lanes = slice(part * plane, (part + 1) * plane)
            mirrored[i, :, lanes] = mm(planes[i, :, lanes], pick, ((1,), (0,))).astype(jnp.bfloat16)
    landing = [got, last]
    for p in range(CHUNKS):
        pltpu.make_async_copy(tau.at[p, me], x.at[p, me], own.at[p]).wait()
        finish(x.at[p], recv.at[p])
        bubble(pair_ref, mirror_ref, x, planes.at[0:2], mirrored, planes.at[2:4], sent, y, g, gm, chi, p)
        exchange(sent.at[p], landing[p], CHUNKS + p)
    pltpu.make_async_copy(sent.at[0, me], got.at[me], own.at[CHUNKS]).wait()
    finish(got, recv.at[CHUNKS])
    loads[2].wait()
    comps = got.shape[2]
    block = comps // 2
    for i in range(2):
        chosen = slice(i * block, (i + 1) * block)
        value = to_frequency(got.at[:, :, chosen], back)
        for part in range(2):
            acc[part, chosen] = value[part]
    store = pltpu.make_async_copy(acc, half_hbm, load.at[4])
    store.start()
    for p in range(CHUNKS):
        finish(tau.at[p], send.at[p])
        finish(sent.at[p], send.at[CHUNKS + p])
    store.wait()
    pltpu.make_async_copy(sent.at[1, me], last.at[me], own.at[CHUNKS + 1]).wait()
    finish(last, recv.at[CHUNKS + 1])


def to_frequency(x_ref, b_ref):
    devices, _, block, slots, points = x_ref.shape
    freqs = b_ref.shape[-1] // 2
    rows = []
    for c in range(block):
        parts = [x_ref[:, part, c].reshape(devices * slots, points).T for part in range(2)]
        rows.append(jnp.concatenate(parts, axis=1))
    value = mm3(split(jnp.concatenate(rows, axis=0)), (b_ref[0], b_ref[1]))
    return [value[:, part * freqs:(part + 1) * freqs].reshape(block, points, freqs) for part in range(2)]


def finish_kernel(x_ref, b_ref, half_ref, o_ref):
    value = to_frequency(x_ref, b_ref)
    for part in range(2):
        o_ref[part] = half_ref[part] + value[part]


def local(devices, green, pair_table, mirror_map):
    entries, points, freqs = green.shape[1:]
    side = mirror_map.shape[1]
    plane = side * side
    comps = pair_table.shape[0]
    slots = freqs // (devices * CHUNKS)
    f32, bf16 = jnp.float32, jnp.bfloat16
    times = [owned_times(devices, freqs, p) for p in range(CHUNKS)]
    time_table = np.stack([np.stack(time_tables(t, freqs)) for t in times])
    plane_tables = np.stack(plane_table(side, 1.0) + plane_table(side, -1.0))
    frequency_table = [np.stack(frequency_tables(t, freqs)) for t in times]
    hbm = pl.BlockSpec(memory_space=pl.ANY)
    cells = (side, entries, slots, 2 * plane)
    exchanged = (devices, 2, comps, slots, points)
    result = (2, comps, points, freqs)
    half, last = pl.pallas_call(
        main_kernel,
        out_shape=[jax.ShapeDtypeStruct(result, f32), jax.ShapeDtypeStruct(exchanged, f32)],
        in_specs=[SMEM, SMEM, hbm, hbm, hbm, hbm],
        out_specs=[hbm, hbm],
        scratch_shapes=[
            pltpu.VMEM(green.shape, f32),
            pltpu.VMEM(time_table.shape, bf16),
            pltpu.VMEM(plane_tables.shape, bf16),
            pltpu.VMEM(frequency_table[0].shape, bf16),
            pltpu.VMEM((2, 2 * plane, 2 * plane), bf16),
            pltpu.VMEM((CHUNKS, devices, 2, entries, slots, points), f32),
            pltpu.VMEM((CHUNKS, devices, 2, entries, slots, points), f32),
            pltpu.VMEM(cells, f32),
            pltpu.VMEM(cells, f32),
            pltpu.VMEM(cells, f32),
            pltpu.VMEM((comps,) + (side, slots, 2 * plane), f32),
            pltpu.VMEM((CHUNKS,) + exchanged, f32),
            pltpu.VMEM(exchanged, f32),
            pltpu.VMEM(result, f32),
            pltpu.SemaphoreType.DMA((5,)),
            pltpu.SemaphoreType.DMA((2 * CHUNKS,)),
            pltpu.SemaphoreType.DMA((2 * CHUNKS,)),
            pltpu.SemaphoreType.DMA((2 * CHUNKS,)),
        ],
        compiler_params=pltpu.CompilerParams(
            vmem_limit_bytes=60 * 1024 * 1024, collective_id=0, has_side_effects=True
        ),
        cost_estimate=pl.CostEstimate(flops=18 * 10**9, bytes_accessed=16 * 2**20, transcendentals=0),
    )(pair_table.T, mirror_map, green, time_table, plane_tables, frequency_table[0])
    block = comps // 4
    whole = pl.BlockSpec((2, block, points, freqs), lambda i: (0, i, 0, 0))
    return pl.pallas_call(
        finish_kernel,
        grid=(comps // block,),
        out_shape=jax.ShapeDtypeStruct(result, f32),
        in_specs=[
            pl.BlockSpec((devices, 2, block, slots, points), lambda i: (0, 0, i, 0, 0)),
            pl.BlockSpec(frequency_table[1].shape, lambda i: (0, 0, 0)),
            whole,
        ],
        out_specs=whole,
        compiler_params=pltpu.CompilerParams(vmem_limit_bytes=58 * 1024 * 1024),
        cost_estimate=pl.CostEstimate(flops=6 * 10**9, bytes_accessed=16 * 2**20, transcendentals=0),
    )(last, frequency_table[1], half)


LEVELS = 4
PIECES = 8
LEAD = 3
GROUP = 2


def piece_times(members, freqs, piece):
    per = freqs // (2 * PIECES * members)
    first = piece * (freqs // (2 * PIECES)) + np.arange(members)[:, None] * per + np.arange(per)[None, :]
    return np.stack([first, freqs - 1 - first], axis=1).reshape(-1)


def stacked_time_table(times, freqs):
    cos_high, cos_low, sin_high, sin_low = time_tables(times, freqs)
    return np.concatenate([cos_high, sin_high, cos_low, sin_low])


def group_table(members, freqs, group):
    rows = []
    for piece in range(group * GROUP, (group + 1) * GROUP):
        times = piece_times(members, freqs, piece)
        angle = ((np.arange(freqs)[None, :] - freqs // 2) * (2 * times[:, None] + 1)) % (2 * freqs)
        angle = angle * (2 * np.pi / (2 * freqs))
        cos, sin = np.cos(angle) * freqs**-0.5, np.sin(angle) * freqs**-0.5
        rows.append(np.block([[cos, sin], [-sin, cos]]))
    return np.stack(split_np(np.concatenate(rows)))


def mm3s(rows, high, low):
    m = rows.shape[0]
    a, b = split(rows)
    both = mm(jnp.concatenate([a, b], axis=0), high, ((1,), (0,)))
    return both[:m] + both[m:] + mm(a, low, ((1,), (0,)))


def dft16_half(columns, sigma):
    out = [None] * 8
    for k1 in range(4):
        a = [twiddle(columns[n2][k1], n2 * k1, -1) for n2 in range(4)]
        s02, d02 = cadd(a[0], a[2]), csub(a[0], a[2])
        s13, d13 = cadd(a[1], a[3]), csub(a[1], a[3])
        out[k1] = (s02[0] + sigma * s13[0], s02[1] + sigma * s13[1])
        out[4 + k1] = (d02[0] + sigma * d13[1], d02[1] - sigma * d13[0])
    return out


def level_kernel(pair_ref, mirror_ref, green_hbm, time_hbm, plane_hbm, back_hbm, half_hbm, last,
                 green, table, planes, back, mirrored, tau, x, zbuf, t, ts, chi, sent, got, acc,
                 load, own, send, recv1, recvz, recvc, recv2):
    members = tau.shape[1]
    entries, slots, points = tau.shape[3:]
    side = t.shape[0]
    lines = side // LEVELS
    plane = side * side
    comps = sent.shape[3]
    freqs = green.shape[-1]
    kept = got.shape[0]
    me = lax.axis_index("kb")
    z, d = me // members, lax.rem(me, members)
    middle = jnp.logical_or(z == 1, z == 2)
    edge = jnp.logical_not(middle)
    mine = lax.rem(z, 2)
    half = slots // 2

    loads = [pltpu.make_async_copy(src, dst, load.at[i])
             for i, (src, dst) in enumerate([(time_hbm, table), (plane_hbm, planes), (back_hbm, back),
                                             (green_hbm, green)])]
    for i in (3, 0, 1, 2):
        loads[i].start()
    barrier = pltpu.get_barrier_semaphore()

    def greet(other):
        pl.semaphore_signal(barrier, inc=1, device_id={"kb": other}, device_id_type=pl.DeviceIdType.MESH)

    def greet_member(s, carry):
        greet(z * members + lax.rem(d + s, members))
        return carry

    lax.fori_loop(1, members, greet_member, 0)
    for s in range(1, LEVELS):
        greet(lax.rem(z + s, LEVELS) * members + d)

    def partner(shift):
        total, bit = 0, 1
        while bit < members:
            total += bit * lax.rem(d // bit + shift // bit, 2)
            bit *= 2
        return total

    def remote(src, dst, send_sem, recv_sem, other):
        pltpu.make_async_remote_copy(
            src_ref=src, dst_ref=dst, send_sem=send_sem, recv_sem=recv_sem,
            device_id={"kb": other}, device_id_type=pl.DeviceIdType.MESH,
        ).start()

    def exchange(src, dst, own_sem, send_sem, recv_sem):
        pltpu.make_async_copy(src.at[d], dst.at[d], own_sem).start()

        def one(i, carry):
            other = partner(members - i)
            remote(src.at[other], dst.at[d], send_sem, recv_sem, z * members + other)
            return carry

        lax.fori_loop(1, members, one, 0)

    def drain(ref, sem):
        pltpu.make_async_copy(ref, ref, sem).wait()

    def finish(src, dst, own_sem, recv_sem):
        pltpu.make_async_copy(src.at[d], dst.at[d], own_sem).wait()
        drain(dst.at[pl.ds(0, members - 1)], recv_sem)

    loads[3].wait()
    loads[0].wait()
    stacks = table.shape[0]
    per = PIECES // stacks
    times = freqs // stacks
    dims = ((1,), (1,))
    re = split(green[0].reshape(entries * points, freqs))
    im = split(green[1].reshape(entries * points, freqs))
    for s in range(stacks):
        outs = []
        for value in (re, im):
            a = mm(table[s], value[0], dims)
            outs.append(a[:2 * times] + a[2 * times:] + mm(table[s, :2 * times], value[1], dims))
        both = (outs[0][:times] + outs[1][times:], outs[1][:times] - outs[0][times:])
        for part in range(2):
            for e in range(entries):
                tau[s * per:(s + 1) * per, :, part, e] = both[part][:, e * points:(e + 1) * points].reshape(
                    per, members, slots, points)
        if s == 0:
            pl.semaphore_wait(barrier, members - 1 + LEVELS - 1)

        def out(p, carry):
            exchange(tau.at[p], x.at[p], own.at[p], send.at[0], recv1.at[p])
            return carry

        lax.fori_loop(s * per, (s + 1) * per, out, 0)
    loads[1].wait()
    lane = lax.broadcasted_iota(jnp.int32, (plane, plane), 1)
    ry, rz = lane // side, lane % side
    target = (mirror_ref[1, 0] + side - ry) % side * side + (mirror_ref[2, 0] + side - rz) % side
    pick = (lax.broadcasted_iota(jnp.int32, (plane, plane), 0) == target).astype(jnp.float32).astype(jnp.bfloat16)
    for i in range(2):
        for part in range(2):
            lanes = slice(part * plane, (part + 1) * plane)
            mirrored[i, :, lanes] = mm(planes[i, :, lanes], pick, ((1,), (0,))).astype(jnp.bfloat16)
            mirrored[2 + i, lanes, :] = mm(pick, planes[2 + i, lanes, :], ((1,), (0,))).astype(jnp.bfloat16)

    def both_ways(rows, base):
        straight = mm3s(rows, planes[base], planes[base + 1])
        turned = mm3s(rows, mirrored[base], mirrored[base + 1])
        slot = lax.broadcasted_iota(jnp.int32, straight.shape, 0) % slots
        return jnp.where(slot < half, straight, turned)

    def forward(p):
        finish(tau.at[p], x.at[p], own.at[p], recv1.at[p])
        v = x[p].reshape(lines, 2, 2, entries, slots, points)
        rows = jnp.concatenate([v[:, h, part].reshape(lines * entries * slots, points)
                                for part in range(2) for h in range(2)], axis=1)
        out = both_ways(rows, 0)
        for h in range(2):
            for part in range(2):
                lanes = slice(part * plane + h * points, part * plane + (h + 1) * points)
                zbuf[p, h, z, part] = out[:, lanes].reshape(lines, entries, slots, points)
            for level in (1, 2):
                @pl.when(z != level)
                def _():
                    remote(zbuf.at[p, h, z], zbuf.at[p, h, z], send.at[1], recvz.at[p, h], level * members + d)

    def middle_work(p, h):
        drain(zbuf.at[p, h, pl.ds(0, LEVELS - 1)], recvz.at[p, h])
        sigma = jnp.where(z == 1, 1.0, -1.0).astype(jnp.float32)

        def forth(e, carry):
            cells = [(zbuf[p, h, k // lines, 0, k % lines, e], zbuf[p, h, k // lines, 1, k % lines, e])
                     for k in range(side)]
            for r, pair in enumerate(dft16(cells, 1)):
                for part in range(2):
                    v = pair[part]
                    t[r, e, part] = v
                    ts[r, e, part] = jnp.concatenate([v[half:], v[:half]], axis=0)
            return carry

        lax.fori_loop(0, entries, forth, 0)

        def one(c, carry):
            left, right = pair_ref[0, c], pair_ref[1, c]
            columns = []
            for n2 in range(4):
                cells = []
                for n1 in range(4):
                    r = 4 * n1 + n2
                    a, b = t[r, left], ts[mirror_ref[0, r], right]
                    cells.append((a[0] * b[0] - a[1] * b[1], a[0] * b[1] + a[1] * b[0]))
                columns.append(dft4(cells, -1))
            for i, pair in enumerate(dft16_half(columns, sigma)):
                for part in range(2):
                    chi[i // lines, p, h, c, part, i % lines] = pair[part]
            remote(chi.at[1 - mine, p, h, c], chi.at[1 - mine, p, h, c], send.at[2], recvc.at[p],
                   jnp.where(z == 1, 0, 3) * members + d)
            return carry

        lax.fori_loop(0, comps, one, 0)

    def backward(p):
        v = chi[mine, p]
        rows = jnp.concatenate([v[h, :, part].reshape(comps * lines * slots, points)
                                for part in range(2) for h in range(2)], axis=1)
        out = both_ways(rows, 2).reshape(comps, lines, slots, 2 * plane)
        for q in range(lines):
            for h in range(2):
                for part in range(2):
                    lanes = slice(part * plane + h * points, part * plane + (h + 1) * points)
                    sent[p, 2 * q + h, part] = out[:, q, :, lanes]

    def frequency(m):
        block = comps // 2
        for i in range(2):
            chosen = slice(i * block, (i + 1) * block)
            value = mm3s(frequency_rows([got.at[m * GROUP + g] for g in range(GROUP)], i * block, block),
                         back[m, 0], back[m, 1])
            for part in range(2):
                acc[part, chosen] += value[:, part * freqs:(part + 1) * freqs].reshape(block, points, freqs)

    acc[...] = jnp.zeros(acc.shape, jnp.float32)
    loads[2].wait()

    def lead(p, carry):
        forward(p)
        return carry

    lax.fori_loop(0, LEAD, lead, 0)

    def step(p, carry):
        @pl.when(p + LEAD < PIECES)
        def _():
            forward(p + LEAD)

        @pl.when(jnp.logical_and(lax.rem(p, GROUP) == GROUP - 1, p >= 2 * GROUP - 1))
        def _():
            m = p // GROUP - 1

            def arrived(q, carry):
                finish(sent.at[q], got.at[q], own.at[PIECES + q], recv2.at[q])
                return carry

            lax.fori_loop(m * GROUP, (m + 1) * GROUP, arrived, 0)
            frequency(m)

        @pl.when(middle)
        def _():
            for h in range(2):
                middle_work(p, h)

        @pl.when(edge)
        def _():
            drain(chi.at[mine, p], recvc.at[p])

        backward(p)

        @pl.when(p < kept)
        def _():
            exchange(sent.at[p], got.at[p], own.at[PIECES + p], send.at[3], recv2.at[p])

        @pl.when(p >= kept)
        def _():
            exchange(sent.at[p], last.at[p - kept], own.at[PIECES + p], send.at[3], recv2.at[p])

        return carry

    lax.fori_loop(0, PIECES, step, 0)
    store = pltpu.make_async_copy(acc, half_hbm, load.at[4])
    store.start()
    drain(tau.at[:, pl.ds(0, members - 1)], send.at[0])
    drain(zbuf.at[pl.ds(0, PIECES // LEVELS)], send.at[1])

    @pl.when(edge)
    def _():
        drain(zbuf.at[pl.ds(0, PIECES // LEVELS)], send.at[1])

    @pl.when(middle)
    def _():
        drain(chi.at[0], send.at[2])

    for p in range(kept, PIECES):
        finish(sent.at[p], last.at[p - kept], own.at[PIECES + p], recv2.at[p])
    drain(sent.at[:, pl.ds(0, members - 1)], send.at[3])
    store.wait()


def frequency_rows(pieces, first, block):
    rows = []
    for c in range(first, first + block):
        parts = []
        for ref in pieces:
            for part in range(2):
                v = ref[:, part, c]
                parts.append(v.reshape(v.shape[0] * v.shape[1], v.shape[2]))
        rows.append(jnp.concatenate(parts, axis=0).T)
    return jnp.concatenate(rows, axis=0)


def level_finish(x_ref, b_ref, half_ref, o_ref):
    block, points, freqs = o_ref.shape[1:]
    value = mm3s(frequency_rows([x_ref.at[g] for g in range(GROUP)], 0, block), b_ref[0], b_ref[1])
    for part in range(2):
        o_ref[part] = half_ref[part] + value[:, part * freqs:(part + 1) * freqs].reshape(block, points, freqs)


def level_local(devices, green, pair_table, mirror_map):
    entries, points, freqs = green.shape[1:]
    side = mirror_map.shape[1]
    plane = side * side
    comps = pair_table.shape[0]
    members = devices // LEVELS
    slots = freqs // (members * PIECES)
    lines = side // LEVELS
    f32, bf16 = jnp.float32, jnp.bfloat16
    times = [piece_times(members, freqs, p) for p in range(PIECES)]
    stacks = 2
    per = PIECES // stacks
    time_table = np.stack([stacked_time_table(np.concatenate(times[s * per:(s + 1) * per]), freqs)
                           for s in range(stacks)])
    plane_tables = np.stack(plane_table(side, 1.0) + plane_table(side, -1.0))
    groups = PIECES // GROUP
    back = [group_table(members, freqs, g) for g in range(groups)]
    early = np.stack(back[:-1])
    kept = PIECES - GROUP
    hbm = pl.BlockSpec(memory_space=pl.ANY)
    exchanged = (members, 2, comps, slots, points)
    result = (2, comps, points, freqs)
    cells = (side, entries, 2, slots, points)
    half, last = pl.pallas_call(
        level_kernel,
        out_shape=[jax.ShapeDtypeStruct(result, f32), jax.ShapeDtypeStruct((GROUP,) + exchanged, f32)],
        in_specs=[SMEM, SMEM, hbm, hbm, hbm, hbm],
        out_specs=[hbm, hbm],
        scratch_shapes=[
            pltpu.VMEM(green.shape, f32),
            pltpu.VMEM(time_table.shape, bf16),
            pltpu.VMEM(plane_tables.shape, bf16),
            pltpu.VMEM(early.shape, bf16),
            pltpu.VMEM(plane_tables.shape, bf16),
            pltpu.VMEM((PIECES, members, 2, entries, slots, points), f32),
            pltpu.VMEM((PIECES, members, 2, entries, slots, points), f32),
            pltpu.VMEM((PIECES, 2, LEVELS, 2, lines, entries, slots, points), f32),
            pltpu.VMEM(cells, f32),
            pltpu.VMEM(cells, f32),
            pltpu.VMEM((2, PIECES, 2, comps, 2, lines, slots, points), f32),
            pltpu.VMEM((PIECES,) + exchanged, f32),
            pltpu.VMEM((kept,) + exchanged, f32),
            pltpu.VMEM(result, f32),
            pltpu.SemaphoreType.DMA((5,)),
            pltpu.SemaphoreType.DMA((2 * PIECES,)),
            pltpu.SemaphoreType.DMA((4,)),
            pltpu.SemaphoreType.DMA((PIECES,)),
            pltpu.SemaphoreType.DMA((PIECES, 2)),
            pltpu.SemaphoreType.DMA((PIECES,)),
            pltpu.SemaphoreType.DMA((PIECES,)),
        ],
        compiler_params=pltpu.CompilerParams(
            vmem_limit_bytes=60 * 1024 * 1024, collective_id=0, has_side_effects=True
        ),
        cost_estimate=pl.CostEstimate(flops=18 * 10**9, bytes_accessed=16 * 2**20, transcendentals=0),
    )(pair_table.T, mirror_map, green, time_table, plane_tables, early)
    block = comps // 4
    whole = pl.BlockSpec((2, block, points, freqs), lambda i: (0, i, 0, 0))
    return pl.pallas_call(
        level_finish,
        grid=(comps // block,),
        out_shape=jax.ShapeDtypeStruct(result, f32),
        in_specs=[
            pl.BlockSpec((GROUP, members, 2, block, slots, points), lambda i: (0, 0, 0, i, 0, 0)),
            pl.BlockSpec(back[-1].shape, lambda i: (0, 0, 0)),
            whole,
        ],
        out_specs=whole,
        compiler_params=pltpu.CompilerParams(vmem_limit_bytes=58 * 1024 * 1024),
        cost_estimate=pl.CostEstimate(flops=6 * 10**9, bytes_accessed=16 * 2**20, transcendentals=0),
    )(last, back[-1], half)


def fits_levels(devices):
    return devices == 32


def solution(mesh):
    placed = (P("set", None, "kb", None), P(), P("set", None))
    devices = mesh.shape["kb"]
    return jax.shard_map(
        functools.partial(level_local if fits_levels(devices) else local, devices),
        mesh=mesh,
        in_specs=placed,
        out_specs=P("set", None, "kb", None),
        check_vma=False,
    )
```

```python
import functools

import numpy as np
import ml_dtypes
import jax
import jax.numpy as jnp
from jax import lax
from jax.experimental import pallas as pl
from jax.experimental.pallas import tpu as pltpu
from jax.sharding import PartitionSpec as P

CHUNKS = 2
SMEM = pl.BlockSpec(memory_space=pltpu.SMEM)


def split_np(table):
    table = table.astype(np.float32)
    high = table.astype(ml_dtypes.bfloat16)
    low = (table - high.astype(np.float32)).astype(ml_dtypes.bfloat16)
    return high, low


def split(x):
    high = x.astype(jnp.bfloat16)
    return high, (x - high.astype(jnp.float32)).astype(jnp.bfloat16)


def mm(a, b, dims):
    return lax.dot_general(a, b, (dims, ((), ())), preferred_element_type=jnp.float32)


def mm3(a, b, dims=((1,), (0,))):
    return mm(a[0], b[0], dims) + mm(a[1], b[0], dims) + mm(a[0], b[1], dims)


def owned_times(devices, freqs, chunk):
    per = freqs // (2 * CHUNKS * devices)
    first = chunk * (freqs // (2 * CHUNKS)) + np.arange(devices)[:, None] * per + np.arange(per)[None, :]
    return np.stack([first, freqs - 1 - first], axis=1).reshape(-1)


def time_tables(times, freqs):
    angle = ((2 * np.arange(freqs)[None, :] - freqs + 1) * (2 * times[:, None] + 1)) % (4 * freqs)
    angle = angle * (2 * np.pi / (4 * freqs))
    scale = freqs**-0.5
    return split_np(scale * np.cos(angle)) + split_np(scale * np.sin(angle))


def frequency_tables(times, freqs):
    angle = ((np.arange(freqs)[None, :] - freqs // 2) * (2 * times[:, None] + 1)) % (2 * freqs)
    angle = angle * (2 * np.pi / (2 * freqs))
    cos, sin = np.cos(angle) * freqs**-0.5, np.sin(angle) * freqs**-0.5
    return split_np(np.block([[cos, sin], [-sin, cos]]))


def plane_table(side, sign):
    index = np.arange(side * side)
    upper, lower = index // side, index % side
    angle = (upper[:, None] * upper[None, :] + lower[:, None] * lower[None, :]) % side * (2 * np.pi / side)
    scale = (side**3) ** -0.5
    cos, sin = scale * np.cos(angle), sign * scale * np.sin(angle)
    return split_np(np.block([[cos, sin], [-sin, cos]]))


def cadd(a, b):
    return a[0] + b[0], a[1] + b[1]


def csub(a, b):
    return a[0] - b[0], a[1] - b[1]


def dft4(a, sign):
    s02, d02 = cadd(a[0], a[2]), csub(a[0], a[2])
    s13, d13 = cadd(a[1], a[3]), csub(a[1], a[3])
    turned = (-d13[1], d13[0]) if sign > 0 else (d13[1], -d13[0])
    return [cadd(s02, s13), cadd(d02, turned), csub(s02, s13), csub(d02, turned)]


def twiddle(a, power, sign):
    if power == 0:
        return a
    if power == 4:
        return (-a[1], a[0]) if sign > 0 else (a[1], -a[0])
    if power in (2, 6):
        r = np.float32(np.sqrt(0.5))
        plus, minus = (a[0] + a[1]) * r, (a[0] - a[1]) * r
        if power == 2:
            return (minus, plus) if sign > 0 else (plus, -minus)
        return (-plus, minus) if sign > 0 else (-minus, -plus)
    c = np.float32(np.cos(2 * np.pi * power / 16))
    s = np.float32(sign * np.sin(2 * np.pi * power / 16))
    return a[0] * c - a[1] * s, a[0] * s + a[1] * c


def dft16(x, sign):
    columns = [dft4([x[4 * n1 + n2] for n1 in range(4)], sign) for n2 in range(4)]
    out = [None] * 16
    for k1 in range(4):
        row = dft4([twiddle(columns[n2][k1], n2 * k1, sign) for n2 in range(4)], sign)
        for k2 in range(4):
            out[k1 + 4 * k2] = row[k2]
    return out


def to_time(g_ref, table, o_ref, p):
    devices, _, entries, slots, points = o_ref.shape[1:]
    freqs = g_ref.shape[-1]
    cos, sin = (table[p, 0], table[p, 1]), (table[p, 2], table[p, 3])
    dims = ((1,), (1,))
    re = split(g_ref[0].reshape(entries * points, freqs))
    im = split(g_ref[1].reshape(entries * points, freqs))
    tau = (mm3(cos, re, dims) + mm3(sin, im, dims), mm3(cos, im, dims) - mm3(sin, re, dims))
    for part in range(2):
        for e in range(entries):
            o_ref[p, :, part, e] = tau[part][:, e * points:(e + 1) * points].reshape(devices, slots, points)


def bubble(pair_ref, mirror_ref, x_ref, ahead, mirrored, inverse, o_ref, y, g, gm, chi, p):
    devices, _, entries, slots, points = x_ref.shape[1:]
    side = y.shape[0]
    plane = side * side
    halves = devices // side
    comps = o_ref.shape[3]

    def forth(e, carry):
        for h in range(halves):
            cells = [(x_ref[p, k * halves + h, 0, e], x_ref[p, k * halves + h, 1, e]) for k in range(side)]
            for k, (re, im) in enumerate(dft16(cells, 1)):
                y[k, e, :, h * points:(h + 1) * points] = re
                y[k, e, :, plane + h * points:plane + (h + 1) * points] = im
        return carry

    lax.fori_loop(0, entries, forth, 0)
    rows = split(y[...].reshape(side * entries * slots, 2 * plane))
    g[...] = mm3(rows, (ahead[0], ahead[1])).reshape(g.shape)
    other = mm3(rows, (mirrored[0], mirrored[1])).reshape(side * entries, slots, 2 * plane)
    other = jnp.concatenate([other[:, slots // 2:], other[:, :slots // 2]], axis=1)
    gm[...] = other.reshape(gm.shape)

    def one(c, carry):
        left, right = pair_ref[0, c], pair_ref[1, c]
        for r in range(side):
            a = g[r, left]
            b = gm[mirror_ref[0, r], right]
            ar, ai, br, bi = a[:, :plane], a[:, plane:], b[:, :plane], b[:, plane:]
            chi[c, r, :, :plane] = ar * br - ai * bi
            chi[c, r, :, plane:] = ar * bi + ai * br
        return carry

    lax.fori_loop(0, comps, one, 0)
    rows = split(chi[...].reshape(comps * side * slots, 2 * plane))
    chi[...] = mm3(rows, (inverse[0], inverse[1])).reshape(chi.shape)

    def back(c, carry):
        for h in range(halves):
            lanes = slice(h * points, (h + 1) * points)
            high = slice(plane + h * points, plane + (h + 1) * points)
            cells = [(chi[c, r, :, lanes], chi[c, r, :, high]) for r in range(side)]
            for q, (re, im) in enumerate(dft16(cells, -1)):
                o_ref[p, q * halves + h, 0, c] = re
                o_ref[p, q * halves + h, 1, c] = im
        return carry

    lax.fori_loop(0, comps, back, 0)


def main_kernel(pair_ref, mirror_ref, green_hbm, time_hbm, plane_hbm, back_hbm, half_hbm, last,
                green, table, planes, back, mirrored, tau, x, y, g, gm, chi, sent, got, acc,
                load, own, send, recv):
    devices = tau.shape[1]
    side = y.shape[0]
    plane = side * side
    me = lax.axis_index("kb")
    loads = [pltpu.make_async_copy(src, dst, load.at[i])
             for i, (src, dst) in enumerate([(time_hbm, table), (plane_hbm, planes), (back_hbm, back),
                                       (green_hbm, green)])]
    for i in (3, 0, 1, 2):
        loads[i].start()
    barrier = pltpu.get_barrier_semaphore()

    def greet(s, carry):
        pl.semaphore_signal(barrier, inc=1, device_id={"kb": lax.rem(me + s, devices)},
                            device_id_type=pl.DeviceIdType.MESH)
        return carry

    lax.fori_loop(1, devices, greet, 0)

    def partner(shift):
        total, bit = 0, 1
        while bit < devices:
            total += bit * lax.rem(me // bit + shift // bit, 2)
            bit *= 2
        return total

    def exchange(src, dst, n):
        pltpu.make_async_copy(src.at[me], dst.at[me], own.at[n]).start()

        def one(i, carry):
            other = partner(i // 4 + devices // 4 * lax.rem(i + 2, 4))
            pltpu.make_async_remote_copy(
                src_ref=src.at[other], dst_ref=dst.at[me], send_sem=send.at[n], recv_sem=recv.at[n],
                device_id={"kb": other}, device_id_type=pl.DeviceIdType.MESH,
            ).start()
            return carry

        lax.fori_loop(0, 2, one, 0)
        lax.fori_loop(3, devices, one, 0)

    def finish(ref, sem):
        part = ref.at[pl.ds(0, devices - 1)]
        pltpu.make_async_copy(part, part, sem).wait()

    loads[3].wait()
    loads[0].wait()
    for p in range(CHUNKS):
        to_time(green, table, tau, p)
        if p == 0:
            pl.semaphore_wait(barrier, devices - 1)
        exchange(tau.at[p], x.at[p], p)
    loads[1].wait()
    lane = lax.broadcasted_iota(jnp.int32, (plane, plane), 1)
    ry, rz = lane // side, lane % side
    target = (mirror_ref[1, 0] + side - ry) % side * side + (mirror_ref[2, 0] + side - rz) % side
    pick = (lax.broadcasted_iota(jnp.int32, (plane, plane), 0) == target).astype(jnp.float32).astype(jnp.bfloat16)
    for i in range(2):
        for part in range(2):
            lanes = slice(part * plane, (part + 1) * plane)
            mirrored[i, :, lanes] = mm(planes[i, :, lanes], pick, ((1,), (0,))).astype(jnp.bfloat16)
    landing = [got, last]
    for p in range(CHUNKS):
        pltpu.make_async_copy(tau.at[p, me], x.at[p, me], own.at[p]).wait()
        finish(x.at[p], recv.at[p])
        bubble(pair_ref, mirror_ref, x, planes.at[0:2], mirrored, planes.at[2:4], sent, y, g, gm, chi, p)
        exchange(sent.at[p], landing[p], CHUNKS + p)
    pltpu.make_async_copy(sent.at[0, me], got.at[me], own.at[CHUNKS]).wait()
    finish(got, recv.at[CHUNKS])
    loads[2].wait()
    comps = got.shape[2]
    block = comps // 2
    for i in range(2):
        chosen = slice(i * block, (i + 1) * block)
        value = to_frequency(got.at[:, :, chosen], back)
        for part in range(2):
            acc[part, chosen] = value[part]
    store = pltpu.make_async_copy(acc, half_hbm, load.at[4])
    store.start()
    for p in range(CHUNKS):
        finish(tau.at[p], send.at[p])
        finish(sent.at[p], send.at[CHUNKS + p])
    store.wait()
    pltpu.make_async_copy(sent.at[1, me], last.at[me], own.at[CHUNKS + 1]).wait()
    finish(last, recv.at[CHUNKS + 1])


def to_frequency(x_ref, b_ref):
    devices, _, block, slots, points = x_ref.shape
    freqs = b_ref.shape[-1] // 2
    rows = []
    for c in range(block):
        parts = [x_ref[:, part, c].reshape(devices * slots, points).T for part in range(2)]
        rows.append(jnp.concatenate(parts, axis=1))
    value = mm3(split(jnp.concatenate(rows, axis=0)), (b_ref[0], b_ref[1]))
    return [value[:, part * freqs:(part + 1) * freqs].reshape(block, points, freqs) for part in range(2)]


def finish_kernel(x_ref, b_ref, half_ref, o_ref):
    value = to_frequency(x_ref, b_ref)
    for part in range(2):
        o_ref[part] = half_ref[part] + value[part]


def local(devices, green, pair_table, mirror_map):
    entries, points, freqs = green.shape[1:]
    side = mirror_map.shape[1]
    plane = side * side
    comps = pair_table.shape[0]
    slots = freqs // (devices * CHUNKS)
    f32, bf16 = jnp.float32, jnp.bfloat16
    times = [owned_times(devices, freqs, p) for p in range(CHUNKS)]
    time_table = np.stack([np.stack(time_tables(t, freqs)) for t in times])
    plane_tables = np.stack(plane_table(side, 1.0) + plane_table(side, -1.0))
    frequency_table = [np.stack(frequency_tables(t, freqs)) for t in times]
    hbm = pl.BlockSpec(memory_space=pl.ANY)
    cells = (side, entries, slots, 2 * plane)
    exchanged = (devices, 2, comps, slots, points)
    result = (2, comps, points, freqs)
    half, last = pl.pallas_call(
        main_kernel,
        out_shape=[jax.ShapeDtypeStruct(result, f32), jax.ShapeDtypeStruct(exchanged, f32)],
        in_specs=[SMEM, SMEM, hbm, hbm, hbm, hbm],
        out_specs=[hbm, hbm],
        scratch_shapes=[
            pltpu.VMEM(green.shape, f32),
            pltpu.VMEM(time_table.shape, bf16),
            pltpu.VMEM(plane_tables.shape, bf16),
            pltpu.VMEM(frequency_table[0].shape, bf16),
            pltpu.VMEM((2, 2 * plane, 2 * plane), bf16),
            pltpu.VMEM((CHUNKS, devices, 2, entries, slots, points), f32),
            pltpu.VMEM((CHUNKS, devices, 2, entries, slots, points), f32),
            pltpu.VMEM(cells, f32),
            pltpu.VMEM(cells, f32),
            pltpu.VMEM(cells, f32),
            pltpu.VMEM((comps,) + (side, slots, 2 * plane), f32),
            pltpu.VMEM((CHUNKS,) + exchanged, f32),
            pltpu.VMEM(exchanged, f32),
            pltpu.VMEM(result, f32),
            pltpu.SemaphoreType.DMA((5,)),
            pltpu.SemaphoreType.DMA((2 * CHUNKS,)),
            pltpu.SemaphoreType.DMA((2 * CHUNKS,)),
            pltpu.SemaphoreType.DMA((2 * CHUNKS,)),
        ],
        compiler_params=pltpu.CompilerParams(
            vmem_limit_bytes=60 * 1024 * 1024, collective_id=0, has_side_effects=True
        ),
        cost_estimate=pl.CostEstimate(flops=18 * 10**9, bytes_accessed=16 * 2**20, transcendentals=0),
    )(pair_table.T, mirror_map, green, time_table, plane_tables, frequency_table[0])
    block = comps // 4
    whole = pl.BlockSpec((2, block, points, freqs), lambda i: (0, i, 0, 0))
    return pl.pallas_call(
        finish_kernel,
        grid=(comps // block,),
        out_shape=jax.ShapeDtypeStruct(result, f32),
        in_specs=[
            pl.BlockSpec((devices, 2, block, slots, points), lambda i: (0, 0, i, 0, 0)),
            pl.BlockSpec(frequency_table[1].shape, lambda i: (0, 0, 0)),
            whole,
        ],
        out_specs=whole,
        compiler_params=pltpu.CompilerParams(vmem_limit_bytes=58 * 1024 * 1024),
        cost_estimate=pl.CostEstimate(flops=6 * 10**9, bytes_accessed=16 * 2**20, transcendentals=0),
    )(last, frequency_table[1], half)


LEVELS = 4
PIECES = 8
STACKS = (1, 3, 4)
PARTS = 2
GROUP = 2


def piece_times(members, freqs, piece):
    per = freqs // (2 * PIECES * members)
    first = piece * (freqs // (2 * PIECES)) + np.arange(members)[:, None] * per + np.arange(per)[None, :]
    return np.stack([first, freqs - 1 - first], axis=1).reshape(-1)


def stacked_time_table(times, freqs):
    cos_high, cos_low, sin_high, sin_low = time_tables(times, freqs)
    return np.concatenate([cos_high, sin_high, cos_low, sin_low])


def group_table(members, freqs, group):
    rows = []
    for piece in range(group * GROUP, (group + 1) * GROUP):
        times = piece_times(members, freqs, piece)
        angle = ((np.arange(freqs)[None, :] - freqs // 2) * (2 * times[:, None] + 1)) % (2 * freqs)
        angle = angle * (2 * np.pi / (2 * freqs))
        cos, sin = np.cos(angle) * freqs**-0.5, np.sin(angle) * freqs**-0.5
        rows.append(np.block([[cos, sin], [-sin, cos]]))
    return np.stack(split_np(np.concatenate(rows)))


def mm3s(rows, high, low):
    m = rows.shape[0]
    a, b = split(rows)
    both = mm(jnp.concatenate([a, b], axis=0), high, ((1,), (0,)))
    return both[:m] + both[m:] + mm(a, low, ((1,), (0,)))


def dft16_half(columns, sigma):
    out = [None] * 8
    for k1 in range(4):
        a = [twiddle(columns[n2][k1], n2 * k1, -1) for n2 in range(4)]
        s02, d02 = cadd(a[0], a[2]), csub(a[0], a[2])
        s13, d13 = cadd(a[1], a[3]), csub(a[1], a[3])
        out[k1] = (s02[0] + sigma * s13[0], s02[1] + sigma * s13[1])
        out[4 + k1] = (d02[0] + sigma * d13[1], d02[1] - sigma * d13[0])
    return out


def level_kernel(pair_ref, mirror_ref, green_hbm, time_hbm, plane_hbm, back_hbm, half_hbm, last,
                 green, table, planes, back, mirrored, tau, x, zbuf, t, ts, chi, sent, got, acc,
                 load, own, send, sendz, recv1, recvz, recvc, recv2):
    members = tau.shape[1]
    entries, slots, points = tau.shape[3:]
    side = t.shape[0]
    lines = side // LEVELS
    plane = side * side
    comps = sent.shape[1] * sent.shape[4]
    group = sent.shape[4]
    freqs = green.shape[-1]
    kept = got.shape[0]
    me = lax.axis_index("kb")
    z, d = me // members, lax.rem(me, members)
    middle = jnp.logical_or(z == 1, z == 2)
    edge = jnp.logical_not(middle)
    mine = lax.rem(z, 2)
    half = slots // 2

    loads = [pltpu.make_async_copy(src, dst, load.at[i])
             for i, (src, dst) in enumerate([(time_hbm, table), (plane_hbm, planes), (back_hbm, back),
                                             (green_hbm, green)])]
    for i in (3, 0, 1, 2):
        loads[i].start()
    barrier = pltpu.get_barrier_semaphore()

    def greet(other):
        pl.semaphore_signal(barrier, inc=1, device_id={"kb": other}, device_id_type=pl.DeviceIdType.MESH)

    def greet_member(s, carry):
        greet(z * members + lax.rem(d + s, members))
        return carry

    lax.fori_loop(1, members, greet_member, 0)
    for s in range(1, LEVELS):
        greet(lax.rem(z + s, LEVELS) * members + d)

    def partner(shift):
        total, bit = 0, 1
        while bit < members:
            total += bit * lax.rem(d // bit + shift // bit, 2)
            bit *= 2
        return total

    def remote(src, dst, send_sem, recv_sem, other):
        pltpu.make_async_remote_copy(
            src_ref=src, dst_ref=dst, send_sem=send_sem, recv_sem=recv_sem,
            device_id={"kb": other}, device_id_type=pl.DeviceIdType.MESH,
        ).start()

    def exchange(src, dst, own_sem, send_sem, recv_sem):
        pltpu.make_async_copy(src.at[d], dst.at[d], own_sem).start()

        def one(i, carry):
            other = partner(members - i)
            remote(src.at[other], dst.at[d], send_sem, recv_sem, z * members + other)
            return carry

        lax.fori_loop(1, members, one, 0)

    def drain(ref, sem):
        pltpu.make_async_copy(ref, ref, sem).wait()

    def finish(src, dst, own_sem, recv_sem):
        pltpu.make_async_copy(src.at[d], dst.at[d], own_sem).wait()
        drain(dst.at[pl.ds(0, members - 1)], recv_sem)

    def finish_parts(p, dst):
        pltpu.make_async_copy(sent.at[p, :, d], dst.at[:, d], own.at[PIECES + p]).wait()
        drain(dst.at[:, pl.ds(0, members - 1)], recv2.at[p])

    dims = ((1,), (1,))

    def times_of(first, count):
        times = count * members * slots
        base = 4 * members * slots * first
        stack = table[base:base + 4 * times]
        outs = []
        for value in (re, im):
            a = mm(stack, value[0], dims)
            outs.append(a[:2 * times] + a[2 * times:] + mm(stack[:2 * times], value[1], dims))
        both = (outs[0][:times] + outs[1][times:], outs[1][:times] - outs[0][times:])
        for part in range(2):
            for e in range(entries):
                tau[first:first + count, :, part, e] = both[part][:, e * points:(e + 1) * points].reshape(
                    count, members, slots, points)

    def exchange_times(p):
        exchange(tau.at[p], x.at[p], own.at[p], send.at[0], recv1.at[p])

    loads[3].wait()
    re = split(green[0].reshape(entries * points, freqs))
    im = split(green[1].reshape(entries * points, freqs))
    loads[0].wait()
    times_of(0, STACKS[0])
    pl.semaphore_wait(barrier, members - 1 + LEVELS - 1)
    exchange_times(0)
    times_of(STACKS[0], STACKS[1])
    loads[1].wait()
    lane = lax.broadcasted_iota(jnp.int32, (plane, plane), 1)
    ry, rz = lane // side, lane % side
    target = (mirror_ref[1, 0] + side - ry) % side * side + (mirror_ref[2, 0] + side - rz) % side
    pick = (lax.broadcasted_iota(jnp.int32, (plane, plane), 0) == target).astype(jnp.float32).astype(jnp.bfloat16)
    for i in range(2):
        for part in range(2):
            lanes = slice(part * plane, (part + 1) * plane)
            mirrored[i, :, lanes] = mm(planes[i, :, lanes], pick, ((1,), (0,))).astype(jnp.bfloat16)
            mirrored[2 + i, lanes, :] = mm(pick, planes[2 + i, lanes, :], ((1,), (0,))).astype(jnp.bfloat16)

    def both_ways(rows, base):
        straight = mm3s(rows, planes[base], planes[base + 1])
        turned = mm3s(rows, mirrored[base], mirrored[base + 1])
        slot = lax.broadcasted_iota(jnp.int32, straight.shape, 0) % slots
        return jnp.where(slot < half, straight, turned)

    def forward(p):
        finish(tau.at[p], x.at[p], own.at[p], recv1.at[p])

        @pl.when(p + 1 < PIECES)
        def _():
            exchange_times(p + 1)

        v = x[p].reshape(lines, 2, 2, entries, slots, points)
        rows = jnp.concatenate([v[:, h, part].reshape(lines * entries * slots, points)
                                for part in range(2) for h in range(2)], axis=1)
        out = both_ways(rows, 0)
        for h in range(2):
            for part in range(2):
                lanes = slice(part * plane + h * points, part * plane + (h + 1) * points)
                zbuf[p, h, z, part] = out[:, lanes].reshape(lines, entries, slots, points)

    def send_lines(p, h):
        for level in (1, 2):
            @pl.when(z != level)
            def _():
                remote(zbuf.at[p, h, z], zbuf.at[p, h, z], sendz.at[p, h], recvz.at[p, h], level * members + d)

    def middle_work(p, h):
        sigma = jnp.where(z == 1, 1.0, -1.0).astype(jnp.float32)

        def forth(e, carry):
            cells = [(zbuf[p, h, k // lines, 0, k % lines, e], zbuf[p, h, k // lines, 1, k % lines, e])
                     for k in range(side)]
            for r, pair in enumerate(dft16(cells, 1)):
                for part in range(2):
                    v = pair[part]
                    t[r, e, part] = v
                    ts[r, e, part] = jnp.concatenate([v[half:], v[:half]], axis=0)
            return carry

        lax.fori_loop(0, entries, forth, 0)

        def one(c, carry):
            left, right = pair_ref[0, c], pair_ref[1, c]
            columns = []
            for n2 in range(4):
                cells = []
                for n1 in range(4):
                    r = 4 * n1 + n2
                    a, b = t[r, left], ts[mirror_ref[0, r], right]
                    cells.append((a[0] * b[0] - a[1] * b[1], a[0] * b[1] + a[1] * b[0]))
                columns.append(dft4(cells, -1))
            for i, pair in enumerate(dft16_half(columns, sigma)):
                for part in range(2):
                    chi[i // lines, p, h, c, part, i % lines] = pair[part]
            remote(chi.at[1 - mine, p, h, c], chi.at[1 - mine, p, h, c], send.at[1], recvc.at[p, c // group],
                   jnp.where(z == 1, 0, 3) * members + d)
            return carry

        lax.fori_loop(0, comps, one, 0)

    def backward(p, n):
        chosen = pl.ds(n * group, group)

        @pl.when(edge)
        def _():
            drain(chi.at[mine, p, :, chosen], recvc.at[p, n])

        v = chi[mine, p, :, n * group:(n + 1) * group]
        rows = jnp.concatenate([v[h, :, part].reshape(group * lines * slots, points)
                                for part in range(2) for h in range(2)], axis=1)
        out = both_ways(rows, 2).reshape(group, lines, slots, 2 * plane)
        for q in range(lines):
            for h in range(2):
                for part in range(2):
                    lanes = slice(part * plane + h * points, part * plane + (h + 1) * points)
                    sent[p, n, 2 * q + h, part] = out[:, q, :, lanes]

        @pl.when(p < kept)
        def _():
            exchange(sent.at[p, n], got.at[p, n], own.at[PIECES + p], send.at[2], recv2.at[p])

        @pl.when(p >= kept)
        def _():
            exchange(sent.at[p, n], last.at[p - kept, n], own.at[PIECES + p], send.at[2], recv2.at[p])

    def backward_all(p):
        for n in range(PARTS):
            backward(p, n)

    def frequency(m):
        for i in range(PARTS):
            chosen = slice(i * group, (i + 1) * group)
            value = mm3s(frequency_rows([got.at[m * GROUP + g, i] for g in range(GROUP)], 0, group),
                         back[m, 0], back[m, 1])
            for part in range(2):
                acc[part, chosen] += value[:, part * freqs:(part + 1) * freqs].reshape(group, points, freqs)

    forward(0)
    for h in range(2):
        send_lines(0, h)
    times_of(STACKS[0] + STACKS[1], STACKS[2])
    acc[...] = jnp.zeros(acc.shape, jnp.float32)
    loads[2].wait()
    forward(1)

    def step(p, carry):
        for h in range(2):
            @pl.when(middle)
            def _():
                drain(zbuf.at[p, h, pl.ds(0, LEVELS - 1)], recvz.at[p, h])

            @pl.when(edge)
            def _():
                drain(zbuf.at[p, h, pl.ds(0, 2)], sendz.at[p, h])

            @pl.when(p + 1 < PIECES)
            def _():
                send_lines(p + 1, h)

            @pl.when(middle)
            def _():
                middle_work(p, h)

        @pl.when(p + 2 < PIECES)
        def _():
            forward(p + 2)

        @pl.when(jnp.logical_or(middle, p > 0))
        def _():
            backward_all(jnp.where(middle, p, p - 1))

        @pl.when(jnp.logical_and(lax.rem(p, GROUP) == GROUP - 1, p >= 2 * GROUP - 1))
        def _():
            m = p // GROUP - 1

            def arrived(q, carry):
                finish_parts(q, got.at[q])
                return carry

            lax.fori_loop(m * GROUP, (m + 1) * GROUP, arrived, 0)
            frequency(m)

        return carry

    lax.fori_loop(0, PIECES, step, 0)
    store = pltpu.make_async_copy(acc, half_hbm, load.at[4])
    store.start()

    @pl.when(edge)
    def _():
        backward_all(PIECES - 1)

    drain(tau.at[:, pl.ds(0, members - 1)], send.at[0])

    @pl.when(middle)
    def _():
        def gone(p, carry):
            for h in range(2):
                drain(zbuf.at[p, h, 0], sendz.at[p, h])
            return carry

        lax.fori_loop(0, PIECES, gone, 0)
        drain(chi.at[0], send.at[1])

    for p in range(kept, PIECES):
        finish_parts(p, last.at[p - kept])
    drain(sent.at[:, :, pl.ds(0, members - 1)], send.at[2])
    store.wait()


def frequency_rows(pieces, first, block):
    rows = []
    for c in range(first, first + block):
        parts = []
        for ref in pieces:
            for part in range(2):
                v = ref[:, part, c]
                parts.append(v.reshape(v.shape[0] * v.shape[1], v.shape[2]))
        rows.append(jnp.concatenate(parts, axis=0).T)
    return jnp.concatenate(rows, axis=0)


def level_finish(x_ref, b_ref, half_ref, o_ref):
    block, points, freqs = o_ref.shape[1:]
    value = mm3s(frequency_rows([x_ref.at[g, 0] for g in range(GROUP)], 0, block), b_ref[0], b_ref[1])
    for part in range(2):
        o_ref[part] = half_ref[part] + value[:, part * freqs:(part + 1) * freqs].reshape(block, points, freqs)


def level_local(devices, green, pair_table, mirror_map):
    entries, points, freqs = green.shape[1:]
    side = mirror_map.shape[1]
    plane = side * side
    comps = pair_table.shape[0]
    members = devices // LEVELS
    slots = freqs // (members * PIECES)
    lines = side // LEVELS
    f32, bf16 = jnp.float32, jnp.bfloat16
    times = [piece_times(members, freqs, p) for p in range(PIECES)]
    edges = np.cumsum((0,) + STACKS)
    time_table = np.concatenate([stacked_time_table(np.concatenate(times[a:b]), freqs)
                                 for a, b in zip(edges[:-1], edges[1:])])
    plane_tables = np.stack(plane_table(side, 1.0) + plane_table(side, -1.0))
    groups = PIECES // GROUP
    back = [group_table(members, freqs, g) for g in range(groups)]
    early = np.stack(back[:-1])
    kept = PIECES - GROUP
    hbm = pl.BlockSpec(memory_space=pl.ANY)
    exchanged = (PARTS, members, 2, comps // PARTS, slots, points)
    result = (2, comps, points, freqs)
    cells = (side, entries, 2, slots, points)
    half, last = pl.pallas_call(
        level_kernel,
        out_shape=[jax.ShapeDtypeStruct(result, f32), jax.ShapeDtypeStruct((GROUP,) + exchanged, f32)],
        in_specs=[SMEM, SMEM, hbm, hbm, hbm, hbm],
        out_specs=[hbm, hbm],
        scratch_shapes=[
            pltpu.VMEM(green.shape, f32),
            pltpu.VMEM(time_table.shape, bf16),
            pltpu.VMEM(plane_tables.shape, bf16),
            pltpu.VMEM(early.shape, bf16),
            pltpu.VMEM(plane_tables.shape, bf16),
            pltpu.VMEM((PIECES, members, 2, entries, slots, points), f32),
            pltpu.VMEM((PIECES, members, 2, entries, slots, points), f32),
            pltpu.VMEM((PIECES, 2, LEVELS, 2, lines, entries, slots, points), f32),
            pltpu.VMEM(cells, f32),
            pltpu.VMEM(cells, f32),
            pltpu.VMEM((2, PIECES, 2, comps, 2, lines, slots, points), f32),
            pltpu.VMEM((PIECES,) + exchanged, f32),
            pltpu.VMEM((kept,) + exchanged, f32),
            pltpu.VMEM(result, f32),
            pltpu.SemaphoreType.DMA((5,)),
            pltpu.SemaphoreType.DMA((2 * PIECES,)),
            pltpu.SemaphoreType.DMA((3,)),
            pltpu.SemaphoreType.DMA((PIECES, 2)),
            pltpu.SemaphoreType.DMA((PIECES,)),
            pltpu.SemaphoreType.DMA((PIECES, 2)),
            pltpu.SemaphoreType.DMA((PIECES, PARTS)),
            pltpu.SemaphoreType.DMA((PIECES,)),
        ],
        compiler_params=pltpu.CompilerParams(
            vmem_limit_bytes=60 * 1024 * 1024, collective_id=0, has_side_effects=True
        ),
        cost_estimate=pl.CostEstimate(flops=18 * 10**9, bytes_accessed=16 * 2**20, transcendentals=0),
    )(pair_table.T, mirror_map, green, time_table, plane_tables, early)
    block = comps // 4
    whole = pl.BlockSpec((2, block, points, freqs), lambda i: (0, i, 0, 0))
    return pl.pallas_call(
        level_finish,
        grid=(comps // block,),
        out_shape=jax.ShapeDtypeStruct(result, f32),
        in_specs=[
            pl.BlockSpec((GROUP, 1, members, 2, block, slots, points), lambda i: (0, i // 2, 0, 0, i % 2, 0, 0)),
            pl.BlockSpec(back[-1].shape, lambda i: (0, 0, 0)),
            whole,
        ],
        out_specs=whole,
        compiler_params=pltpu.CompilerParams(vmem_limit_bytes=58 * 1024 * 1024),
        cost_estimate=pl.CostEstimate(flops=6 * 10**9, bytes_accessed=16 * 2**20, transcendentals=0),
    )(last, back[-1], half)


def fits_levels(devices):
    return devices == 32


def solution(mesh):
    placed = (P("set", None, "kb", None), P(), P("set", None))
    devices = mesh.shape["kb"]
    return jax.shard_map(
        functools.partial(level_local if fits_levels(devices) else local, devices),
        mesh=mesh,
        in_specs=placed,
        out_specs=P("set", None, "kb", None),
        check_vma=False,
    )
```

```python
import functools

import numpy as np
import ml_dtypes
import jax
import jax.numpy as jnp
from jax import lax
from jax.experimental import pallas as pl
from jax.experimental.pallas import tpu as pltpu
from jax.sharding import PartitionSpec as P

CHUNKS = 2
SMEM = pl.BlockSpec(memory_space=pltpu.SMEM)


def split_np(table):
    table = table.astype(np.float32)
    high = table.astype(ml_dtypes.bfloat16)
    low = (table - high.astype(np.float32)).astype(ml_dtypes.bfloat16)
    return high, low


def split(x):
    high = x.astype(jnp.bfloat16)
    return high, (x - high.astype(jnp.float32)).astype(jnp.bfloat16)


def mm(a, b, dims):
    return lax.dot_general(a, b, (dims, ((), ())), preferred_element_type=jnp.float32)


def mm3(a, b, dims=((1,), (0,))):
    return mm(a[0], b[0], dims) + mm(a[1], b[0], dims) + mm(a[0], b[1], dims)


def owned_times(devices, freqs, chunk):
    per = freqs // (2 * CHUNKS * devices)
    first = chunk * (freqs // (2 * CHUNKS)) + np.arange(devices)[:, None] * per + np.arange(per)[None, :]
    return np.stack([first, freqs - 1 - first], axis=1).reshape(-1)


def time_tables(times, freqs):
    angle = ((2 * np.arange(freqs)[None, :] - freqs + 1) * (2 * times[:, None] + 1)) % (4 * freqs)
    angle = angle * (2 * np.pi / (4 * freqs))
    scale = freqs**-0.5
    return split_np(scale * np.cos(angle)) + split_np(scale * np.sin(angle))


def frequency_tables(times, freqs):
    angle = ((np.arange(freqs)[None, :] - freqs // 2) * (2 * times[:, None] + 1)) % (2 * freqs)
    angle = angle * (2 * np.pi / (2 * freqs))
    cos, sin = np.cos(angle) * freqs**-0.5, np.sin(angle) * freqs**-0.5
    return split_np(np.block([[cos, sin], [-sin, cos]]))


def plane_table(side, sign):
    index = np.arange(side * side)
    upper, lower = index // side, index % side
    angle = (upper[:, None] * upper[None, :] + lower[:, None] * lower[None, :]) % side * (2 * np.pi / side)
    scale = (side**3) ** -0.5
    cos, sin = scale * np.cos(angle), sign * scale * np.sin(angle)
    return split_np(np.block([[cos, sin], [-sin, cos]]))


def cadd(a, b):
    return a[0] + b[0], a[1] + b[1]


def csub(a, b):
    return a[0] - b[0], a[1] - b[1]


def dft4(a, sign):
    s02, d02 = cadd(a[0], a[2]), csub(a[0], a[2])
    s13, d13 = cadd(a[1], a[3]), csub(a[1], a[3])
    turned = (-d13[1], d13[0]) if sign > 0 else (d13[1], -d13[0])
    return [cadd(s02, s13), cadd(d02, turned), csub(s02, s13), csub(d02, turned)]


def twiddle(a, power, sign):
    if power == 0:
        return a
    if power == 4:
        return (-a[1], a[0]) if sign > 0 else (a[1], -a[0])
    if power in (2, 6):
        r = np.float32(np.sqrt(0.5))
        plus, minus = (a[0] + a[1]) * r, (a[0] - a[1]) * r
        if power == 2:
            return (minus, plus) if sign > 0 else (plus, -minus)
        return (-plus, minus) if sign > 0 else (-minus, -plus)
    c = np.float32(np.cos(2 * np.pi * power / 16))
    s = np.float32(sign * np.sin(2 * np.pi * power / 16))
    return a[0] * c - a[1] * s, a[0] * s + a[1] * c


def dft16(x, sign):
    columns = [dft4([x[4 * n1 + n2] for n1 in range(4)], sign) for n2 in range(4)]
    out = [None] * 16
    for k1 in range(4):
        row = dft4([twiddle(columns[n2][k1], n2 * k1, sign) for n2 in range(4)], sign)
        for k2 in range(4):
            out[k1 + 4 * k2] = row[k2]
    return out


def to_time(g_ref, table, o_ref, p):
    devices, _, entries, slots, points = o_ref.shape[1:]
    freqs = g_ref.shape[-1]
    cos, sin = (table[p, 0], table[p, 1]), (table[p, 2], table[p, 3])
    dims = ((1,), (1,))
    re = split(g_ref[0].reshape(entries * points, freqs))
    im = split(g_ref[1].reshape(entries * points, freqs))
    tau = (mm3(cos, re, dims) + mm3(sin, im, dims), mm3(cos, im, dims) - mm3(sin, re, dims))
    for part in range(2):
        for e in range(entries):
            o_ref[p, :, part, e] = tau[part][:, e * points:(e + 1) * points].reshape(devices, slots, points)


def bubble(pair_ref, mirror_ref, x_ref, ahead, mirrored, inverse, o_ref, y, g, gm, chi, p):
    devices, _, entries, slots, points = x_ref.shape[1:]
    side = y.shape[0]
    plane = side * side
    halves = devices // side
    comps = o_ref.shape[3]

    def forth(e, carry):
        for h in range(halves):
            cells = [(x_ref[p, k * halves + h, 0, e], x_ref[p, k * halves + h, 1, e]) for k in range(side)]
            for k, (re, im) in enumerate(dft16(cells, 1)):
                y[k, e, :, h * points:(h + 1) * points] = re
                y[k, e, :, plane + h * points:plane + (h + 1) * points] = im
        return carry

    lax.fori_loop(0, entries, forth, 0)
    rows = split(y[...].reshape(side * entries * slots, 2 * plane))
    g[...] = mm3(rows, (ahead[0], ahead[1])).reshape(g.shape)
    other = mm3(rows, (mirrored[0], mirrored[1])).reshape(side * entries, slots, 2 * plane)
    other = jnp.concatenate([other[:, slots // 2:], other[:, :slots // 2]], axis=1)
    gm[...] = other.reshape(gm.shape)

    def one(c, carry):
        left, right = pair_ref[0, c], pair_ref[1, c]
        for r in range(side):
            a = g[r, left]
            b = gm[mirror_ref[0, r], right]
            ar, ai, br, bi = a[:, :plane], a[:, plane:], b[:, :plane], b[:, plane:]
            chi[c, r, :, :plane] = ar * br - ai * bi
            chi[c, r, :, plane:] = ar * bi + ai * br
        return carry

    lax.fori_loop(0, comps, one, 0)
    rows = split(chi[...].reshape(comps * side * slots, 2 * plane))
    chi[...] = mm3(rows, (inverse[0], inverse[1])).reshape(chi.shape)

    def back(c, carry):
        for h in range(halves):
            lanes = slice(h * points, (h + 1) * points)
            high = slice(plane + h * points, plane + (h + 1) * points)
            cells = [(chi[c, r, :, lanes], chi[c, r, :, high]) for r in range(side)]
            for q, (re, im) in enumerate(dft16(cells, -1)):
                o_ref[p, q * halves + h, 0, c] = re
                o_ref[p, q * halves + h, 1, c] = im
        return carry

    lax.fori_loop(0, comps, back, 0)


def main_kernel(pair_ref, mirror_ref, green_hbm, time_hbm, plane_hbm, back_hbm, half_hbm, last,
                green, table, planes, back, mirrored, tau, x, y, g, gm, chi, sent, got, acc,
                load, own, send, recv):
    devices = tau.shape[1]
    side = y.shape[0]
    plane = side * side
    me = lax.axis_index("kb")
    loads = [pltpu.make_async_copy(src, dst, load.at[i])
             for i, (src, dst) in enumerate([(time_hbm, table), (plane_hbm, planes), (back_hbm, back),
                                       (green_hbm, green)])]
    for i in (3, 0, 1, 2):
        loads[i].start()
    barrier = pltpu.get_barrier_semaphore()

    def greet(s, carry):
        pl.semaphore_signal(barrier, inc=1, device_id={"kb": lax.rem(me + s, devices)},
                            device_id_type=pl.DeviceIdType.MESH)
        return carry

    lax.fori_loop(1, devices, greet, 0)

    def partner(shift):
        total, bit = 0, 1
        while bit < devices:
            total += bit * lax.rem(me // bit + shift // bit, 2)
            bit *= 2
        return total

    def exchange(src, dst, n):
        pltpu.make_async_copy(src.at[me], dst.at[me], own.at[n]).start()

        def one(i, carry):
            other = partner(i // 4 + devices // 4 * lax.rem(i + 2, 4))
            pltpu.make_async_remote_copy(
                src_ref=src.at[other], dst_ref=dst.at[me], send_sem=send.at[n], recv_sem=recv.at[n],
                device_id={"kb": other}, device_id_type=pl.DeviceIdType.MESH,
            ).start()
            return carry

        lax.fori_loop(0, 2, one, 0)
        lax.fori_loop(3, devices, one, 0)

    def finish(ref, sem):
        part = ref.at[pl.ds(0, devices - 1)]
        pltpu.make_async_copy(part, part, sem).wait()

    loads[3].wait()
    loads[0].wait()
    for p in range(CHUNKS):
        to_time(green, table, tau, p)
        if p == 0:
            pl.semaphore_wait(barrier, devices - 1)
        exchange(tau.at[p], x.at[p], p)
    loads[1].wait()
    lane = lax.broadcasted_iota(jnp.int32, (plane, plane), 1)
    ry, rz = lane // side, lane % side
    target = (mirror_ref[1, 0] + side - ry) % side * side + (mirror_ref[2, 0] + side - rz) % side
    pick = (lax.broadcasted_iota(jnp.int32, (plane, plane), 0) == target).astype(jnp.float32).astype(jnp.bfloat16)
    for i in range(2):
        for part in range(2):
            lanes = slice(part * plane, (part + 1) * plane)
            mirrored[i, :, lanes] = mm(planes[i, :, lanes], pick, ((1,), (0,))).astype(jnp.bfloat16)
    landing = [got, last]
    for p in range(CHUNKS):
        pltpu.make_async_copy(tau.at[p, me], x.at[p, me], own.at[p]).wait()
        finish(x.at[p], recv.at[p])
        bubble(pair_ref, mirror_ref, x, planes.at[0:2], mirrored, planes.at[2:4], sent, y, g, gm, chi, p)
        exchange(sent.at[p], landing[p], CHUNKS + p)
    pltpu.make_async_copy(sent.at[0, me], got.at[me], own.at[CHUNKS]).wait()
    finish(got, recv.at[CHUNKS])
    loads[2].wait()
    comps = got.shape[2]
    block = comps // 2
    for i in range(2):
        chosen = slice(i * block, (i + 1) * block)
        value = to_frequency(got.at[:, :, chosen], back)
        for part in range(2):
            acc[part, chosen] = value[part]
    store = pltpu.make_async_copy(acc, half_hbm, load.at[4])
    store.start()
    for p in range(CHUNKS):
        finish(tau.at[p], send.at[p])
        finish(sent.at[p], send.at[CHUNKS + p])
    store.wait()
    pltpu.make_async_copy(sent.at[1, me], last.at[me], own.at[CHUNKS + 1]).wait()
    finish(last, recv.at[CHUNKS + 1])


def to_frequency(x_ref, b_ref):
    devices, _, block, slots, points = x_ref.shape
    freqs = b_ref.shape[-1] // 2
    rows = []
    for c in range(block):
        parts = [x_ref[:, part, c].reshape(devices * slots, points).T for part in range(2)]
        rows.append(jnp.concatenate(parts, axis=1))
    value = mm3(split(jnp.concatenate(rows, axis=0)), (b_ref[0], b_ref[1]))
    return [value[:, part * freqs:(part + 1) * freqs].reshape(block, points, freqs) for part in range(2)]


def finish_kernel(x_ref, b_ref, half_ref, o_ref):
    value = to_frequency(x_ref, b_ref)
    for part in range(2):
        o_ref[part] = half_ref[part] + value[part]


def local(devices, green, pair_table, mirror_map):
    entries, points, freqs = green.shape[1:]
    side = mirror_map.shape[1]
    plane = side * side
    comps = pair_table.shape[0]
    slots = freqs // (devices * CHUNKS)
    f32, bf16 = jnp.float32, jnp.bfloat16
    times = [owned_times(devices, freqs, p) for p in range(CHUNKS)]
    time_table = np.stack([np.stack(time_tables(t, freqs)) for t in times])
    plane_tables = np.stack(plane_table(side, 1.0) + plane_table(side, -1.0))
    frequency_table = [np.stack(frequency_tables(t, freqs)) for t in times]
    hbm = pl.BlockSpec(memory_space=pl.ANY)
    cells = (side, entries, slots, 2 * plane)
    exchanged = (devices, 2, comps, slots, points)
    result = (2, comps, points, freqs)
    half, last = pl.pallas_call(
        main_kernel,
        out_shape=[jax.ShapeDtypeStruct(result, f32), jax.ShapeDtypeStruct(exchanged, f32)],
        in_specs=[SMEM, SMEM, hbm, hbm, hbm, hbm],
        out_specs=[hbm, hbm],
        scratch_shapes=[
            pltpu.VMEM(green.shape, f32),
            pltpu.VMEM(time_table.shape, bf16),
            pltpu.VMEM(plane_tables.shape, bf16),
            pltpu.VMEM(frequency_table[0].shape, bf16),
            pltpu.VMEM((2, 2 * plane, 2 * plane), bf16),
            pltpu.VMEM((CHUNKS, devices, 2, entries, slots, points), f32),
            pltpu.VMEM((CHUNKS, devices, 2, entries, slots, points), f32),
            pltpu.VMEM(cells, f32),
            pltpu.VMEM(cells, f32),
            pltpu.VMEM(cells, f32),
            pltpu.VMEM((comps,) + (side, slots, 2 * plane), f32),
            pltpu.VMEM((CHUNKS,) + exchanged, f32),
            pltpu.VMEM(exchanged, f32),
            pltpu.VMEM(result, f32),
            pltpu.SemaphoreType.DMA((5,)),
            pltpu.SemaphoreType.DMA((2 * CHUNKS,)),
            pltpu.SemaphoreType.DMA((2 * CHUNKS,)),
            pltpu.SemaphoreType.DMA((2 * CHUNKS,)),
        ],
        compiler_params=pltpu.CompilerParams(
            vmem_limit_bytes=60 * 1024 * 1024, collective_id=0, has_side_effects=True
        ),
        cost_estimate=pl.CostEstimate(flops=18 * 10**9, bytes_accessed=16 * 2**20, transcendentals=0),
    )(pair_table.T, mirror_map, green, time_table, plane_tables, frequency_table[0])
    block = comps // 4
    whole = pl.BlockSpec((2, block, points, freqs), lambda i: (0, i, 0, 0))
    return pl.pallas_call(
        finish_kernel,
        grid=(comps // block,),
        out_shape=jax.ShapeDtypeStruct(result, f32),
        in_specs=[
            pl.BlockSpec((devices, 2, block, slots, points), lambda i: (0, 0, i, 0, 0)),
            pl.BlockSpec(frequency_table[1].shape, lambda i: (0, 0, 0)),
            whole,
        ],
        out_specs=whole,
        compiler_params=pltpu.CompilerParams(vmem_limit_bytes=58 * 1024 * 1024),
        cost_estimate=pl.CostEstimate(flops=6 * 10**9, bytes_accessed=16 * 2**20, transcendentals=0),
    )(last, frequency_table[1], half)


LEVELS = 4
PIECES = 8
STACKS = (1, 3, 4)
PARTS = 4
HALVES = 2
GROUP = 2


def piece_times(members, freqs, piece):
    per = freqs // (2 * PIECES * members)
    first = piece * (freqs // (2 * PIECES)) + np.arange(members)[:, None] * per + np.arange(per)[None, :]
    return np.stack([first, freqs - 1 - first], axis=1).reshape(-1)


def stacked_time_table(times, freqs):
    cos_high, cos_low, sin_high, sin_low = time_tables(times, freqs)
    return np.concatenate([cos_high, sin_high, cos_low, sin_low])


def group_table(members, freqs, pieces):
    rows = []
    for piece in pieces:
        times = piece_times(members, freqs, piece)
        angle = ((np.arange(freqs)[None, :] - freqs // 2) * (2 * times[:, None] + 1)) % (2 * freqs)
        angle = angle * (2 * np.pi / (2 * freqs))
        cos, sin = np.cos(angle) * freqs**-0.5, np.sin(angle) * freqs**-0.5
        rows.append(np.block([[cos, sin], [-sin, cos]]))
    return np.stack(split_np(np.concatenate(rows)))


def mm3s(rows, high, low):
    m = rows.shape[0]
    a, b = split(rows)
    both = mm(jnp.concatenate([a, b], axis=0), high, ((1,), (0,)))
    return both[:m] + both[m:] + mm(a, low, ((1,), (0,)))


def dft16_half(columns, sigma):
    out = [None] * 8
    for k1 in range(4):
        a = [twiddle(columns[n2][k1], n2 * k1, -1) for n2 in range(4)]
        s02, d02 = cadd(a[0], a[2]), csub(a[0], a[2])
        s13, d13 = cadd(a[1], a[3]), csub(a[1], a[3])
        out[k1] = (s02[0] + sigma * s13[0], s02[1] + sigma * s13[1])
        out[4 + k1] = (d02[0] + sigma * d13[1], d02[1] - sigma * d13[0])
    return out


def level_kernel(pair_ref, mirror_ref, green_hbm, time_hbm, plane_hbm, back_hbm, half_hbm, last,
                 green, table, planes, back, mirrored, tau, x, zbuf, t, ts, chi, sent, got, acc,
                 load, own, send, sendz, recv1, recvz, recvc, recv2):
    members = tau.shape[2]
    entries = green.shape[1]
    few, slots, points = tau.shape[4:]
    side = t.shape[0]
    lines = side // LEVELS
    plane = side * side
    comps = sent.shape[1] * sent.shape[4]
    group = sent.shape[4]
    freqs = green.shape[-1]
    kept = got.shape[0]
    me = lax.axis_index("kb")
    z, d = me // members, lax.rem(me, members)
    middle = jnp.logical_or(z == 1, z == 2)
    edge = jnp.logical_not(middle)
    mine = lax.rem(z, 2)
    half = slots // 2

    start = 4 * members * slots * STACKS[0]
    pairs = [(green_hbm.at[:, pl.ds(i * few, few)], green.at[:, pl.ds(i * few, few)]) for i in range(HALVES)]
    pairs += [(time_hbm.at[pl.ds(0, start)], table.at[pl.ds(0, start)]),
              (time_hbm.at[pl.ds(start, table.shape[0] - start)], table.at[pl.ds(start, table.shape[0] - start)]),
              (plane_hbm, planes), (back_hbm, back)]
    loads = [pltpu.make_async_copy(src, dst, load.at[i]) for i, (src, dst) in enumerate(pairs)]
    for i in (0, 2, 1):
        loads[i].start()
    barrier = pltpu.get_barrier_semaphore()

    def greet(other):
        pl.semaphore_signal(barrier, inc=1, device_id={"kb": other}, device_id_type=pl.DeviceIdType.MESH)

    def greet_member(s, carry):
        greet(z * members + lax.rem(d + s, members))
        return carry

    lax.fori_loop(1, members, greet_member, 0)
    for s in range(1, LEVELS):
        greet(lax.rem(z + s, LEVELS) * members + d)

    def partner(shift):
        total, bit = 0, 1
        while bit < members:
            total += bit * lax.rem(d // bit + shift // bit, 2)
            bit *= 2
        return total

    def remote(src, dst, send_sem, recv_sem, other):
        pltpu.make_async_remote_copy(
            src_ref=src, dst_ref=dst, send_sem=send_sem, recv_sem=recv_sem,
            device_id={"kb": other}, device_id_type=pl.DeviceIdType.MESH,
        ).start()

    def exchange(src, dst, own_sem, send_sem, recv_sem):
        pltpu.make_async_copy(src.at[d], dst.at[d], own_sem).start()

        def one(i, carry):
            other = partner(members - i)
            remote(src.at[other], dst.at[d], send_sem, recv_sem, z * members + other)
            return carry

        lax.fori_loop(1, members, one, 0)

    def drain(ref, sem):
        pltpu.make_async_copy(ref, ref, sem).wait()

    def finish(src, dst, own_sem, recv_sem):
        pltpu.make_async_copy(src.at[d], dst.at[d], own_sem).wait()
        drain(dst.at[pl.ds(0, members - 1)], recv_sem)

    def finish_parts(p, dst):
        pltpu.make_async_copy(sent.at[p, :, d], dst.at[:, d], own.at[PIECES + p, 0]).wait()
        drain(dst.at[:, pl.ds(0, members - 1)], recv2.at[p])

    dims = ((1,), (1,))

    def split_entries(i):
        return [split(green[part, i * few:(i + 1) * few].reshape(few * points, freqs)) for part in range(2)]

    def times_of(first, count, i, values):
        times = count * members * slots
        base = 4 * members * slots * first
        stack = table[base:base + 4 * times]
        outs = []
        for value in values:
            a = mm(stack, value[0], dims)
            outs.append(a[:2 * times] + a[2 * times:] + mm(stack[:2 * times], value[1], dims))
        both = (outs[0][:times] + outs[1][times:], outs[1][:times] - outs[0][times:])
        for part in range(2):
            for e in range(few):
                tau[first:first + count, i, :, part, e] = both[part][:, e * points:(e + 1) * points].reshape(
                    count, members, slots, points)

    def exchange_times(p, i):
        exchange(tau.at[p, i], x.at[p, i], own.at[p, i], send.at[0], recv1.at[p, i])

    loads[0].wait()
    loads[2].wait()
    values = []
    for i in range(HALVES):
        if i == 1:
            loads[1].wait()
        values.append(split_entries(i))
        times_of(0, STACKS[0], i, values[i])
        if i == 0:
            pl.semaphore_wait(barrier, members - 1 + LEVELS - 1)
            for n in range(3, len(loads)):
                loads[n].start()
        exchange_times(0, i)
    loads[4].wait()
    lane = lax.broadcasted_iota(jnp.int32, (plane, plane), 1)
    ry, rz = lane // side, lane % side
    target = (mirror_ref[1, 0] + side - ry) % side * side + (mirror_ref[2, 0] + side - rz) % side
    pick = (lax.broadcasted_iota(jnp.int32, (plane, plane), 0) == target).astype(jnp.float32).astype(jnp.bfloat16)
    for i in range(2):
        for part in range(2):
            lanes = slice(part * plane, (part + 1) * plane)
            mirrored[i, :, lanes] = mm(planes[i, :, lanes], pick, ((1,), (0,))).astype(jnp.bfloat16)
            mirrored[2 + i, lanes, :] = mm(pick, planes[2 + i, lanes, :], ((1,), (0,))).astype(jnp.bfloat16)

    def both_ways(rows, base):
        straight = mm3s(rows, planes[base], planes[base + 1])
        turned = mm3s(rows, mirrored[base], mirrored[base + 1])
        slot = lax.broadcasted_iota(jnp.int32, straight.shape, 0) % slots
        return jnp.where(slot < half, straight, turned)

    def forward(p, first, count, follow=True):
        for i in range(first, first + count):
            finish(tau.at[p, i], x.at[p, i], own.at[p, i], recv1.at[p, i])

            if follow:
                @pl.when(p + 1 < PIECES)
                def _():
                    exchange_times(p + 1, i)

        v = x[p, first:first + count].reshape(count, lines, 2, 2, few, slots, points)
        rows = jnp.concatenate([v[:, :, h, part].reshape(count * lines * few * slots, points)
                                for part in range(2) for h in range(2)], axis=1)
        out = both_ways(rows, 0)
        for h in range(2):
            for part in range(2):
                lanes = slice(part * plane + h * points, part * plane + (h + 1) * points)
                zbuf[p, h, first:first + count, z, part] = out[:, lanes].reshape(count, lines, few, slots, points)

    def send_lines(p, h, first, count):
        for i in range(first, first + count):
            for level in (1, 2):
                @pl.when(z != level)
                def _():
                    remote(zbuf.at[p, h, i, z], zbuf.at[p, h, i, z], sendz.at[p, h], recvz.at[p, h],
                           level * members + d)

    def middle_work(p, h):
        sigma = jnp.where(z == 1, 1.0, -1.0).astype(jnp.float32)

        def forth(e, carry):
            i, f = e // few, lax.rem(e, few)
            cells = [(zbuf[p, h, i, k // lines, 0, k % lines, f], zbuf[p, h, i, k // lines, 1, k % lines, f])
                     for k in range(side)]
            for r, pair in enumerate(dft16(cells, 1)):
                for part in range(2):
                    v = pair[part]
                    t[r, e, part] = v
                    ts[r, e, part] = jnp.concatenate([v[half:], v[:half]], axis=0)
            return carry

        lax.fori_loop(0, entries, forth, 0)

        def one(c, carry):
            left, right = pair_ref[0, c], pair_ref[1, c]
            columns = []
            for n2 in range(4):
                cells = []
                for n1 in range(4):
                    r = 4 * n1 + n2
                    a, b = t[r, left], ts[mirror_ref[0, r], right]
                    cells.append((a[0] * b[0] - a[1] * b[1], a[0] * b[1] + a[1] * b[0]))
                columns.append(dft4(cells, -1))
            for i, pair in enumerate(dft16_half(columns, sigma)):
                for part in range(2):
                    chi[i // lines, p, h, c, part, i % lines] = pair[part]
            remote(chi.at[1 - mine, p, h, c], chi.at[1 - mine, p, h, c], send.at[1], recvc.at[p, c // group],
                   jnp.where(z == 1, 0, 3) * members + d)
            return carry

        lax.fori_loop(0, comps, one, 0)

    def backward(p, first, count):
        @pl.when(edge)
        def _():
            for n in range(first, first + count):
                drain(chi.at[mine, p, :, pl.ds(n * group, group)], recvc.at[p, n])

        v = chi[mine, p, :, first * group:(first + count) * group]
        rows = jnp.concatenate([v[h, :, part].reshape(count * group * lines * slots, points)
                                for part in range(2) for h in range(2)], axis=1)
        out = both_ways(rows, 2).reshape(count, group, lines, slots, 2 * plane)
        for q in range(lines):
            for h in range(2):
                for part in range(2):
                    lanes = slice(part * plane + h * points, part * plane + (h + 1) * points)
                    sent[p, first:first + count, 2 * q + h, part] = out[:, :, q, :, lanes]

        for n in range(first, first + count):
            @pl.when(p < kept)
            def _():
                exchange(sent.at[p, n], got.at[p, n], own.at[PIECES + p, 0], send.at[2], recv2.at[p])

            @pl.when(p >= kept)
            def _():
                exchange(sent.at[p, n], last.at[p - kept, n], own.at[PIECES + p, 0], send.at[2], recv2.at[p])

    span = 2 * GROUP * members * slots

    def frequency(pieces, first, depth):
        block = 2 * group
        high, low = back[0, pl.ds(first, depth)], back[1, pl.ds(first, depth)]
        for i in range(comps // block):
            chosen = slice(i * block, (i + 1) * block)
            rows = frequency_rows([[got.at[p, c // group, :, :, c % group] for p in pieces]
                                   for c in range(i * block, (i + 1) * block)])
            value = mm3s(rows, high, low)
            for part in range(2):
                acc[part, chosen] += value[:, part * freqs:(part + 1) * freqs].reshape(block, points, freqs)

    for i in range(HALVES):
        forward(0, i, 1, False)
        send_lines(0, 0, i, 1)
    send_lines(0, 1, 0, HALVES)
    loads[3].wait()
    for i in range(HALVES):
        times_of(STACKS[0], STACKS[1], i, values[i])
        exchange_times(1, i)
    for i in range(HALVES):
        times_of(STACKS[0] + STACKS[1], STACKS[2], i, values[i])
    acc[...] = jnp.zeros(acc.shape, jnp.float32)
    forward(1, 0, HALVES)
    loads[5].wait()

    def step(p, carry):
        for h in range(2):
            @pl.when(middle)
            def _():
                drain(zbuf.at[p, h, :, pl.ds(0, LEVELS - 1)], recvz.at[p, h])

            @pl.when(edge)
            def _():
                drain(zbuf.at[p, h, :, pl.ds(0, 2)], sendz.at[p, h])

            @pl.when(p + 1 < PIECES)
            def _():
                send_lines(p + 1, h, 0, HALVES)

            @pl.when(middle)
            def _():
                middle_work(p, h)

            @pl.when(middle if h == 1 else jnp.logical_and(edge, p > 0))
            def _():
                backward(p if h == 1 else p - 1, 0, PARTS)

        @pl.when(p + 2 < PIECES)
        def _():
            forward(p + 2, 0, HALVES)

        @pl.when(jnp.logical_and(lax.rem(p, GROUP) == GROUP - 1, p >= 2 * GROUP - 1))
        def _():
            m = p // GROUP - 1

            def arrived(q, carry):
                finish_parts(q, got.at[q])
                return carry

            lax.fori_loop(m * GROUP, (m + 1) * GROUP, arrived, 0)
            frequency([m * GROUP + g for g in range(GROUP)], m * span, span)

        return carry

    lax.fori_loop(0, PIECES, step, 0)
    end = PIECES - 1

    @pl.when(edge)
    def _():
        backward(end, 0, 2)

    finish_parts(end - 1, got.at[end - 1])
    frequency([end - 1], back.shape[1] - span // GROUP, span // GROUP)
    store = pltpu.make_async_copy(acc, half_hbm, load.at[7])
    store.start()

    @pl.when(edge)
    def _():
        for n in range(2, PARTS):
            backward(end, n, 1)

    drain(tau.at[:, :, pl.ds(0, members - 1)], send.at[0])

    @pl.when(middle)
    def _():
        def gone(p, carry):
            for h in range(2):
                drain(zbuf.at[p, h, :, 0], sendz.at[p, h])
            return carry

        lax.fori_loop(0, PIECES, gone, 0)
        drain(chi.at[0], send.at[1])

    finish_parts(end, last.at[end - kept])
    drain(sent.at[:, :, pl.ds(0, members - 1)], send.at[2])
    store.wait()


def frequency_rows(blocks):
    rows = []
    for pieces in blocks:
        parts = []
        for ref in pieces:
            for part in range(2):
                v = ref[:, part]
                parts.append(v.reshape(v.shape[0] * v.shape[1], v.shape[2]))
        rows.append(jnp.concatenate(parts, axis=0).T)
    return jnp.concatenate(rows, axis=0)


def level_finish(x_hbm, b_hbm, half_hbm, o_hbm, x, b_ref, total, sem):
    points, freqs = total.shape[2:]
    group = x.shape[3]
    spans = [pl.ds(n * group, group) for n in range(PARTS)]
    ahead = [pltpu.make_async_copy(x_hbm.at[0, n], x.at[n], sem.at[0, n]) for n in range(PARTS)]
    halves = [pltpu.make_async_copy(half_hbm.at[:, span], total.at[:, span], sem.at[1, n])
              for n, span in enumerate(spans)]
    stores = [pltpu.make_async_copy(total.at[:, span], o_hbm.at[:, span], sem.at[2, n])
              for n, span in enumerate(spans)]
    tables = pltpu.make_async_copy(b_hbm, b_ref, sem.at[3, 0])
    for copy in [tables] + ahead + halves:
        copy.start()
    tables.wait()
    for n in range(PARTS):
        chosen = slice(n * group, (n + 1) * group)
        ahead[n].wait()
        value = mm3s(frequency_rows([[x.at[n, :, :, c]] for c in range(group)]), b_ref[0], b_ref[1])
        halves[n].wait()
        for part in range(2):
            total[part, chosen] += value[:, part * freqs:(part + 1) * freqs].reshape(group, points, freqs)
        stores[n].start()
    for store in stores:
        store.wait()


def level_local(devices, green, pair_table, mirror_map):
    entries, points, freqs = green.shape[1:]
    side = mirror_map.shape[1]
    plane = side * side
    comps = pair_table.shape[0]
    members = devices // LEVELS
    slots = freqs // (members * PIECES)
    lines = side // LEVELS
    few = entries // HALVES
    f32, bf16 = jnp.float32, jnp.bfloat16
    times = [piece_times(members, freqs, p) for p in range(PIECES)]
    edges = np.cumsum((0,) + STACKS)
    time_table = np.concatenate([stacked_time_table(np.concatenate(times[a:b]), freqs)
                                 for a, b in zip(edges[:-1], edges[1:])])
    plane_tables = np.stack(plane_table(side, 1.0) + plane_table(side, -1.0))
    groups = PIECES // GROUP
    early = np.concatenate([group_table(members, freqs, range(g * GROUP, (g + 1) * GROUP)) for g in range(groups - 1)]
                           + [group_table(members, freqs, [PIECES - 2])], axis=1)
    final = group_table(members, freqs, [PIECES - 1])
    kept = PIECES - 1
    hbm = pl.BlockSpec(memory_space=pl.ANY)
    exchanged = (PARTS, members, 2, comps // PARTS, slots, points)
    result = (2, comps, points, freqs)
    cells = (side, entries, 2, slots, points)
    half, last = pl.pallas_call(
        level_kernel,
        out_shape=[jax.ShapeDtypeStruct(result, f32), jax.ShapeDtypeStruct((1,) + exchanged, f32)],
        in_specs=[SMEM, SMEM, hbm, hbm, hbm, hbm],
        out_specs=[hbm, hbm],
        scratch_shapes=[
            pltpu.VMEM(green.shape, f32),
            pltpu.VMEM(time_table.shape, bf16),
            pltpu.VMEM(plane_tables.shape, bf16),
            pltpu.VMEM(early.shape, bf16),
            pltpu.VMEM(plane_tables.shape, bf16),
            pltpu.VMEM((PIECES, HALVES, members, 2, few, slots, points), f32),
            pltpu.VMEM((PIECES, HALVES, members, 2, few, slots, points), f32),
            pltpu.VMEM((PIECES, 2, HALVES, LEVELS, 2, lines, few, slots, points), f32),
            pltpu.VMEM(cells, f32),
            pltpu.VMEM(cells, f32),
            pltpu.VMEM((2, PIECES, 2, comps, 2, lines, slots, points), f32),
            pltpu.VMEM((PIECES,) + exchanged, f32),
            pltpu.VMEM((kept,) + exchanged, f32),
            pltpu.VMEM(result, f32),
            pltpu.SemaphoreType.DMA((8,)),
            pltpu.SemaphoreType.DMA((2 * PIECES, HALVES)),
            pltpu.SemaphoreType.DMA((3,)),
            pltpu.SemaphoreType.DMA((PIECES, 2)),
            pltpu.SemaphoreType.DMA((PIECES, HALVES)),
            pltpu.SemaphoreType.DMA((PIECES, 2)),
            pltpu.SemaphoreType.DMA((PIECES, PARTS)),
            pltpu.SemaphoreType.DMA((PIECES,)),
        ],
        compiler_params=pltpu.CompilerParams(
            vmem_limit_bytes=60 * 1024 * 1024, collective_id=0, has_side_effects=True
        ),
        cost_estimate=pl.CostEstimate(flops=18 * 10**9, bytes_accessed=16 * 2**20, transcendentals=0),
    )(pair_table.T, mirror_map, green, time_table, plane_tables, early)
    return pl.pallas_call(
        level_finish,
        out_shape=jax.ShapeDtypeStruct(result, f32),
        in_specs=[hbm, hbm, hbm],
        out_specs=hbm,
        scratch_shapes=[
            pltpu.VMEM(exchanged, f32),
            pltpu.VMEM(final.shape, bf16),
            pltpu.VMEM(result, f32),
            pltpu.SemaphoreType.DMA((4, PARTS)),
        ],
        compiler_params=pltpu.CompilerParams(vmem_limit_bytes=60 * 1024 * 1024),
        cost_estimate=pl.CostEstimate(flops=6 * 10**9, bytes_accessed=16 * 2**20, transcendentals=0),
    )(last, final, half)


def fits_levels(devices):
    return devices == 32


def solution(mesh):
    placed = (P("set", None, "kb", None), P(), P("set", None))
    devices = mesh.shape["kb"]
    return jax.shard_map(
        functools.partial(level_local if fits_levels(devices) else local, devices),
        mesh=mesh,
        in_specs=placed,
        out_specs=P("set", None, "kb", None),
        check_vma=False,
    )
```

```python
import functools

import numpy as np
import ml_dtypes
import jax
import jax.numpy as jnp
from jax import lax
from jax.experimental import pallas as pl
from jax.experimental.pallas import tpu as pltpu
from jax.sharding import PartitionSpec as P

CHUNKS = 2
SMEM = pl.BlockSpec(memory_space=pltpu.SMEM)


def split_np(table):
    table = table.astype(np.float32)
    high = table.astype(ml_dtypes.bfloat16)
    low = (table - high.astype(np.float32)).astype(ml_dtypes.bfloat16)
    return high, low


def split(x):
    high = x.astype(jnp.bfloat16)
    return high, (x - high.astype(jnp.float32)).astype(jnp.bfloat16)


def mm(a, b, dims):
    return lax.dot_general(a, b, (dims, ((), ())), preferred_element_type=jnp.float32)


def mm3(a, b, dims=((1,), (0,))):
    return mm(a[0], b[0], dims) + mm(a[1], b[0], dims) + mm(a[0], b[1], dims)


def owned_times(devices, freqs, chunk):
    per = freqs // (2 * CHUNKS * devices)
    first = chunk * (freqs // (2 * CHUNKS)) + np.arange(devices)[:, None] * per + np.arange(per)[None, :]
    return np.stack([first, freqs - 1 - first], axis=1).reshape(-1)


def time_tables(times, freqs):
    angle = ((2 * np.arange(freqs)[None, :] - freqs + 1) * (2 * times[:, None] + 1)) % (4 * freqs)
    angle = angle * (2 * np.pi / (4 * freqs))
    scale = freqs**-0.5
    return split_np(scale * np.cos(angle)) + split_np(scale * np.sin(angle))


def frequency_tables(times, freqs):
    angle = ((np.arange(freqs)[None, :] - freqs // 2) * (2 * times[:, None] + 1)) % (2 * freqs)
    angle = angle * (2 * np.pi / (2 * freqs))
    cos, sin = np.cos(angle) * freqs**-0.5, np.sin(angle) * freqs**-0.5
    return split_np(np.block([[cos, sin], [-sin, cos]]))


def plane_table(side, sign):
    index = np.arange(side * side)
    upper, lower = index // side, index % side
    angle = (upper[:, None] * upper[None, :] + lower[:, None] * lower[None, :]) % side * (2 * np.pi / side)
    scale = (side**3) ** -0.5
    cos, sin = scale * np.cos(angle), sign * scale * np.sin(angle)
    return split_np(np.block([[cos, sin], [-sin, cos]]))


def cadd(a, b):
    return a[0] + b[0], a[1] + b[1]


def csub(a, b):
    return a[0] - b[0], a[1] - b[1]


def dft4(a, sign):
    s02, d02 = cadd(a[0], a[2]), csub(a[0], a[2])
    s13, d13 = cadd(a[1], a[3]), csub(a[1], a[3])
    turned = (-d13[1], d13[0]) if sign > 0 else (d13[1], -d13[0])
    return [cadd(s02, s13), cadd(d02, turned), csub(s02, s13), csub(d02, turned)]


def twiddle(a, power, sign):
    if power == 0:
        return a
    if power == 4:
        return (-a[1], a[0]) if sign > 0 else (a[1], -a[0])
    if power in (2, 6):
        r = np.float32(np.sqrt(0.5))
        plus, minus = (a[0] + a[1]) * r, (a[0] - a[1]) * r
        if power == 2:
            return (minus, plus) if sign > 0 else (plus, -minus)
        return (-plus, minus) if sign > 0 else (-minus, -plus)
    c = np.float32(np.cos(2 * np.pi * power / 16))
    s = np.float32(sign * np.sin(2 * np.pi * power / 16))
    return a[0] * c - a[1] * s, a[0] * s + a[1] * c


def dft16(x, sign):
    columns = [dft4([x[4 * n1 + n2] for n1 in range(4)], sign) for n2 in range(4)]
    out = [None] * 16
    for k1 in range(4):
        row = dft4([twiddle(columns[n2][k1], n2 * k1, sign) for n2 in range(4)], sign)
        for k2 in range(4):
            out[k1 + 4 * k2] = row[k2]
    return out


def to_time(g_ref, table, o_ref, p):
    devices, _, entries, slots, points = o_ref.shape[1:]
    freqs = g_ref.shape[-1]
    cos, sin = (table[p, 0], table[p, 1]), (table[p, 2], table[p, 3])
    dims = ((1,), (1,))
    re = split(g_ref[0].reshape(entries * points, freqs))
    im = split(g_ref[1].reshape(entries * points, freqs))
    tau = (mm3(cos, re, dims) + mm3(sin, im, dims), mm3(cos, im, dims) - mm3(sin, re, dims))
    for part in range(2):
        for e in range(entries):
            o_ref[p, :, part, e] = tau[part][:, e * points:(e + 1) * points].reshape(devices, slots, points)


def bubble(pair_ref, mirror_ref, x_ref, ahead, mirrored, inverse, o_ref, y, g, gm, chi, p):
    devices, _, entries, slots, points = x_ref.shape[1:]
    side = y.shape[0]
    plane = side * side
    halves = devices // side
    comps = o_ref.shape[3]

    def forth(e, carry):
        for h in range(halves):
            cells = [(x_ref[p, k * halves + h, 0, e], x_ref[p, k * halves + h, 1, e]) for k in range(side)]
            for k, (re, im) in enumerate(dft16(cells, 1)):
                y[k, e, :, h * points:(h + 1) * points] = re
                y[k, e, :, plane + h * points:plane + (h + 1) * points] = im
        return carry

    lax.fori_loop(0, entries, forth, 0)
    rows = split(y[...].reshape(side * entries * slots, 2 * plane))
    g[...] = mm3(rows, (ahead[0], ahead[1])).reshape(g.shape)
    other = mm3(rows, (mirrored[0], mirrored[1])).reshape(side * entries, slots, 2 * plane)
    other = jnp.concatenate([other[:, slots // 2:], other[:, :slots // 2]], axis=1)
    gm[...] = other.reshape(gm.shape)

    def one(c, carry):
        left, right = pair_ref[0, c], pair_ref[1, c]
        for r in range(side):
            a = g[r, left]
            b = gm[mirror_ref[0, r], right]
            ar, ai, br, bi = a[:, :plane], a[:, plane:], b[:, :plane], b[:, plane:]
            chi[c, r, :, :plane] = ar * br - ai * bi
            chi[c, r, :, plane:] = ar * bi + ai * br
        return carry

    lax.fori_loop(0, comps, one, 0)
    rows = split(chi[...].reshape(comps * side * slots, 2 * plane))
    chi[...] = mm3(rows, (inverse[0], inverse[1])).reshape(chi.shape)

    def back(c, carry):
        for h in range(halves):
            lanes = slice(h * points, (h + 1) * points)
            high = slice(plane + h * points, plane + (h + 1) * points)
            cells = [(chi[c, r, :, lanes], chi[c, r, :, high]) for r in range(side)]
            for q, (re, im) in enumerate(dft16(cells, -1)):
                o_ref[p, q * halves + h, 0, c] = re
                o_ref[p, q * halves + h, 1, c] = im
        return carry

    lax.fori_loop(0, comps, back, 0)


def main_kernel(pair_ref, mirror_ref, green_hbm, time_hbm, plane_hbm, back_hbm, half_hbm, last,
                green, table, planes, back, mirrored, tau, x, y, g, gm, chi, sent, got, acc,
                load, own, send, recv):
    devices = tau.shape[1]
    side = y.shape[0]
    plane = side * side
    me = lax.axis_index("kb")
    loads = [pltpu.make_async_copy(src, dst, load.at[i])
             for i, (src, dst) in enumerate([(time_hbm, table), (plane_hbm, planes), (back_hbm, back),
                                       (green_hbm, green)])]
    for i in (3, 0, 1, 2):
        loads[i].start()
    barrier = pltpu.get_barrier_semaphore()

    def greet(s, carry):
        pl.semaphore_signal(barrier, inc=1, device_id={"kb": lax.rem(me + s, devices)},
                            device_id_type=pl.DeviceIdType.MESH)
        return carry

    lax.fori_loop(1, devices, greet, 0)

    def partner(shift):
        total, bit = 0, 1
        while bit < devices:
            total += bit * lax.rem(me // bit + shift // bit, 2)
            bit *= 2
        return total

    def exchange(src, dst, n):
        pltpu.make_async_copy(src.at[me], dst.at[me], own.at[n]).start()

        def one(i, carry):
            other = partner(i // 4 + devices // 4 * lax.rem(i + 2, 4))
            pltpu.make_async_remote_copy(
                src_ref=src.at[other], dst_ref=dst.at[me], send_sem=send.at[n], recv_sem=recv.at[n],
                device_id={"kb": other}, device_id_type=pl.DeviceIdType.MESH,
            ).start()
            return carry

        lax.fori_loop(0, 2, one, 0)
        lax.fori_loop(3, devices, one, 0)

    def finish(ref, sem):
        part = ref.at[pl.ds(0, devices - 1)]
        pltpu.make_async_copy(part, part, sem).wait()

    loads[3].wait()
    loads[0].wait()
    for p in range(CHUNKS):
        to_time(green, table, tau, p)
        if p == 0:
            pl.semaphore_wait(barrier, devices - 1)
        exchange(tau.at[p], x.at[p], p)
    loads[1].wait()
    lane = lax.broadcasted_iota(jnp.int32, (plane, plane), 1)
    ry, rz = lane // side, lane % side
    target = (mirror_ref[1, 0] + side - ry) % side * side + (mirror_ref[2, 0] + side - rz) % side
    pick = (lax.broadcasted_iota(jnp.int32, (plane, plane), 0) == target).astype(jnp.float32).astype(jnp.bfloat16)
    for i in range(2):
        for part in range(2):
            lanes = slice(part * plane, (part + 1) * plane)
            mirrored[i, :, lanes] = mm(planes[i, :, lanes], pick, ((1,), (0,))).astype(jnp.bfloat16)
    landing = [got, last]
    for p in range(CHUNKS):
        pltpu.make_async_copy(tau.at[p, me], x.at[p, me], own.at[p]).wait()
        finish(x.at[p], recv.at[p])
        bubble(pair_ref, mirror_ref, x, planes.at[0:2], mirrored, planes.at[2:4], sent, y, g, gm, chi, p)
        exchange(sent.at[p], landing[p], CHUNKS + p)
    pltpu.make_async_copy(sent.at[0, me], got.at[me], own.at[CHUNKS]).wait()
    finish(got, recv.at[CHUNKS])
    loads[2].wait()
    comps = got.shape[2]
    block = comps // 2
    for i in range(2):
        chosen = slice(i * block, (i + 1) * block)
        value = to_frequency(got.at[:, :, chosen], back)
        for part in range(2):
            acc[part, chosen] = value[part]
    store = pltpu.make_async_copy(acc, half_hbm, load.at[4])
    store.start()
    for p in range(CHUNKS):
        finish(tau.at[p], send.at[p])
        finish(sent.at[p], send.at[CHUNKS + p])
    store.wait()
    pltpu.make_async_copy(sent.at[1, me], last.at[me], own.at[CHUNKS + 1]).wait()
    finish(last, recv.at[CHUNKS + 1])


def to_frequency(x_ref, b_ref):
    devices, _, block, slots, points = x_ref.shape
    freqs = b_ref.shape[-1] // 2
    rows = []
    for c in range(block):
        parts = [x_ref[:, part, c].reshape(devices * slots, points).T for part in range(2)]
        rows.append(jnp.concatenate(parts, axis=1))
    value = mm3(split(jnp.concatenate(rows, axis=0)), (b_ref[0], b_ref[1]))
    return [value[:, part * freqs:(part + 1) * freqs].reshape(block, points, freqs) for part in range(2)]


def finish_kernel(x_ref, b_ref, half_ref, o_ref):
    value = to_frequency(x_ref, b_ref)
    for part in range(2):
        o_ref[part] = half_ref[part] + value[part]


def local(devices, green, pair_table, mirror_map):
    entries, points, freqs = green.shape[1:]
    side = mirror_map.shape[1]
    plane = side * side
    comps = pair_table.shape[0]
    slots = freqs // (devices * CHUNKS)
    f32, bf16 = jnp.float32, jnp.bfloat16
    times = [owned_times(devices, freqs, p) for p in range(CHUNKS)]
    time_table = np.stack([np.stack(time_tables(t, freqs)) for t in times])
    plane_tables = np.stack(plane_table(side, 1.0) + plane_table(side, -1.0))
    frequency_table = [np.stack(frequency_tables(t, freqs)) for t in times]
    hbm = pl.BlockSpec(memory_space=pl.ANY)
    cells = (side, entries, slots, 2 * plane)
    exchanged = (devices, 2, comps, slots, points)
    result = (2, comps, points, freqs)
    half, last = pl.pallas_call(
        main_kernel,
        out_shape=[jax.ShapeDtypeStruct(result, f32), jax.ShapeDtypeStruct(exchanged, f32)],
        in_specs=[SMEM, SMEM, hbm, hbm, hbm, hbm],
        out_specs=[hbm, hbm],
        scratch_shapes=[
            pltpu.VMEM(green.shape, f32),
            pltpu.VMEM(time_table.shape, bf16),
            pltpu.VMEM(plane_tables.shape, bf16),
            pltpu.VMEM(frequency_table[0].shape, bf16),
            pltpu.VMEM((2, 2 * plane, 2 * plane), bf16),
            pltpu.VMEM((CHUNKS, devices, 2, entries, slots, points), f32),
            pltpu.VMEM((CHUNKS, devices, 2, entries, slots, points), f32),
            pltpu.VMEM(cells, f32),
            pltpu.VMEM(cells, f32),
            pltpu.VMEM(cells, f32),
            pltpu.VMEM((comps,) + (side, slots, 2 * plane), f32),
            pltpu.VMEM((CHUNKS,) + exchanged, f32),
            pltpu.VMEM(exchanged, f32),
            pltpu.VMEM(result, f32),
            pltpu.SemaphoreType.DMA((5,)),
            pltpu.SemaphoreType.DMA((2 * CHUNKS,)),
            pltpu.SemaphoreType.DMA((2 * CHUNKS,)),
            pltpu.SemaphoreType.DMA((2 * CHUNKS,)),
        ],
        compiler_params=pltpu.CompilerParams(
            vmem_limit_bytes=60 * 1024 * 1024, collective_id=0, has_side_effects=True
        ),
        cost_estimate=pl.CostEstimate(flops=18 * 10**9, bytes_accessed=16 * 2**20, transcendentals=0),
    )(pair_table.T, mirror_map, green, time_table, plane_tables, frequency_table[0])
    block = comps // 4
    whole = pl.BlockSpec((2, block, points, freqs), lambda i: (0, i, 0, 0))
    return pl.pallas_call(
        finish_kernel,
        grid=(comps // block,),
        out_shape=jax.ShapeDtypeStruct(result, f32),
        in_specs=[
            pl.BlockSpec((devices, 2, block, slots, points), lambda i: (0, 0, i, 0, 0)),
            pl.BlockSpec(frequency_table[1].shape, lambda i: (0, 0, 0)),
            whole,
        ],
        out_specs=whole,
        compiler_params=pltpu.CompilerParams(vmem_limit_bytes=58 * 1024 * 1024),
        cost_estimate=pl.CostEstimate(flops=6 * 10**9, bytes_accessed=16 * 2**20, transcendentals=0),
    )(last, frequency_table[1], half)


LEVELS = 4
PIECES = 8
STACKS = (1, 3, 4)
PARTS = 4
HALVES = 2
GROUP = 2


def piece_times(members, freqs, piece):
    per = freqs // (2 * PIECES * members)
    first = piece * (freqs // (2 * PIECES)) + np.arange(members)[:, None] * per + np.arange(per)[None, :]
    return np.stack([first, freqs - 1 - first], axis=1).reshape(-1)


def stacked_time_table(times, freqs):
    cos_high, cos_low, sin_high, sin_low = time_tables(times, freqs)
    return np.concatenate([cos_high, sin_high, cos_low, sin_low])


def group_table(members, freqs, pieces):
    rows = []
    for piece in pieces:
        times = piece_times(members, freqs, piece)
        angle = ((np.arange(freqs)[None, :] - freqs // 2) * (2 * times[:, None] + 1)) % (2 * freqs)
        angle = angle * (2 * np.pi / (2 * freqs))
        cos, sin = np.cos(angle) * freqs**-0.5, np.sin(angle) * freqs**-0.5
        rows.append(np.block([[cos, sin], [-sin, cos]]))
    return np.stack(split_np(np.concatenate(rows)))


def mm3s(rows, high, low):
    m = rows.shape[0]
    a, b = split(rows)
    both = mm(jnp.concatenate([a, b], axis=0), high, ((1,), (0,)))
    return both[:m] + both[m:] + mm(a, low, ((1,), (0,)))


def dft16_half(columns, sigma):
    out = [None] * 8
    for k1 in range(4):
        a = [twiddle(columns[n2][k1], n2 * k1, -1) for n2 in range(4)]
        s02, d02 = cadd(a[0], a[2]), csub(a[0], a[2])
        s13, d13 = cadd(a[1], a[3]), csub(a[1], a[3])
        out[k1] = (s02[0] + sigma * s13[0], s02[1] + sigma * s13[1])
        out[4 + k1] = (d02[0] + sigma * d13[1], d02[1] - sigma * d13[0])
    return out


def level_kernel(pair_hbm, mirror_hbm, green_hbm, time_hbm, plane_hbm, back_hbm, half_hbm, last,
                 pair_ref, mirror_ref, green, table, planes, back, mirrored, tau, x, zbuf, t, ts, chi, sent, got, acc,
                 load, own, send, sendz, recv1, recvz, recvc, recv2):
    members = tau.shape[2]
    entries = green.shape[1]
    few, slots, points = tau.shape[4:]
    side = t.shape[0]
    lines = side // LEVELS
    plane = side * side
    comps = sent.shape[1] * sent.shape[4]
    group = sent.shape[4]
    freqs = green.shape[-1]
    kept = got.shape[0]
    me = lax.axis_index("kb")
    z, d = me // members, lax.rem(me, members)
    middle = jnp.logical_or(z == 1, z == 2)
    edge = jnp.logical_not(middle)
    mine = lax.rem(z, 2)
    half = slots // 2

    start = 4 * members * slots * STACKS[0]
    pairs = [(pair_hbm, pair_ref), (mirror_hbm, mirror_ref)]
    small = [pltpu.make_async_copy(src, dst, load.at[8 + i]) for i, (src, dst) in enumerate(pairs)]
    pairs = [(green_hbm.at[:, pl.ds(i * few, few)], green.at[:, pl.ds(i * few, few)]) for i in range(HALVES)]
    pairs += [(time_hbm.at[pl.ds(0, start)], table.at[pl.ds(0, start)]),
              (time_hbm.at[pl.ds(start, table.shape[0] - start)], table.at[pl.ds(start, table.shape[0] - start)]),
              (plane_hbm, planes), (back_hbm, back)]
    loads = [pltpu.make_async_copy(src, dst, load.at[i]) for i, (src, dst) in enumerate(pairs)]
    for i in (0, 2, 1):
        loads[i].start()
    for copy in small:
        copy.start()
    barrier = pltpu.get_barrier_semaphore()

    def greet(other):
        pl.semaphore_signal(barrier, inc=1, device_id={"kb": other}, device_id_type=pl.DeviceIdType.MESH)

    def greet_member(s, carry):
        greet(z * members + lax.rem(d + s, members))
        return carry

    lax.fori_loop(1, members, greet_member, 0)
    for s in range(1, LEVELS):
        greet(lax.rem(z + s, LEVELS) * members + d)

    def partner(shift):
        total, bit = 0, 1
        while bit < members:
            total += bit * lax.rem(d // bit + shift // bit, 2)
            bit *= 2
        return total

    def remote(src, dst, send_sem, recv_sem, other):
        pltpu.make_async_remote_copy(
            src_ref=src, dst_ref=dst, send_sem=send_sem, recv_sem=recv_sem,
            device_id={"kb": other}, device_id_type=pl.DeviceIdType.MESH,
        ).start()

    def exchange(src, dst, own_sem, send_sem, recv_sem):
        pltpu.make_async_copy(src.at[d], dst.at[d], own_sem).start()

        def one(i, carry):
            other = partner(members - i)
            remote(src.at[other], dst.at[d], send_sem, recv_sem, z * members + other)
            return carry

        lax.fori_loop(1, members, one, 0)

    def drain(ref, sem):
        pltpu.make_async_copy(ref, ref, sem).wait()

    def finish(src, dst, own_sem, recv_sem):
        pltpu.make_async_copy(src.at[d], dst.at[d], own_sem).wait()
        drain(dst.at[pl.ds(0, members - 1)], recv_sem)

    def finish_parts(p, dst):
        pltpu.make_async_copy(sent.at[p, :, d], dst.at[:, d], own.at[PIECES + p, 0]).wait()
        drain(dst.at[:, pl.ds(0, members - 1)], recv2.at[p])

    dims = ((1,), (1,))

    def split_entries(i):
        return [split(green[part, i * few:(i + 1) * few].reshape(few * points, freqs)) for part in range(2)]

    def times_of(first, count, i, values):
        times = count * members * slots
        base = 4 * members * slots * first
        stack = table[base:base + 4 * times]
        outs = []
        for value in values:
            a = mm(stack, value[0], dims)
            outs.append(a[:2 * times] + a[2 * times:] + mm(stack[:2 * times], value[1], dims))
        both = (outs[0][:times] + outs[1][times:], outs[1][:times] - outs[0][times:])
        for part in range(2):
            for e in range(few):
                tau[first:first + count, i, :, part, e] = both[part][:, e * points:(e + 1) * points].reshape(
                    count, members, slots, points)

    def exchange_times(p, i):
        exchange(tau.at[p, i], x.at[p, i], own.at[p, i], send.at[0], recv1.at[p, i])

    loads[0].wait()
    loads[2].wait()
    values = []
    for i in range(HALVES):
        if i == 1:
            loads[1].wait()
        values.append(split_entries(i))
        times_of(0, STACKS[0], i, values[i])
        if i == 0:
            pl.semaphore_wait(barrier, members - 1 + LEVELS - 1)
            for n in range(3, len(loads)):
                loads[n].start()
        exchange_times(0, i)
    loads[4].wait()
    for copy in small:
        copy.wait()
    lane = lax.broadcasted_iota(jnp.int32, (plane, plane), 1)
    ry, rz = lane // side, lane % side
    target = (mirror_ref[1, 0] + side - ry) % side * side + (mirror_ref[2, 0] + side - rz) % side
    pick = (lax.broadcasted_iota(jnp.int32, (plane, plane), 0) == target).astype(jnp.float32).astype(jnp.bfloat16)
    for i in range(2):
        for part in range(2):
            lanes = slice(part * plane, (part + 1) * plane)
            mirrored[i, :, lanes] = mm(planes[i, :, lanes], pick, ((1,), (0,))).astype(jnp.bfloat16)
            mirrored[2 + i, lanes, :] = mm(pick, planes[2 + i, lanes, :], ((1,), (0,))).astype(jnp.bfloat16)

    def both_ways(rows, base):
        straight = mm3s(rows, planes[base], planes[base + 1])
        turned = mm3s(rows, mirrored[base], mirrored[base + 1])
        slot = lax.broadcasted_iota(jnp.int32, straight.shape, 0) % slots
        return jnp.where(slot < half, straight, turned)

    def forward(p, first, count, follow=True):
        for i in range(first, first + count):
            finish(tau.at[p, i], x.at[p, i], own.at[p, i], recv1.at[p, i])

            if follow:
                @pl.when(p + 1 < PIECES)
                def _():
                    exchange_times(p + 1, i)

        v = x[p, first:first + count].reshape(count, lines, 2, 2, few, slots, points)
        rows = jnp.concatenate([v[:, :, h, part].reshape(count * lines * few * slots, points)
                                for part in range(2) for h in range(2)], axis=1)
        out = both_ways(rows, 0)
        for h in range(2):
            for part in range(2):
                lanes = slice(part * plane + h * points, part * plane + (h + 1) * points)
                zbuf[p, h, first:first + count, z, part] = out[:, lanes].reshape(count, lines, few, slots, points)

    def send_lines(p, h, first, count):
        for i in range(first, first + count):
            for level in (1, 2):
                @pl.when(z != level)
                def _():
                    remote(zbuf.at[p, h, i, z], zbuf.at[p, h, i, z], sendz.at[p, h], recvz.at[p, h],
                           level * members + d)

    def middle_work(p, h):
        sigma = jnp.where(z == 1, 1.0, -1.0).astype(jnp.float32)

        def forth(e, carry):
            i, f = e // few, lax.rem(e, few)
            cells = [(zbuf[p, h, i, k // lines, 0, k % lines, f], zbuf[p, h, i, k // lines, 1, k % lines, f])
                     for k in range(side)]
            for r, pair in enumerate(dft16(cells, 1)):
                for part in range(2):
                    v = pair[part]
                    t[r, e, part] = v
                    ts[r, e, part] = jnp.concatenate([v[half:], v[:half]], axis=0)
            return carry

        lax.fori_loop(0, entries, forth, 0)

        def one(c, carry):
            left, right = pair_ref[0, c], pair_ref[1, c]
            columns = []
            for n2 in range(4):
                cells = []
                for n1 in range(4):
                    r = 4 * n1 + n2
                    a, b = t[r, left], ts[mirror_ref[0, r], right]
                    cells.append((a[0] * b[0] - a[1] * b[1], a[0] * b[1] + a[1] * b[0]))
                columns.append(dft4(cells, -1))
            for i, pair in enumerate(dft16_half(columns, sigma)):
                for part in range(2):
                    chi[i // lines, p, h, c, part, i % lines] = pair[part]
            remote(chi.at[1 - mine, p, h, c], chi.at[1 - mine, p, h, c], send.at[1], recvc.at[p, c // group],
                   jnp.where(z == 1, 0, 3) * members + d)
            return carry

        lax.fori_loop(0, comps, one, 0)

    def backward(p, first, count):
        @pl.when(edge)
        def _():
            for n in range(first, first + count):
                drain(chi.at[mine, p, :, pl.ds(n * group, group)], recvc.at[p, n])

        v = chi[mine, p, :, first * group:(first + count) * group]
        rows = jnp.concatenate([v[h, :, part].reshape(count * group * lines * slots, points)
                                for part in range(2) for h in range(2)], axis=1)
        out = both_ways(rows, 2).reshape(count, group, lines, slots, 2 * plane)
        for q in range(lines):
            for h in range(2):
                for part in range(2):
                    lanes = slice(part * plane + h * points, part * plane + (h + 1) * points)
                    sent[p, first:first + count, 2 * q + h, part] = out[:, :, q, :, lanes]

        for n in range(first, first + count):
            @pl.when(p < kept)
            def _():
                exchange(sent.at[p, n], got.at[p, n], own.at[PIECES + p, 0], send.at[2], recv2.at[p])

            @pl.when(p >= kept)
            def _():
                exchange(sent.at[p, n], last.at[p - kept, n], own.at[PIECES + p, 0], send.at[2], recv2.at[p])

    span = 2 * GROUP * members * slots

    def frequency(pieces, first, depth):
        block = 2 * group
        high, low = back[0, pl.ds(first, depth)], back[1, pl.ds(first, depth)]
        for i in range(comps // block):
            chosen = slice(i * block, (i + 1) * block)
            rows = frequency_rows([[got.at[p, c // group, :, :, c % group] for p in pieces]
                                   for c in range(i * block, (i + 1) * block)])
            value = mm3s(rows, high, low)
            for part in range(2):
                acc[part, chosen] += value[:, part * freqs:(part + 1) * freqs].reshape(block, points, freqs)

    for i in range(HALVES):
        forward(0, i, 1, False)
        send_lines(0, 0, i, 1)
    send_lines(0, 1, 0, HALVES)
    loads[3].wait()
    for i in range(HALVES):
        times_of(STACKS[0], STACKS[1], i, values[i])
        exchange_times(1, i)
    for i in range(HALVES):
        times_of(STACKS[0] + STACKS[1], STACKS[2], i, values[i])
    acc[...] = jnp.zeros(acc.shape, jnp.float32)
    forward(1, 0, HALVES)
    loads[5].wait()

    def step(p, carry):
        for h in range(2):
            @pl.when(middle)
            def _():
                drain(zbuf.at[p, h, :, pl.ds(0, LEVELS - 1)], recvz.at[p, h])

            @pl.when(edge)
            def _():
                drain(zbuf.at[p, h, :, pl.ds(0, 2)], sendz.at[p, h])

            @pl.when(p + 1 < PIECES)
            def _():
                send_lines(p + 1, h, 0, HALVES)

            @pl.when(middle)
            def _():
                middle_work(p, h)

            @pl.when(middle if h == 1 else jnp.logical_and(edge, p > 0))
            def _():
                backward(p if h == 1 else p - 1, 0, PARTS)

        @pl.when(p + 2 < PIECES)
        def _():
            forward(p + 2, 0, HALVES)

        @pl.when(jnp.logical_and(lax.rem(p, GROUP) == GROUP - 1, p >= 2 * GROUP - 1))
        def _():
            m = p // GROUP - 1

            def arrived(q, carry):
                finish_parts(q, got.at[q])
                return carry

            lax.fori_loop(m * GROUP, (m + 1) * GROUP, arrived, 0)
            frequency([m * GROUP + g for g in range(GROUP)], m * span, span)

        return carry

    lax.fori_loop(0, PIECES, step, 0)
    end = PIECES - 1

    @pl.when(edge)
    def _():
        backward(end, 0, 2)

    @pl.when(edge)
    def _():
        for n in range(2, PARTS):
            backward(end, n, 1)

    finish_parts(end - 1, got.at[end - 1])
    frequency([end - 1], back.shape[1] - span // GROUP, span // GROUP)
    store = pltpu.make_async_copy(acc, half_hbm, load.at[7])
    store.start()
    drain(tau.at[:, :, pl.ds(0, members - 1)], send.at[0])

    @pl.when(middle)
    def _():
        def gone(p, carry):
            for h in range(2):
                drain(zbuf.at[p, h, :, 0], sendz.at[p, h])
            return carry

        lax.fori_loop(0, PIECES, gone, 0)
        drain(chi.at[0], send.at[1])

    finish_parts(end, last.at[end - kept])
    drain(sent.at[:, :, pl.ds(0, members - 1)], send.at[2])
    store.wait()


def frequency_rows(blocks):
    rows = []
    for pieces in blocks:
        parts = []
        for ref in pieces:
            for part in range(2):
                v = ref[:, part]
                parts.append(v.reshape(v.shape[0] * v.shape[1], v.shape[2]))
        rows.append(jnp.concatenate(parts, axis=0).T)
    return jnp.concatenate(rows, axis=0)


def level_finish(x_hbm, b_hbm, half_hbm, o_hbm, x, b_ref, total, sem):
    points, freqs = total.shape[2:]
    group = x.shape[3]
    spans = [pl.ds(n * group, group) for n in range(PARTS)]
    ahead = [pltpu.make_async_copy(x_hbm.at[0, n], x.at[n], sem.at[0, n]) for n in range(PARTS)]
    halves = [pltpu.make_async_copy(half_hbm.at[:, span], total.at[:, span], sem.at[1, n])
              for n, span in enumerate(spans)]
    stores = [pltpu.make_async_copy(total.at[:, span], o_hbm.at[:, span], sem.at[2, n])
              for n, span in enumerate(spans)]
    tables = pltpu.make_async_copy(b_hbm, b_ref, sem.at[3, 0])
    for copy in [tables] + ahead + halves:
        copy.start()
    tables.wait()
    for n in range(PARTS):
        chosen = slice(n * group, (n + 1) * group)
        ahead[n].wait()
        value = mm3s(frequency_rows([[x.at[n, :, :, c]] for c in range(group)]), b_ref[0], b_ref[1])
        halves[n].wait()
        for part in range(2):
            total[part, chosen] += value[:, part * freqs:(part + 1) * freqs].reshape(group, points, freqs)
        stores[n].start()
    for store in stores:
        store.wait()


def level_local(devices, green, pair_table, mirror_map):
    entries, points, freqs = green.shape[1:]
    side = mirror_map.shape[1]
    plane = side * side
    comps = pair_table.shape[0]
    members = devices // LEVELS
    slots = freqs // (members * PIECES)
    lines = side // LEVELS
    few = entries // HALVES
    f32, bf16 = jnp.float32, jnp.bfloat16
    times = [piece_times(members, freqs, p) for p in range(PIECES)]
    edges = np.cumsum((0,) + STACKS)
    time_table = np.concatenate([stacked_time_table(np.concatenate(times[a:b]), freqs)
                                 for a, b in zip(edges[:-1], edges[1:])])
    plane_tables = np.stack(plane_table(side, 1.0) + plane_table(side, -1.0))
    groups = PIECES // GROUP
    early = np.concatenate([group_table(members, freqs, range(g * GROUP, (g + 1) * GROUP)) for g in range(groups - 1)]
                           + [group_table(members, freqs, [PIECES - 2])], axis=1)
    final = group_table(members, freqs, [PIECES - 1])
    kept = PIECES - 1
    hbm = pl.BlockSpec(memory_space=pl.ANY)
    exchanged = (PARTS, members, 2, comps // PARTS, slots, points)
    result = (2, comps, points, freqs)
    cells = (side, entries, 2, slots, points)
    half, last = pl.pallas_call(
        level_kernel,
        out_shape=[jax.ShapeDtypeStruct(result, f32), jax.ShapeDtypeStruct((1,) + exchanged, f32)],
        in_specs=[hbm] * 6,
        out_specs=[hbm, hbm],
        scratch_shapes=[
            pltpu.SMEM((2, comps), jnp.int32),
            pltpu.SMEM(mirror_map.shape, jnp.int32),
            pltpu.VMEM(green.shape, f32),
            pltpu.VMEM(time_table.shape, bf16),
            pltpu.VMEM(plane_tables.shape, bf16),
            pltpu.VMEM(early.shape, bf16),
            pltpu.VMEM(plane_tables.shape, bf16),
            pltpu.VMEM((PIECES, HALVES, members, 2, few, slots, points), f32),
            pltpu.VMEM((PIECES, HALVES, members, 2, few, slots, points), f32),
            pltpu.VMEM((PIECES, 2, HALVES, LEVELS, 2, lines, few, slots, points), f32),
            pltpu.VMEM(cells, f32),
            pltpu.VMEM(cells, f32),
            pltpu.VMEM((2, PIECES, 2, comps, 2, lines, slots, points), f32),
            pltpu.VMEM((PIECES,) + exchanged, f32),
            pltpu.VMEM((kept,) + exchanged, f32),
            pltpu.VMEM(result, f32),
            pltpu.SemaphoreType.DMA((10,)),
            pltpu.SemaphoreType.DMA((2 * PIECES, HALVES)),
            pltpu.SemaphoreType.DMA((3,)),
            pltpu.SemaphoreType.DMA((PIECES, 2)),
            pltpu.SemaphoreType.DMA((PIECES, HALVES)),
            pltpu.SemaphoreType.DMA((PIECES, 2)),
            pltpu.SemaphoreType.DMA((PIECES, PARTS)),
            pltpu.SemaphoreType.DMA((PIECES,)),
        ],
        compiler_params=pltpu.CompilerParams(
            vmem_limit_bytes=60 * 1024 * 1024, collective_id=0, has_side_effects=True
        ),
        cost_estimate=pl.CostEstimate(flops=18 * 10**9, bytes_accessed=16 * 2**20, transcendentals=0),
    )(pair_table.T, mirror_map, green, time_table, plane_tables, early)
    return pl.pallas_call(
        level_finish,
        out_shape=jax.ShapeDtypeStruct(result, f32),
        in_specs=[hbm, hbm, hbm],
        out_specs=hbm,
        scratch_shapes=[
            pltpu.VMEM(exchanged, f32),
            pltpu.VMEM(final.shape, bf16),
            pltpu.VMEM(result, f32),
            pltpu.SemaphoreType.DMA((4, PARTS)),
        ],
        compiler_params=pltpu.CompilerParams(vmem_limit_bytes=60 * 1024 * 1024),
        cost_estimate=pl.CostEstimate(flops=6 * 10**9, bytes_accessed=16 * 2**20, transcendentals=0),
    )(last, final, half)


def fits_levels(devices):
    return devices == 32


def solution(mesh):
    placed = (P("set", None, "kb", None), P(), P("set", None))
    devices = mesh.shape["kb"]
    return jax.shard_map(
        functools.partial(level_local if fits_levels(devices) else local, devices),
        mesh=mesh,
        in_specs=placed,
        out_specs=P("set", None, "kb", None),
        check_vma=False,
    )
```

```python
import functools

import numpy as np
import ml_dtypes
import jax
import jax.numpy as jnp
from jax import lax
from jax.experimental import pallas as pl
from jax.experimental.pallas import tpu as pltpu
from jax.sharding import PartitionSpec as P

CHUNKS = 2
SMEM = pl.BlockSpec(memory_space=pltpu.SMEM)


def split_np(table):
    table = table.astype(np.float32)
    high = table.astype(ml_dtypes.bfloat16)
    low = (table - high.astype(np.float32)).astype(ml_dtypes.bfloat16)
    return high, low


def split(x):
    high = x.astype(jnp.bfloat16)
    return high, (x - high.astype(jnp.float32)).astype(jnp.bfloat16)


def mm(a, b, dims):
    return lax.dot_general(a, b, (dims, ((), ())), preferred_element_type=jnp.float32)


def mm3(a, b, dims=((1,), (0,))):
    return mm(a[0], b[0], dims) + mm(a[1], b[0], dims) + mm(a[0], b[1], dims)


def owned_times(devices, freqs, chunk):
    per = freqs // (2 * CHUNKS * devices)
    first = chunk * (freqs // (2 * CHUNKS)) + np.arange(devices)[:, None] * per + np.arange(per)[None, :]
    return np.stack([first, freqs - 1 - first], axis=1).reshape(-1)


def time_tables(times, freqs):
    angle = ((2 * np.arange(freqs)[None, :] - freqs + 1) * (2 * times[:, None] + 1)) % (4 * freqs)
    angle = angle * (2 * np.pi / (4 * freqs))
    scale = freqs**-0.5
    return split_np(scale * np.cos(angle)) + split_np(scale * np.sin(angle))


def frequency_tables(times, freqs):
    angle = ((np.arange(freqs)[None, :] - freqs // 2) * (2 * times[:, None] + 1)) % (2 * freqs)
    angle = angle * (2 * np.pi / (2 * freqs))
    cos, sin = np.cos(angle) * freqs**-0.5, np.sin(angle) * freqs**-0.5
    return split_np(np.block([[cos, sin], [-sin, cos]]))


def plane_table(side, sign):
    index = np.arange(side * side)
    upper, lower = index // side, index % side
    angle = (upper[:, None] * upper[None, :] + lower[:, None] * lower[None, :]) % side * (2 * np.pi / side)
    scale = (side**3) ** -0.5
    cos, sin = scale * np.cos(angle), sign * scale * np.sin(angle)
    return split_np(np.block([[cos, sin], [-sin, cos]]))


def cadd(a, b):
    return a[0] + b[0], a[1] + b[1]


def csub(a, b):
    return a[0] - b[0], a[1] - b[1]


def dft4(a, sign):
    s02, d02 = cadd(a[0], a[2]), csub(a[0], a[2])
    s13, d13 = cadd(a[1], a[3]), csub(a[1], a[3])
    turned = (-d13[1], d13[0]) if sign > 0 else (d13[1], -d13[0])
    return [cadd(s02, s13), cadd(d02, turned), csub(s02, s13), csub(d02, turned)]


def twiddle(a, power, sign):
    if power == 0:
        return a
    if power == 4:
        return (-a[1], a[0]) if sign > 0 else (a[1], -a[0])
    if power in (2, 6):
        r = np.float32(np.sqrt(0.5))
        plus, minus = (a[0] + a[1]) * r, (a[0] - a[1]) * r
        if power == 2:
            return (minus, plus) if sign > 0 else (plus, -minus)
        return (-plus, minus) if sign > 0 else (-minus, -plus)
    c = np.float32(np.cos(2 * np.pi * power / 16))
    s = np.float32(sign * np.sin(2 * np.pi * power / 16))
    return a[0] * c - a[1] * s, a[0] * s + a[1] * c


def dft16(x, sign):
    columns = [dft4([x[4 * n1 + n2] for n1 in range(4)], sign) for n2 in range(4)]
    out = [None] * 16
    for k1 in range(4):
        row = dft4([twiddle(columns[n2][k1], n2 * k1, sign) for n2 in range(4)], sign)
        for k2 in range(4):
            out[k1 + 4 * k2] = row[k2]
    return out


def to_time(g_ref, table, o_ref, p):
    devices, _, entries, slots, points = o_ref.shape[1:]
    freqs = g_ref.shape[-1]
    cos, sin = (table[p, 0], table[p, 1]), (table[p, 2], table[p, 3])
    dims = ((1,), (1,))
    re = split(g_ref[0].reshape(entries * points, freqs))
    im = split(g_ref[1].reshape(entries * points, freqs))
    tau = (mm3(cos, re, dims) + mm3(sin, im, dims), mm3(cos, im, dims) - mm3(sin, re, dims))
    for part in range(2):
        for e in range(entries):
            o_ref[p, :, part, e] = tau[part][:, e * points:(e + 1) * points].reshape(devices, slots, points)


def bubble(pair_ref, mirror_ref, x_ref, ahead, mirrored, inverse, o_ref, y, g, gm, chi, p):
    devices, _, entries, slots, points = x_ref.shape[1:]
    side = y.shape[0]
    plane = side * side
    halves = devices // side
    comps = o_ref.shape[3]

    def forth(e, carry):
        for h in range(halves):
            cells = [(x_ref[p, k * halves + h, 0, e], x_ref[p, k * halves + h, 1, e]) for k in range(side)]
            for k, (re, im) in enumerate(dft16(cells, 1)):
                y[k, e, :, h * points:(h + 1) * points] = re
                y[k, e, :, plane + h * points:plane + (h + 1) * points] = im
        return carry

    lax.fori_loop(0, entries, forth, 0)
    rows = split(y[...].reshape(side * entries * slots, 2 * plane))
    g[...] = mm3(rows, (ahead[0], ahead[1])).reshape(g.shape)
    other = mm3(rows, (mirrored[0], mirrored[1])).reshape(side * entries, slots, 2 * plane)
    other = jnp.concatenate([other[:, slots // 2:], other[:, :slots // 2]], axis=1)
    gm[...] = other.reshape(gm.shape)

    def one(c, carry):
        left, right = pair_ref[0, c], pair_ref[1, c]
        for r in range(side):
            a = g[r, left]
            b = gm[mirror_ref[0, r], right]
            ar, ai, br, bi = a[:, :plane], a[:, plane:], b[:, :plane], b[:, plane:]
            chi[c, r, :, :plane] = ar * br - ai * bi
            chi[c, r, :, plane:] = ar * bi + ai * br
        return carry

    lax.fori_loop(0, comps, one, 0)
    rows = split(chi[...].reshape(comps * side * slots, 2 * plane))
    chi[...] = mm3(rows, (inverse[0], inverse[1])).reshape(chi.shape)

    def back(c, carry):
        for h in range(halves):
            lanes = slice(h * points, (h + 1) * points)
            high = slice(plane + h * points, plane + (h + 1) * points)
            cells = [(chi[c, r, :, lanes], chi[c, r, :, high]) for r in range(side)]
            for q, (re, im) in enumerate(dft16(cells, -1)):
                o_ref[p, q * halves + h, 0, c] = re
                o_ref[p, q * halves + h, 1, c] = im
        return carry

    lax.fori_loop(0, comps, back, 0)


def main_kernel(pair_ref, mirror_ref, green_hbm, time_hbm, plane_hbm, back_hbm, half_hbm, last,
                green, table, planes, back, mirrored, tau, x, y, g, gm, chi, sent, got, acc,
                load, own, send, recv):
    devices = tau.shape[1]
    side = y.shape[0]
    plane = side * side
    me = lax.axis_index("kb")
    loads = [pltpu.make_async_copy(src, dst, load.at[i])
             for i, (src, dst) in enumerate([(time_hbm, table), (plane_hbm, planes), (back_hbm, back),
                                       (green_hbm, green)])]
    for i in (3, 0, 1, 2):
        loads[i].start()
    barrier = pltpu.get_barrier_semaphore()

    def greet(s, carry):
        pl.semaphore_signal(barrier, inc=1, device_id={"kb": lax.rem(me + s, devices)},
                            device_id_type=pl.DeviceIdType.MESH)
        return carry

    lax.fori_loop(1, devices, greet, 0)

    def partner(shift):
        total, bit = 0, 1
        while bit < devices:
            total += bit * lax.rem(me // bit + shift // bit, 2)
            bit *= 2
        return total

    def exchange(src, dst, n):
        pltpu.make_async_copy(src.at[me], dst.at[me], own.at[n]).start()

        def one(i, carry):
            other = partner(i // 4 + devices // 4 * lax.rem(i + 2, 4))
            pltpu.make_async_remote_copy(
                src_ref=src.at[other], dst_ref=dst.at[me], send_sem=send.at[n], recv_sem=recv.at[n],
                device_id={"kb": other}, device_id_type=pl.DeviceIdType.MESH,
            ).start()
            return carry

        lax.fori_loop(0, 2, one, 0)
        lax.fori_loop(3, devices, one, 0)

    def finish(ref, sem):
        part = ref.at[pl.ds(0, devices - 1)]
        pltpu.make_async_copy(part, part, sem).wait()

    loads[3].wait()
    loads[0].wait()
    for p in range(CHUNKS):
        to_time(green, table, tau, p)
        if p == 0:
            pl.semaphore_wait(barrier, devices - 1)
        exchange(tau.at[p], x.at[p], p)
    loads[1].wait()
    lane = lax.broadcasted_iota(jnp.int32, (plane, plane), 1)
    ry, rz = lane // side, lane % side
    target = (mirror_ref[1, 0] + side - ry) % side * side + (mirror_ref[2, 0] + side - rz) % side
    pick = (lax.broadcasted_iota(jnp.int32, (plane, plane), 0) == target).astype(jnp.float32).astype(jnp.bfloat16)
    for i in range(2):
        for part in range(2):
            lanes = slice(part * plane, (part + 1) * plane)
            mirrored[i, :, lanes] = mm(planes[i, :, lanes], pick, ((1,), (0,))).astype(jnp.bfloat16)
    landing = [got, last]
    for p in range(CHUNKS):
        pltpu.make_async_copy(tau.at[p, me], x.at[p, me], own.at[p]).wait()
        finish(x.at[p], recv.at[p])
        bubble(pair_ref, mirror_ref, x, planes.at[0:2], mirrored, planes.at[2:4], sent, y, g, gm, chi, p)
        exchange(sent.at[p], landing[p], CHUNKS + p)
    pltpu.make_async_copy(sent.at[0, me], got.at[me], own.at[CHUNKS]).wait()
    finish(got, recv.at[CHUNKS])
    loads[2].wait()
    comps = got.shape[2]
    block = comps // 2
    for i in range(2):
        chosen = slice(i * block, (i + 1) * block)
        value = to_frequency(got.at[:, :, chosen], back)
        for part in range(2):
            acc[part, chosen] = value[part]
    store = pltpu.make_async_copy(acc, half_hbm, load.at[4])
    store.start()
    for p in range(CHUNKS):
        finish(tau.at[p], send.at[p])
        finish(sent.at[p], send.at[CHUNKS + p])
    store.wait()
    pltpu.make_async_copy(sent.at[1, me], last.at[me], own.at[CHUNKS + 1]).wait()
    finish(last, recv.at[CHUNKS + 1])


def to_frequency(x_ref, b_ref):
    devices, _, block, slots, points = x_ref.shape
    freqs = b_ref.shape[-1] // 2
    rows = []
    for c in range(block):
        parts = [x_ref[:, part, c].reshape(devices * slots, points).T for part in range(2)]
        rows.append(jnp.concatenate(parts, axis=1))
    value = mm3(split(jnp.concatenate(rows, axis=0)), (b_ref[0], b_ref[1]))
    return [value[:, part * freqs:(part + 1) * freqs].reshape(block, points, freqs) for part in range(2)]


def finish_kernel(x_ref, b_ref, half_ref, o_ref):
    value = to_frequency(x_ref, b_ref)
    for part in range(2):
        o_ref[part] = half_ref[part] + value[part]


def local(devices, green, pair_table, mirror_map):
    entries, points, freqs = green.shape[1:]
    side = mirror_map.shape[1]
    plane = side * side
    comps = pair_table.shape[0]
    slots = freqs // (devices * CHUNKS)
    f32, bf16 = jnp.float32, jnp.bfloat16
    times = [owned_times(devices, freqs, p) for p in range(CHUNKS)]
    time_table = np.stack([np.stack(time_tables(t, freqs)) for t in times])
    plane_tables = np.stack(plane_table(side, 1.0) + plane_table(side, -1.0))
    frequency_table = [np.stack(frequency_tables(t, freqs)) for t in times]
    hbm = pl.BlockSpec(memory_space=pl.ANY)
    cells = (side, entries, slots, 2 * plane)
    exchanged = (devices, 2, comps, slots, points)
    result = (2, comps, points, freqs)
    half, last = pl.pallas_call(
        main_kernel,
        out_shape=[jax.ShapeDtypeStruct(result, f32), jax.ShapeDtypeStruct(exchanged, f32)],
        in_specs=[SMEM, SMEM, hbm, hbm, hbm, hbm],
        out_specs=[hbm, hbm],
        scratch_shapes=[
            pltpu.VMEM(green.shape, f32),
            pltpu.VMEM(time_table.shape, bf16),
            pltpu.VMEM(plane_tables.shape, bf16),
            pltpu.VMEM(frequency_table[0].shape, bf16),
            pltpu.VMEM((2, 2 * plane, 2 * plane), bf16),
            pltpu.VMEM((CHUNKS, devices, 2, entries, slots, points), f32),
            pltpu.VMEM((CHUNKS, devices, 2, entries, slots, points), f32),
            pltpu.VMEM(cells, f32),
            pltpu.VMEM(cells, f32),
            pltpu.VMEM(cells, f32),
            pltpu.VMEM((comps,) + (side, slots, 2 * plane), f32),
            pltpu.VMEM((CHUNKS,) + exchanged, f32),
            pltpu.VMEM(exchanged, f32),
            pltpu.VMEM(result, f32),
            pltpu.SemaphoreType.DMA((5,)),
            pltpu.SemaphoreType.DMA((2 * CHUNKS,)),
            pltpu.SemaphoreType.DMA((2 * CHUNKS,)),
            pltpu.SemaphoreType.DMA((2 * CHUNKS,)),
        ],
        compiler_params=pltpu.CompilerParams(
            vmem_limit_bytes=60 * 1024 * 1024, collective_id=0, has_side_effects=True
        ),
        cost_estimate=pl.CostEstimate(flops=18 * 10**9, bytes_accessed=16 * 2**20, transcendentals=0),
    )(pair_table.T, mirror_map, green, time_table, plane_tables, frequency_table[0])
    block = comps // 4
    whole = pl.BlockSpec((2, block, points, freqs), lambda i: (0, i, 0, 0))
    return pl.pallas_call(
        finish_kernel,
        grid=(comps // block,),
        out_shape=jax.ShapeDtypeStruct(result, f32),
        in_specs=[
            pl.BlockSpec((devices, 2, block, slots, points), lambda i: (0, 0, i, 0, 0)),
            pl.BlockSpec(frequency_table[1].shape, lambda i: (0, 0, 0)),
            whole,
        ],
        out_specs=whole,
        compiler_params=pltpu.CompilerParams(vmem_limit_bytes=58 * 1024 * 1024),
        cost_estimate=pl.CostEstimate(flops=6 * 10**9, bytes_accessed=16 * 2**20, transcendentals=0),
    )(last, frequency_table[1], half)


LEVELS = 4
PIECES = 8
STACKS = (1, 3, 4)
PARTS = 4
HALVES = 2
GROUP = 2


def piece_times(members, freqs, piece):
    per = freqs // (2 * PIECES * members)
    first = piece * (freqs // (2 * PIECES)) + np.arange(members)[:, None] * per + np.arange(per)[None, :]
    return np.stack([first, freqs - 1 - first], axis=1).reshape(-1)


def stacked_time_table(times, freqs):
    cos_high, cos_low, sin_high, sin_low = time_tables(times, freqs)
    return np.concatenate([cos_high, sin_high, cos_low, sin_low])


def group_table(members, freqs, pieces):
    rows = []
    for piece in pieces:
        times = piece_times(members, freqs, piece)
        angle = ((np.arange(freqs)[None, :] - freqs // 2) * (2 * times[:, None] + 1)) % (2 * freqs)
        angle = angle * (2 * np.pi / (2 * freqs))
        cos, sin = np.cos(angle) * freqs**-0.5, np.sin(angle) * freqs**-0.5
        rows.append(np.block([[cos, sin], [-sin, cos]]))
    return np.stack(split_np(np.concatenate(rows)))


def mm3s(rows, high, low):
    m = rows.shape[0]
    a, b = split(rows)
    both = mm(jnp.concatenate([a, b], axis=0), high, ((1,), (0,)))
    return both[:m] + both[m:] + mm(a, low, ((1,), (0,)))


def dft16_half(columns, sigma):
    out = [None] * 8
    for k1 in range(4):
        a = [twiddle(columns[n2][k1], n2 * k1, -1) for n2 in range(4)]
        s02, d02 = cadd(a[0], a[2]), csub(a[0], a[2])
        s13, d13 = cadd(a[1], a[3]), csub(a[1], a[3])
        out[k1] = (s02[0] + sigma * s13[0], s02[1] + sigma * s13[1])
        out[4 + k1] = (d02[0] + sigma * d13[1], d02[1] - sigma * d13[0])
    return out


def level_kernel(pair_hbm, mirror_hbm, green_hbm, time_hbm, plane_hbm, back_hbm, half_hbm, last,
                 pair_ref, mirror_ref, green, table, planes, back, mirrored, tau, x, zbuf, t, ts, chi, sent, got, acc,
                 load, own, send, sendz, recv1, recvz, recvc, recv2):
    members = tau.shape[2]
    entries = green.shape[1]
    few, slots, points = tau.shape[4:]
    side = t.shape[0]
    lines = side // LEVELS
    plane = side * side
    comps = sent.shape[1] * sent.shape[4]
    group = sent.shape[4]
    freqs = green.shape[-1]
    kept = got.shape[0]
    me = lax.axis_index("kb")
    z, d = me // members, lax.rem(me, members)
    middle = jnp.logical_or(z == 1, z == 2)
    edge = jnp.logical_not(middle)
    mine = lax.rem(z, 2)
    half = slots // 2

    start = 4 * members * slots * STACKS[0]
    pairs = [(pair_hbm, pair_ref), (mirror_hbm, mirror_ref)]
    small = [pltpu.make_async_copy(src, dst, load.at[8 + i]) for i, (src, dst) in enumerate(pairs)]
    pairs = [(green_hbm.at[:, pl.ds(i * few, few)], green.at[:, pl.ds(i * few, few)]) for i in range(HALVES)]
    pairs += [(time_hbm.at[pl.ds(0, start)], table.at[pl.ds(0, start)]),
              (time_hbm.at[pl.ds(start, table.shape[0] - start)], table.at[pl.ds(start, table.shape[0] - start)]),
              (plane_hbm, planes), (back_hbm, back)]
    loads = [pltpu.make_async_copy(src, dst, load.at[i]) for i, (src, dst) in enumerate(pairs)]
    for i in (0, 2, 1):
        loads[i].start()
    for copy in small:
        copy.start()
    barrier = pltpu.get_barrier_semaphore()

    def greet(other):
        pl.semaphore_signal(barrier, inc=1, device_id={"kb": other}, device_id_type=pl.DeviceIdType.MESH)

    def greet_member(s, carry):
        greet(z * members + lax.rem(d + s, members))
        return carry

    lax.fori_loop(1, members, greet_member, 0)
    for s in range(1, LEVELS):
        greet(lax.rem(z + s, LEVELS) * members + d)

    def partner(shift):
        total, bit = 0, 1
        while bit < members:
            total += bit * lax.rem(d // bit + shift // bit, 2)
            bit *= 2
        return total

    def remote(src, dst, send_sem, recv_sem, other):
        pltpu.make_async_remote_copy(
            src_ref=src, dst_ref=dst, send_sem=send_sem, recv_sem=recv_sem,
            device_id={"kb": other}, device_id_type=pl.DeviceIdType.MESH,
        ).start()

    def exchange(src, dst, own_sem, send_sem, recv_sem):
        pltpu.make_async_copy(src.at[d], dst.at[d], own_sem).start()

        def one(i, carry):
            other = partner(members - i)
            remote(src.at[other], dst.at[d], send_sem, recv_sem, z * members + other)
            return carry

        for i in range(1, members):
            one(i, 0)

    def drain(ref, sem):
        pltpu.make_async_copy(ref, ref, sem).wait()

    def finish(src, dst, own_sem, recv_sem):
        pltpu.make_async_copy(src.at[d], dst.at[d], own_sem).wait()
        drain(dst.at[pl.ds(0, members - 1)], recv_sem)

    def finish_parts(p, dst):
        pltpu.make_async_copy(sent.at[p, :, d], dst.at[:, d], own.at[PIECES + p, 0]).wait()
        drain(dst.at[:, pl.ds(0, members - 1)], recv2.at[p])

    dims = ((1,), (1,))

    def split_entries(i):
        return [split(green[part, i * few:(i + 1) * few].reshape(few * points, freqs)) for part in range(2)]

    def times_of(first, count, i, values):
        times = count * members * slots
        base = 4 * members * slots * first
        stack = table[base:base + 4 * times]
        outs = []
        for value in values:
            a = mm(stack, value[0], dims)
            outs.append(a[:2 * times] + a[2 * times:] + mm(stack[:2 * times], value[1], dims))
        both = (outs[0][:times] + outs[1][times:], outs[1][:times] - outs[0][times:])
        for part in range(2):
            for e in range(few):
                tau[first:first + count, i, :, part, e] = both[part][:, e * points:(e + 1) * points].reshape(
                    count, members, slots, points)

    def exchange_times(p, i):
        exchange(tau.at[p, i], x.at[p, i], own.at[p, i], send.at[0], recv1.at[p, i])

    loads[0].wait()
    loads[2].wait()
    values = []
    for i in range(HALVES):
        if i == 1:
            loads[1].wait()
        values.append(split_entries(i))
        times_of(0, STACKS[0], i, values[i])
        if i == 0:
            pl.semaphore_wait(barrier, members - 1 + LEVELS - 1)
            for n in range(3, len(loads)):
                loads[n].start()
        exchange_times(0, i)
    loads[4].wait()
    for copy in small:
        copy.wait()
    lane = lax.broadcasted_iota(jnp.int32, (plane, plane), 1)
    ry, rz = lane // side, lane % side
    target = (mirror_ref[1, 0] + side - ry) % side * side + (mirror_ref[2, 0] + side - rz) % side
    pick = (lax.broadcasted_iota(jnp.int32, (plane, plane), 0) == target).astype(jnp.float32).astype(jnp.bfloat16)
    for i in range(2):
        for part in range(2):
            lanes = slice(part * plane, (part + 1) * plane)
            mirrored[i, :, lanes] = mm(planes[i, :, lanes], pick, ((1,), (0,))).astype(jnp.bfloat16)
            mirrored[2 + i, lanes, :] = mm(pick, planes[2 + i, lanes, :], ((1,), (0,))).astype(jnp.bfloat16)

    def both_ways(rows, base):
        straight = mm3s(rows, planes[base], planes[base + 1])
        turned = mm3s(rows, mirrored[base], mirrored[base + 1])
        slot = lax.broadcasted_iota(jnp.int32, straight.shape, 0) % slots
        return jnp.where(slot < half, straight, turned)

    def forward(p, first, count, follow=True):
        for i in range(first, first + count):
            finish(tau.at[p, i], x.at[p, i], own.at[p, i], recv1.at[p, i])

            if follow:
                @pl.when(p + 1 < PIECES)
                def _():
                    exchange_times(p + 1, i)

        v = x[p, first:first + count].reshape(count, lines, 2, 2, few, slots, points)
        rows = jnp.concatenate([v[:, :, h, part].reshape(count * lines * few * slots, points)
                                for part in range(2) for h in range(2)], axis=1)
        out = both_ways(rows, 0)
        for h in range(2):
            for part in range(2):
                lanes = slice(part * plane + h * points, part * plane + (h + 1) * points)
                zbuf[p, h, first:first + count, z, part] = out[:, lanes].reshape(count, lines, few, slots, points)

    def send_lines(p, h, first, count):
        for i in range(first, first + count):
            for level in (1, 2):
                @pl.when(z != level)
                def _():
                    remote(zbuf.at[p, h, i, z], zbuf.at[p, h, i, z], sendz.at[p, h], recvz.at[p, h],
                           level * members + d)

    def middle_work(p, h):
        sigma = jnp.where(z == 1, 1.0, -1.0).astype(jnp.float32)

        def forth(e, carry):
            i, f = e // few, lax.rem(e, few)
            cells = [(zbuf[p, h, i, k // lines, 0, k % lines, f], zbuf[p, h, i, k // lines, 1, k % lines, f])
                     for k in range(side)]
            for r, pair in enumerate(dft16(cells, 1)):
                for part in range(2):
                    v = pair[part]
                    t[r, e, part] = v
                    ts[r, e, part] = jnp.concatenate([v[half:], v[:half]], axis=0)
            return carry

        lax.fori_loop(0, entries, forth, 0)

        def one(c, carry):
            left, right = pair_ref[0, c], pair_ref[1, c]
            columns = []
            for n2 in range(4):
                cells = []
                for n1 in range(4):
                    r = 4 * n1 + n2
                    a, b = t[r, left], ts[mirror_ref[0, r], right]
                    cells.append((a[0] * b[0] - a[1] * b[1], a[0] * b[1] + a[1] * b[0]))
                columns.append(dft4(cells, -1))
            for i, pair in enumerate(dft16_half(columns, sigma)):
                for part in range(2):
                    chi[i // lines, p, h, c, part, i % lines] = pair[part]
            remote(chi.at[1 - mine, p, h, c], chi.at[1 - mine, p, h, c], send.at[1], recvc.at[p, c // group],
                   jnp.where(z == 1, 0, 3) * members + d)
            return carry

        lax.fori_loop(0, comps, one, 0)

    def backward(p, first, count):
        @pl.when(edge)
        def _():
            for n in range(first, first + count):
                drain(chi.at[mine, p, :, pl.ds(n * group, group)], recvc.at[p, n])

        v = chi[mine, p, :, first * group:(first + count) * group]
        rows = jnp.concatenate([v[h, :, part].reshape(count * group * lines * slots, points)
                                for part in range(2) for h in range(2)], axis=1)
        out = both_ways(rows, 2).reshape(count, group, lines, slots, 2 * plane)
        for q in range(lines):
            for h in range(2):
                for part in range(2):
                    lanes = slice(part * plane + h * points, part * plane + (h + 1) * points)
                    sent[p, first:first + count, 2 * q + h, part] = out[:, :, q, :, lanes]

        for n in range(first, first + count):
            @pl.when(p < kept)
            def _():
                exchange(sent.at[p, n], got.at[p, n], own.at[PIECES + p, 0], send.at[2], recv2.at[p])

            @pl.when(p >= kept)
            def _():
                exchange(sent.at[p, n], last.at[p - kept, n], own.at[PIECES + p, 0], send.at[2], recv2.at[p])

    span = 2 * GROUP * members * slots

    def frequency(pieces, first, depth):
        block = 2 * group
        high, low = back[0, pl.ds(first, depth)], back[1, pl.ds(first, depth)]
        for i in range(comps // block):
            chosen = slice(i * block, (i + 1) * block)
            rows = frequency_rows([[got.at[p, c // group, :, :, c % group] for p in pieces]
                                   for c in range(i * block, (i + 1) * block)])
            value = mm3s(rows, high, low)
            for part in range(2):
                acc[part, chosen] += value[:, part * freqs:(part + 1) * freqs].reshape(block, points, freqs)

    for i in range(HALVES):
        forward(0, i, 1, False)
        send_lines(0, 0, i, 1)
    loads[3].wait()
    for i in range(HALVES):
        times_of(STACKS[0], STACKS[1], i, values[i])
        exchange_times(1, i)
    send_lines(0, 1, 0, HALVES)
    for i in range(HALVES):
        times_of(STACKS[0] + STACKS[1], STACKS[2], i, values[i])
    acc[...] = jnp.zeros(acc.shape, jnp.float32)
    forward(1, 0, HALVES)
    loads[5].wait()

    def step(p, carry):
        for h in range(2):
            @pl.when(middle)
            def _():
                drain(zbuf.at[p, h, :, pl.ds(0, LEVELS - 1)], recvz.at[p, h])

            @pl.when(edge)
            def _():
                drain(zbuf.at[p, h, :, pl.ds(0, 2)], sendz.at[p, h])

            @pl.when(p + 1 < PIECES)
            def _():
                send_lines(p + 1, h, 0, HALVES)

            @pl.when(middle)
            def _():
                middle_work(p, h)

            @pl.when(middle if h == 1 else jnp.logical_and(edge, p > 0))
            def _():
                backward(p if h == 1 else p - 1, 0, PARTS)

        @pl.when(p + 2 < PIECES)
        def _():
            forward(p + 2, 0, HALVES)

        @pl.when(jnp.logical_and(lax.rem(p, GROUP) == GROUP - 1, p >= 2 * GROUP - 1))
        def _():
            m = p // GROUP - 1

            def arrived(q, carry):
                finish_parts(q, got.at[q])
                return carry

            lax.fori_loop(m * GROUP, (m + 1) * GROUP, arrived, 0)
            frequency([m * GROUP + g for g in range(GROUP)], m * span, span)

        return carry

    lax.fori_loop(0, PIECES, step, 0)
    end = PIECES - 1

    @pl.when(edge)
    def _():
        backward(end, 0, 1)
        backward(end, 1, 1)

    @pl.when(edge)
    def _():
        for n in range(2, PARTS):
            backward(end, n, 1)

    finish_parts(end - 1, got.at[end - 1])
    frequency([end - 1], back.shape[1] - span // GROUP, span // GROUP)
    store = pltpu.make_async_copy(acc, half_hbm, load.at[7])
    store.start()
    drain(tau.at[:, :, pl.ds(0, members - 1)], send.at[0])

    @pl.when(middle)
    def _():
        def gone(p, carry):
            for h in range(2):
                drain(zbuf.at[p, h, :, 0], sendz.at[p, h])
            return carry

        lax.fori_loop(0, PIECES, gone, 0)
        drain(chi.at[0], send.at[1])

    finish_parts(end, last.at[end - kept])
    drain(sent.at[:, :, pl.ds(0, members - 1)], send.at[2])
    store.wait()


def frequency_rows(blocks):
    rows = []
    for pieces in blocks:
        parts = []
        for ref in pieces:
            for part in range(2):
                v = ref[:, part]
                parts.append(v.reshape(v.shape[0] * v.shape[1], v.shape[2]))
        rows.append(jnp.concatenate(parts, axis=0).T)
    return jnp.concatenate(rows, axis=0)


def level_finish(x_hbm, b_hbm, half_hbm, o_hbm, x, b_ref, total, sem):
    points, freqs = total.shape[2:]
    group = x.shape[3]
    spans = [pl.ds(n * group, group) for n in range(PARTS)]
    ahead = [pltpu.make_async_copy(x_hbm.at[0, n], x.at[n], sem.at[0, n]) for n in range(PARTS)]
    halves = [pltpu.make_async_copy(half_hbm.at[:, span], total.at[:, span], sem.at[1, n])
              for n, span in enumerate(spans)]
    stores = [pltpu.make_async_copy(total.at[:, span], o_hbm.at[:, span], sem.at[2, n])
              for n, span in enumerate(spans)]
    tables = pltpu.make_async_copy(b_hbm, b_ref, sem.at[3, 0])
    for copy in [tables] + ahead + halves:
        copy.start()
    tables.wait()
    for n in range(PARTS):
        chosen = slice(n * group, (n + 1) * group)
        ahead[n].wait()
        value = mm3s(frequency_rows([[x.at[n, :, :, c]] for c in range(group)]), b_ref[0], b_ref[1])
        halves[n].wait()
        for part in range(2):
            total[part, chosen] += value[:, part * freqs:(part + 1) * freqs].reshape(group, points, freqs)
        stores[n].start()
    for store in stores:
        store.wait()


def level_local(devices, green, pair_table, mirror_map):
    entries, points, freqs = green.shape[1:]
    side = mirror_map.shape[1]
    plane = side * side
    comps = pair_table.shape[0]
    members = devices // LEVELS
    slots = freqs // (members * PIECES)
    lines = side // LEVELS
    few = entries // HALVES
    f32, bf16 = jnp.float32, jnp.bfloat16
    times = [piece_times(members, freqs, p) for p in range(PIECES)]
    edges = np.cumsum((0,) + STACKS)
    time_table = np.concatenate([stacked_time_table(np.concatenate(times[a:b]), freqs)
                                 for a, b in zip(edges[:-1], edges[1:])])
    plane_tables = np.stack(plane_table(side, 1.0) + plane_table(side, -1.0))
    groups = PIECES // GROUP
    early = np.concatenate([group_table(members, freqs, range(g * GROUP, (g + 1) * GROUP)) for g in range(groups - 1)]
                           + [group_table(members, freqs, [PIECES - 2])], axis=1)
    final = group_table(members, freqs, [PIECES - 1])
    kept = PIECES - 1
    hbm = pl.BlockSpec(memory_space=pl.ANY)
    exchanged = (PARTS, members, 2, comps // PARTS, slots, points)
    result = (2, comps, points, freqs)
    cells = (side, entries, 2, slots, points)
    half, last = pl.pallas_call(
        level_kernel,
        out_shape=[jax.ShapeDtypeStruct(result, f32), jax.ShapeDtypeStruct((1,) + exchanged, f32)],
        in_specs=[hbm] * 6,
        out_specs=[hbm, hbm],
        scratch_shapes=[
            pltpu.SMEM((2, comps), jnp.int32),
            pltpu.SMEM(mirror_map.shape, jnp.int32),
            pltpu.VMEM(green.shape, f32),
            pltpu.VMEM(time_table.shape, bf16),
            pltpu.VMEM(plane_tables.shape, bf16),
            pltpu.VMEM(early.shape, bf16),
            pltpu.VMEM(plane_tables.shape, bf16),
            pltpu.VMEM((PIECES, HALVES, members, 2, few, slots, points), f32),
            pltpu.VMEM((PIECES, HALVES, members, 2, few, slots, points), f32),
            pltpu.VMEM((PIECES, 2, HALVES, LEVELS, 2, lines, few, slots, points), f32),
            pltpu.VMEM(cells, f32),
            pltpu.VMEM(cells, f32),
            pltpu.VMEM((2, PIECES, 2, comps, 2, lines, slots, points), f32),
            pltpu.VMEM((PIECES,) + exchanged, f32),
            pltpu.VMEM((kept,) + exchanged, f32),
            pltpu.VMEM(result, f32),
            pltpu.SemaphoreType.DMA((10,)),
            pltpu.SemaphoreType.DMA((2 * PIECES, HALVES)),
            pltpu.SemaphoreType.DMA((3,)),
            pltpu.SemaphoreType.DMA((PIECES, 2)),
            pltpu.SemaphoreType.DMA((PIECES, HALVES)),
            pltpu.SemaphoreType.DMA((PIECES, 2)),
            pltpu.SemaphoreType.DMA((PIECES, PARTS)),
            pltpu.SemaphoreType.DMA((PIECES,)),
        ],
        compiler_params=pltpu.CompilerParams(
            vmem_limit_bytes=60 * 1024 * 1024, collective_id=0, has_side_effects=True
        ),
        cost_estimate=pl.CostEstimate(flops=18 * 10**9, bytes_accessed=16 * 2**20, transcendentals=0),
    )(pair_table.T, mirror_map, green, time_table, plane_tables, early)
    return pl.pallas_call(
        level_finish,
        out_shape=jax.ShapeDtypeStruct(result, f32),
        in_specs=[hbm, hbm, hbm],
        out_specs=hbm,
        scratch_shapes=[
            pltpu.VMEM(exchanged, f32),
            pltpu.VMEM(final.shape, bf16),
            pltpu.VMEM(result, f32),
            pltpu.SemaphoreType.DMA((4, PARTS)),
        ],
        compiler_params=pltpu.CompilerParams(vmem_limit_bytes=60 * 1024 * 1024),
        cost_estimate=pl.CostEstimate(flops=6 * 10**9, bytes_accessed=16 * 2**20, transcendentals=0),
    )(last, final, half)


def fits_levels(devices):
    return devices == 32


def solution(mesh):
    placed = (P("set", None, "kb", None), P(), P("set", None))
    devices = mesh.shape["kb"]
    return jax.shard_map(
        functools.partial(level_local if fits_levels(devices) else local, devices),
        mesh=mesh,
        in_specs=placed,
        out_specs=P("set", None, "kb", None),
        check_vma=False,
    )
```

```python
import functools

import numpy as np
import ml_dtypes
import jax
import jax.numpy as jnp
from jax import lax
from jax.experimental import pallas as pl
from jax.experimental.pallas import tpu as pltpu
from jax.sharding import PartitionSpec as P

CHUNKS = 2
SMEM = pl.BlockSpec(memory_space=pltpu.SMEM)


def split_np(table):
    table = table.astype(np.float32)
    high = table.astype(ml_dtypes.bfloat16)
    low = (table - high.astype(np.float32)).astype(ml_dtypes.bfloat16)
    return high, low


def split(x):
    high = x.astype(jnp.bfloat16)
    return high, (x - high.astype(jnp.float32)).astype(jnp.bfloat16)


def mm(a, b, dims):
    return lax.dot_general(a, b, (dims, ((), ())), preferred_element_type=jnp.float32)


def mm3(a, b, dims=((1,), (0,))):
    return mm(a[0], b[0], dims) + mm(a[1], b[0], dims) + mm(a[0], b[1], dims)


def owned_times(devices, freqs, chunk):
    per = freqs // (2 * CHUNKS * devices)
    first = chunk * (freqs // (2 * CHUNKS)) + np.arange(devices)[:, None] * per + np.arange(per)[None, :]
    return np.stack([first, freqs - 1 - first], axis=1).reshape(-1)


def time_tables(times, freqs):
    angle = ((2 * np.arange(freqs)[None, :] - freqs + 1) * (2 * times[:, None] + 1)) % (4 * freqs)
    angle = angle * (2 * np.pi / (4 * freqs))
    scale = freqs**-0.5
    return split_np(scale * np.cos(angle)) + split_np(scale * np.sin(angle))


def frequency_tables(times, freqs):
    angle = ((np.arange(freqs)[None, :] - freqs // 2) * (2 * times[:, None] + 1)) % (2 * freqs)
    angle = angle * (2 * np.pi / (2 * freqs))
    cos, sin = np.cos(angle) * freqs**-0.5, np.sin(angle) * freqs**-0.5
    return split_np(np.block([[cos, sin], [-sin, cos]]))


def plane_table(side, sign):
    index = np.arange(side * side)
    upper, lower = index // side, index % side
    angle = (upper[:, None] * upper[None, :] + lower[:, None] * lower[None, :]) % side * (2 * np.pi / side)
    scale = (side**3) ** -0.5
    cos, sin = scale * np.cos(angle), sign * scale * np.sin(angle)
    return split_np(np.block([[cos, sin], [-sin, cos]]))


def cadd(a, b):
    return a[0] + b[0], a[1] + b[1]


def csub(a, b):
    return a[0] - b[0], a[1] - b[1]


def dft4(a, sign):
    s02, d02 = cadd(a[0], a[2]), csub(a[0], a[2])
    s13, d13 = cadd(a[1], a[3]), csub(a[1], a[3])
    turned = (-d13[1], d13[0]) if sign > 0 else (d13[1], -d13[0])
    return [cadd(s02, s13), cadd(d02, turned), csub(s02, s13), csub(d02, turned)]


def twiddle(a, power, sign):
    if power == 0:
        return a
    if power == 4:
        return (-a[1], a[0]) if sign > 0 else (a[1], -a[0])
    if power in (2, 6):
        r = np.float32(np.sqrt(0.5))
        plus, minus = (a[0] + a[1]) * r, (a[0] - a[1]) * r
        if power == 2:
            return (minus, plus) if sign > 0 else (plus, -minus)
        return (-plus, minus) if sign > 0 else (-minus, -plus)
    c = np.float32(np.cos(2 * np.pi * power / 16))
    s = np.float32(sign * np.sin(2 * np.pi * power / 16))
    return a[0] * c - a[1] * s, a[0] * s + a[1] * c


def dft16(x, sign):
    columns = [dft4([x[4 * n1 + n2] for n1 in range(4)], sign) for n2 in range(4)]
    out = [None] * 16
    for k1 in range(4):
        row = dft4([twiddle(columns[n2][k1], n2 * k1, sign) for n2 in range(4)], sign)
        for k2 in range(4):
            out[k1 + 4 * k2] = row[k2]
    return out


def to_time(g_ref, table, o_ref, p):
    devices, _, entries, slots, points = o_ref.shape[1:]
    freqs = g_ref.shape[-1]
    cos, sin = (table[p, 0], table[p, 1]), (table[p, 2], table[p, 3])
    dims = ((1,), (1,))
    re = split(g_ref[0].reshape(entries * points, freqs))
    im = split(g_ref[1].reshape(entries * points, freqs))
    tau = (mm3(cos, re, dims) + mm3(sin, im, dims), mm3(cos, im, dims) - mm3(sin, re, dims))
    for part in range(2):
        for e in range(entries):
            o_ref[p, :, part, e] = tau[part][:, e * points:(e + 1) * points].reshape(devices, slots, points)


def bubble(pair_ref, mirror_ref, x_ref, ahead, mirrored, inverse, o_ref, y, g, gm, chi, p):
    devices, _, entries, slots, points = x_ref.shape[1:]
    side = y.shape[0]
    plane = side * side
    halves = devices // side
    comps = o_ref.shape[3]

    def forth(e, carry):
        for h in range(halves):
            cells = [(x_ref[p, k * halves + h, 0, e], x_ref[p, k * halves + h, 1, e]) for k in range(side)]
            for k, (re, im) in enumerate(dft16(cells, 1)):
                y[k, e, :, h * points:(h + 1) * points] = re
                y[k, e, :, plane + h * points:plane + (h + 1) * points] = im
        return carry

    lax.fori_loop(0, entries, forth, 0)
    rows = split(y[...].reshape(side * entries * slots, 2 * plane))
    g[...] = mm3(rows, (ahead[0], ahead[1])).reshape(g.shape)
    other = mm3(rows, (mirrored[0], mirrored[1])).reshape(side * entries, slots, 2 * plane)
    other = jnp.concatenate([other[:, slots // 2:], other[:, :slots // 2]], axis=1)
    gm[...] = other.reshape(gm.shape)

    def one(c, carry):
        left, right = pair_ref[0, c], pair_ref[1, c]
        for r in range(side):
            a = g[r, left]
            b = gm[mirror_ref[0, r], right]
            ar, ai, br, bi = a[:, :plane], a[:, plane:], b[:, :plane], b[:, plane:]
            chi[c, r, :, :plane] = ar * br - ai * bi
            chi[c, r, :, plane:] = ar * bi + ai * br
        return carry

    lax.fori_loop(0, comps, one, 0)
    rows = split(chi[...].reshape(comps * side * slots, 2 * plane))
    chi[...] = mm3(rows, (inverse[0], inverse[1])).reshape(chi.shape)

    def back(c, carry):
        for h in range(halves):
            lanes = slice(h * points, (h + 1) * points)
            high = slice(plane + h * points, plane + (h + 1) * points)
            cells = [(chi[c, r, :, lanes], chi[c, r, :, high]) for r in range(side)]
            for q, (re, im) in enumerate(dft16(cells, -1)):
                o_ref[p, q * halves + h, 0, c] = re
                o_ref[p, q * halves + h, 1, c] = im
        return carry

    lax.fori_loop(0, comps, back, 0)


def main_kernel(pair_ref, mirror_ref, green_hbm, time_hbm, plane_hbm, back_hbm, half_hbm, last,
                green, table, planes, back, mirrored, tau, x, y, g, gm, chi, sent, got, acc,
                load, own, send, recv):
    devices = tau.shape[1]
    side = y.shape[0]
    plane = side * side
    me = lax.axis_index("kb")
    loads = [pltpu.make_async_copy(src, dst, load.at[i])
             for i, (src, dst) in enumerate([(time_hbm, table), (plane_hbm, planes), (back_hbm, back),
                                       (green_hbm, green)])]
    for i in (3, 0, 1, 2):
        loads[i].start()
    barrier = pltpu.get_barrier_semaphore()

    def greet(s, carry):
        pl.semaphore_signal(barrier, inc=1, device_id={"kb": lax.rem(me + s, devices)},
                            device_id_type=pl.DeviceIdType.MESH)
        return carry

    lax.fori_loop(1, devices, greet, 0)

    def partner(shift):
        total, bit = 0, 1
        while bit < devices:
            total += bit * lax.rem(me // bit + shift // bit, 2)
            bit *= 2
        return total

    def exchange(src, dst, n):
        pltpu.make_async_copy(src.at[me], dst.at[me], own.at[n]).start()

        def one(i, carry):
            other = partner(i // 4 + devices // 4 * lax.rem(i + 2, 4))
            pltpu.make_async_remote_copy(
                src_ref=src.at[other], dst_ref=dst.at[me], send_sem=send.at[n], recv_sem=recv.at[n],
                device_id={"kb": other}, device_id_type=pl.DeviceIdType.MESH,
            ).start()
            return carry

        lax.fori_loop(0, 2, one, 0)
        lax.fori_loop(3, devices, one, 0)

    def finish(ref, sem):
        part = ref.at[pl.ds(0, devices - 1)]
        pltpu.make_async_copy(part, part, sem).wait()

    loads[3].wait()
    loads[0].wait()
    for p in range(CHUNKS):
        to_time(green, table, tau, p)
        if p == 0:
            pl.semaphore_wait(barrier, devices - 1)
        exchange(tau.at[p], x.at[p], p)
    loads[1].wait()
    lane = lax.broadcasted_iota(jnp.int32, (plane, plane), 1)
    ry, rz = lane // side, lane % side
    target = (mirror_ref[1, 0] + side - ry) % side * side + (mirror_ref[2, 0] + side - rz) % side
    pick = (lax.broadcasted_iota(jnp.int32, (plane, plane), 0) == target).astype(jnp.float32).astype(jnp.bfloat16)
    for i in range(2):
        for part in range(2):
            lanes = slice(part * plane, (part + 1) * plane)
            mirrored[i, :, lanes] = mm(planes[i, :, lanes], pick, ((1,), (0,))).astype(jnp.bfloat16)
    landing = [got, last]
    for p in range(CHUNKS):
        pltpu.make_async_copy(tau.at[p, me], x.at[p, me], own.at[p]).wait()
        finish(x.at[p], recv.at[p])
        bubble(pair_ref, mirror_ref, x, planes.at[0:2], mirrored, planes.at[2:4], sent, y, g, gm, chi, p)
        exchange(sent.at[p], landing[p], CHUNKS + p)
    pltpu.make_async_copy(sent.at[0, me], got.at[me], own.at[CHUNKS]).wait()
    finish(got, recv.at[CHUNKS])
    loads[2].wait()
    comps = got.shape[2]
    block = comps // 2
    for i in range(2):
        chosen = slice(i * block, (i + 1) * block)
        value = to_frequency(got.at[:, :, chosen], back)
        for part in range(2):
            acc[part, chosen] = value[part]
    store = pltpu.make_async_copy(acc, half_hbm, load.at[4])
    store.start()
    for p in range(CHUNKS):
        finish(tau.at[p], send.at[p])
        finish(sent.at[p], send.at[CHUNKS + p])
    store.wait()
    pltpu.make_async_copy(sent.at[1, me], last.at[me], own.at[CHUNKS + 1]).wait()
    finish(last, recv.at[CHUNKS + 1])


def to_frequency(x_ref, b_ref):
    devices, _, block, slots, points = x_ref.shape
    freqs = b_ref.shape[-1] // 2
    rows = []
    for c in range(block):
        parts = [x_ref[:, part, c].reshape(devices * slots, points).T for part in range(2)]
        rows.append(jnp.concatenate(parts, axis=1))
    value = mm3(split(jnp.concatenate(rows, axis=0)), (b_ref[0], b_ref[1]))
    return [value[:, part * freqs:(part + 1) * freqs].reshape(block, points, freqs) for part in range(2)]


def finish_kernel(x_ref, b_ref, half_ref, o_ref):
    value = to_frequency(x_ref, b_ref)
    for part in range(2):
        o_ref[part] = half_ref[part] + value[part]


def local(devices, green, pair_table, mirror_map):
    entries, points, freqs = green.shape[1:]
    side = mirror_map.shape[1]
    plane = side * side
    comps = pair_table.shape[0]
    slots = freqs // (devices * CHUNKS)
    f32, bf16 = jnp.float32, jnp.bfloat16
    times = [owned_times(devices, freqs, p) for p in range(CHUNKS)]
    time_table = np.stack([np.stack(time_tables(t, freqs)) for t in times])
    plane_tables = np.stack(plane_table(side, 1.0) + plane_table(side, -1.0))
    frequency_table = [np.stack(frequency_tables(t, freqs)) for t in times]
    hbm = pl.BlockSpec(memory_space=pl.ANY)
    cells = (side, entries, slots, 2 * plane)
    exchanged = (devices, 2, comps, slots, points)
    result = (2, comps, points, freqs)
    half, last = pl.pallas_call(
        main_kernel,
        out_shape=[jax.ShapeDtypeStruct(result, f32), jax.ShapeDtypeStruct(exchanged, f32)],
        in_specs=[SMEM, SMEM, hbm, hbm, hbm, hbm],
        out_specs=[hbm, hbm],
        scratch_shapes=[
            pltpu.VMEM(green.shape, f32),
            pltpu.VMEM(time_table.shape, bf16),
            pltpu.VMEM(plane_tables.shape, bf16),
            pltpu.VMEM(frequency_table[0].shape, bf16),
            pltpu.VMEM((2, 2 * plane, 2 * plane), bf16),
            pltpu.VMEM((CHUNKS, devices, 2, entries, slots, points), f32),
            pltpu.VMEM((CHUNKS, devices, 2, entries, slots, points), f32),
            pltpu.VMEM(cells, f32),
            pltpu.VMEM(cells, f32),
            pltpu.VMEM(cells, f32),
            pltpu.VMEM((comps,) + (side, slots, 2 * plane), f32),
            pltpu.VMEM((CHUNKS,) + exchanged, f32),
            pltpu.VMEM(exchanged, f32),
            pltpu.VMEM(result, f32),
            pltpu.SemaphoreType.DMA((5,)),
            pltpu.SemaphoreType.DMA((2 * CHUNKS,)),
            pltpu.SemaphoreType.DMA((2 * CHUNKS,)),
            pltpu.SemaphoreType.DMA((2 * CHUNKS,)),
        ],
        compiler_params=pltpu.CompilerParams(
            vmem_limit_bytes=60 * 1024 * 1024, collective_id=0, has_side_effects=True
        ),
        cost_estimate=pl.CostEstimate(flops=18 * 10**9, bytes_accessed=16 * 2**20, transcendentals=0),
    )(pair_table.T, mirror_map, green, time_table, plane_tables, frequency_table[0])
    block = comps // 4
    whole = pl.BlockSpec((2, block, points, freqs), lambda i: (0, i, 0, 0))
    return pl.pallas_call(
        finish_kernel,
        grid=(comps // block,),
        out_shape=jax.ShapeDtypeStruct(result, f32),
        in_specs=[
            pl.BlockSpec((devices, 2, block, slots, points), lambda i: (0, 0, i, 0, 0)),
            pl.BlockSpec(frequency_table[1].shape, lambda i: (0, 0, 0)),
            whole,
        ],
        out_specs=whole,
        compiler_params=pltpu.CompilerParams(vmem_limit_bytes=58 * 1024 * 1024),
        cost_estimate=pl.CostEstimate(flops=6 * 10**9, bytes_accessed=16 * 2**20, transcendentals=0),
    )(last, frequency_table[1], half)


LEVELS = 4
PIECES = 8
STACKS = (1, 1, 6)
PARTS = 4
HALVES = 2
GROUP = 2


def piece_times(members, freqs, piece):
    per = freqs // (2 * PIECES * members)
    first = piece * (freqs // (2 * PIECES)) + np.arange(members)[:, None] * per + np.arange(per)[None, :]
    return np.stack([first, freqs - 1 - first], axis=1).reshape(-1)


def stacked_time_table(times, freqs):
    cos_high, cos_low, sin_high, sin_low = time_tables(times, freqs)
    return np.concatenate([cos_high, sin_high, cos_low, sin_low])


def group_table(members, freqs, pieces):
    rows = []
    for piece in pieces:
        times = piece_times(members, freqs, piece)
        angle = ((np.arange(freqs)[None, :] - freqs // 2) * (2 * times[:, None] + 1)) % (2 * freqs)
        angle = angle * (2 * np.pi / (2 * freqs))
        cos, sin = np.cos(angle) * freqs**-0.5, np.sin(angle) * freqs**-0.5
        rows.append(np.block([[cos, sin], [-sin, cos]]))
    return np.stack(split_np(np.concatenate(rows)))


def mm3s(rows, high, low):
    m = rows.shape[0]
    a, b = split(rows)
    both = mm(jnp.concatenate([a, b], axis=0), high, ((1,), (0,)))
    return both[:m] + both[m:] + mm(a, low, ((1,), (0,)))


def dft16_half(columns, sigma):
    out = [None] * 8
    for k1 in range(4):
        a = [twiddle(columns[n2][k1], n2 * k1, -1) for n2 in range(4)]
        s02, d02 = cadd(a[0], a[2]), csub(a[0], a[2])
        s13, d13 = cadd(a[1], a[3]), csub(a[1], a[3])
        out[k1] = (s02[0] + sigma * s13[0], s02[1] + sigma * s13[1])
        out[4 + k1] = (d02[0] + sigma * d13[1], d02[1] - sigma * d13[0])
    return out


def level_kernel(pair_hbm, mirror_hbm, green_hbm, time_hbm, plane_hbm, back_hbm, half_hbm, last,
                 pair_ref, mirror_ref, green, table, planes, back, mirrored, tau, x, zbuf, t, ts, chi, sent, got, acc,
                 load, own, send, sendz, recv1, recvz, recvc, recv2):
    members = tau.shape[2]
    entries = green.shape[1]
    few, slots, points = tau.shape[4:]
    side = t.shape[0]
    lines = side // LEVELS
    plane = side * side
    comps = sent.shape[1] * sent.shape[4]
    group = sent.shape[4]
    freqs = green.shape[-1]
    kept = got.shape[0]
    me = lax.axis_index("kb")
    z, d = me // members, lax.rem(me, members)
    middle = jnp.logical_or(z == 1, z == 2)
    edge = jnp.logical_not(middle)
    mine = lax.rem(z, 2)
    half = slots // 2

    start = 4 * members * slots * STACKS[0]
    pairs = [(pair_hbm, pair_ref), (mirror_hbm, mirror_ref)]
    small = [pltpu.make_async_copy(src, dst, load.at[8 + i]) for i, (src, dst) in enumerate(pairs)]
    pairs = [(green_hbm.at[:, pl.ds(i * few, few)], green.at[:, pl.ds(i * few, few)]) for i in range(HALVES)]
    pairs += [(time_hbm.at[pl.ds(0, start)], table.at[pl.ds(0, start)]),
              (time_hbm.at[pl.ds(start, table.shape[0] - start)], table.at[pl.ds(start, table.shape[0] - start)]),
              (plane_hbm, planes), (back_hbm, back)]
    loads = [pltpu.make_async_copy(src, dst, load.at[i]) for i, (src, dst) in enumerate(pairs)]
    for i in (0, 2, 1):
        loads[i].start()
    for copy in small:
        copy.start()
    barrier = pltpu.get_barrier_semaphore()

    def greet(other):
        pl.semaphore_signal(barrier, inc=1, device_id={"kb": other}, device_id_type=pl.DeviceIdType.MESH)

    def greet_member(s, carry):
        greet(z * members + lax.rem(d + s, members))
        return carry

    lax.fori_loop(1, members, greet_member, 0)
    for s in range(1, LEVELS):
        greet(lax.rem(z + s, LEVELS) * members + d)

    def partner(shift):
        total, bit = 0, 1
        while bit < members:
            total += bit * lax.rem(d // bit + shift // bit, 2)
            bit *= 2
        return total

    def remote(src, dst, send_sem, recv_sem, other):
        pltpu.make_async_remote_copy(
            src_ref=src, dst_ref=dst, send_sem=send_sem, recv_sem=recv_sem,
            device_id={"kb": other}, device_id_type=pl.DeviceIdType.MESH,
        ).start()

    def exchange(src, dst, own_sem, send_sem, recv_sem):
        pltpu.make_async_copy(src.at[d], dst.at[d], own_sem).start()

        def one(i, carry):
            other = partner(members - i)
            remote(src.at[other], dst.at[d], send_sem, recv_sem, z * members + other)
            return carry

        for i in range(1, members):
            one(i, 0)

    def drain(ref, sem):
        pltpu.make_async_copy(ref, ref, sem).wait()

    def finish(src, dst, own_sem, recv_sem):
        pltpu.make_async_copy(src.at[d], dst.at[d], own_sem).wait()
        drain(dst.at[pl.ds(0, members - 1)], recv_sem)

    def finish_parts(p, dst):
        pltpu.make_async_copy(sent.at[p, :, d], dst.at[:, d], own.at[PIECES + p, 0]).wait()
        drain(dst.at[:, pl.ds(0, members - 1)], recv2.at[p])

    dims = ((1,), (1,))

    def split_entries(i):
        return [split(green[part, i * few:(i + 1) * few].reshape(few * points, freqs)) for part in range(2)]

    def times_of(first, count, i, values):
        times = count * members * slots
        base = 4 * members * slots * first
        stack = table[base:base + 4 * times]
        outs = []
        for value in values:
            a = mm(stack, value[0], dims)
            outs.append(a[:2 * times] + a[2 * times:] + mm(stack[:2 * times], value[1], dims))
        both = (outs[0][:times] + outs[1][times:], outs[1][:times] - outs[0][times:])
        for part in range(2):
            for e in range(few):
                tau[first:first + count, i, :, part, e] = both[part][:, e * points:(e + 1) * points].reshape(
                    count, members, slots, points)

    def exchange_times(p, i):
        exchange(tau.at[p, i], x.at[p, i], own.at[p, i], send.at[0], recv1.at[p, i])

    loads[0].wait()
    loads[2].wait()
    values = []
    for i in range(HALVES):
        if i == 1:
            loads[1].wait()
        values.append(split_entries(i))
        times_of(0, STACKS[0], i, values[i])
        if i == 0:
            pl.semaphore_wait(barrier, members - 1 + LEVELS - 1)
            for n in range(3, len(loads)):
                loads[n].start()
        exchange_times(0, i)
    loads[4].wait()
    for copy in small:
        copy.wait()
    lane = lax.broadcasted_iota(jnp.int32, (plane, plane), 1)
    ry, rz = lane // side, lane % side
    target = (mirror_ref[1, 0] + side - ry) % side * side + (mirror_ref[2, 0] + side - rz) % side
    pick = (lax.broadcasted_iota(jnp.int32, (plane, plane), 0) == target).astype(jnp.float32).astype(jnp.bfloat16)
    for i in range(2):
        for part in range(2):
            lanes = slice(part * plane, (part + 1) * plane)
            mirrored[i, :, lanes] = mm(planes[i, :, lanes], pick, ((1,), (0,))).astype(jnp.bfloat16)
            mirrored[2 + i, lanes, :] = mm(pick, planes[2 + i, lanes, :], ((1,), (0,))).astype(jnp.bfloat16)

    def both_ways(rows, base):
        straight = mm3s(rows, planes[base], planes[base + 1])
        turned = mm3s(rows, mirrored[base], mirrored[base + 1])
        slot = lax.broadcasted_iota(jnp.int32, straight.shape, 0) % slots
        return jnp.where(slot < half, straight, turned)

    def forward(p, first, count, follow=True):
        for i in range(first, first + count):
            finish(tau.at[p, i], x.at[p, i], own.at[p, i], recv1.at[p, i])

            if follow:
                @pl.when(p + 1 < PIECES)
                def _():
                    exchange_times(p + 1, i)

        v = x[p, first:first + count].reshape(count, lines, 2, 2, few, slots, points)
        rows = jnp.concatenate([v[:, :, h, part].reshape(count * lines * few * slots, points)
                                for part in range(2) for h in range(2)], axis=1)
        out = both_ways(rows, 0)
        for h in range(2):
            for part in range(2):
                lanes = slice(part * plane + h * points, part * plane + (h + 1) * points)
                zbuf[p, h, first:first + count, z, part] = out[:, lanes].reshape(count, lines, few, slots, points)

    def send_lines(p, h, first, count):
        for i in range(first, first + count):
            for level in (1, 2):
                @pl.when(z != level)
                def _():
                    remote(zbuf.at[p, h, i, z], zbuf.at[p, h, i, z], sendz.at[p, h], recvz.at[p, h],
                           level * members + d)

    def middle_work(p, h):
        sigma = jnp.where(z == 1, 1.0, -1.0).astype(jnp.float32)

        def forth(e, carry):
            i, f = e // few, lax.rem(e, few)
            cells = [(zbuf[p, h, i, k // lines, 0, k % lines, f], zbuf[p, h, i, k // lines, 1, k % lines, f])
                     for k in range(side)]
            for r, pair in enumerate(dft16(cells, 1)):
                for part in range(2):
                    v = pair[part]
                    t[r, e, part] = v
                    ts[r, e, part] = jnp.concatenate([v[half:], v[:half]], axis=0)
            return carry

        lax.fori_loop(0, entries, forth, 0)

        def one(c, carry):
            left, right = pair_ref[0, c], pair_ref[1, c]
            columns = []
            for n2 in range(4):
                cells = []
                for n1 in range(4):
                    r = 4 * n1 + n2
                    a, b = t[r, left], ts[mirror_ref[0, r], right]
                    cells.append((a[0] * b[0] - a[1] * b[1], a[0] * b[1] + a[1] * b[0]))
                columns.append(dft4(cells, -1))
            for i, pair in enumerate(dft16_half(columns, sigma)):
                for part in range(2):
                    chi[i // lines, p, h, c, part, i % lines] = pair[part]
            remote(chi.at[1 - mine, p, h, c], chi.at[1 - mine, p, h, c], send.at[1], recvc.at[p, c // group],
                   jnp.where(z == 1, 0, 3) * members + d)
            return carry

        lax.fori_loop(0, comps, one, 0)

    def backward(p, first, count):
        @pl.when(edge)
        def _():
            for n in range(first, first + count):
                drain(chi.at[mine, p, :, pl.ds(n * group, group)], recvc.at[p, n])

        v = chi[mine, p, :, first * group:(first + count) * group]
        rows = jnp.concatenate([v[h, :, part].reshape(count * group * lines * slots, points)
                                for part in range(2) for h in range(2)], axis=1)
        out = both_ways(rows, 2).reshape(count, group, lines, slots, 2 * plane)
        for q in range(lines):
            for h in range(2):
                for part in range(2):
                    lanes = slice(part * plane + h * points, part * plane + (h + 1) * points)
                    sent[p, first:first + count, 2 * q + h, part] = out[:, :, q, :, lanes]

        for n in range(first, first + count):
            @pl.when(p < kept)
            def _():
                exchange(sent.at[p, n], got.at[p, n], own.at[PIECES + p, 0], send.at[2], recv2.at[p])

            @pl.when(p >= kept)
            def _():
                exchange(sent.at[p, n], last.at[p - kept, n], own.at[PIECES + p, 0], send.at[2], recv2.at[p])

    span = 2 * GROUP * members * slots

    def frequency(pieces, first, depth):
        block = 2 * group
        high, low = back[0, pl.ds(first, depth)], back[1, pl.ds(first, depth)]
        for i in range(comps // block):
            chosen = slice(i * block, (i + 1) * block)
            rows = frequency_rows([[got.at[p, c // group, :, :, c % group] for p in pieces]
                                   for c in range(i * block, (i + 1) * block)])
            value = mm3s(rows, high, low)
            for part in range(2):
                acc[part, chosen] += value[:, part * freqs:(part + 1) * freqs].reshape(block, points, freqs)

    for i in range(HALVES):
        forward(0, i, 1, False)
        send_lines(0, 0, i, 1)
    loads[3].wait()
    for i in range(HALVES):
        times_of(STACKS[0], STACKS[1], i, values[i])
        exchange_times(1, i)
    send_lines(0, 1, 0, HALVES)
    for i in range(HALVES):
        times_of(STACKS[0] + STACKS[1], STACKS[2], i, values[i])
    acc[...] = jnp.zeros(acc.shape, jnp.float32)
    forward(1, 0, HALVES)
    loads[5].wait()

    def step(p, carry):
        for h in range(2):
            @pl.when(middle)
            def _():
                drain(zbuf.at[p, h, :, pl.ds(0, LEVELS - 1)], recvz.at[p, h])

            @pl.when(edge)
            def _():
                drain(zbuf.at[p, h, :, pl.ds(0, 2)], sendz.at[p, h])

            @pl.when(p + 1 < PIECES)
            def _():
                send_lines(p + 1, h, 0, HALVES)

            @pl.when(middle)
            def _():
                middle_work(p, h)

            @pl.when(middle if h == 1 else jnp.logical_and(edge, p > 0))
            def _():
                backward(p if h == 1 else p - 1, 0, PARTS)

        @pl.when(p + 2 < PIECES)
        def _():
            forward(p + 2, 0, HALVES)

        @pl.when(jnp.logical_and(lax.rem(p, GROUP) == GROUP - 1, p >= 2 * GROUP - 1))
        def _():
            m = p // GROUP - 1

            def arrived(q, carry):
                finish_parts(q, got.at[q])
                return carry

            lax.fori_loop(m * GROUP, (m + 1) * GROUP, arrived, 0)
            frequency([m * GROUP + g for g in range(GROUP)], m * span, span)

        return carry

    lax.fori_loop(0, PIECES, step, 0)
    end = PIECES - 1

    @pl.when(edge)
    def _():
        backward(end, 0, 1)
        backward(end, 1, 1)

    @pl.when(edge)
    def _():
        for n in range(2, PARTS):
            backward(end, n, 1)

    finish_parts(end - 1, got.at[end - 1])
    frequency([end - 1], back.shape[1] - span // GROUP, span // GROUP)
    store = pltpu.make_async_copy(acc, half_hbm, load.at[7])
    store.start()
    drain(tau.at[:, :, pl.ds(0, members - 1)], send.at[0])

    @pl.when(middle)
    def _():
        def gone(p, carry):
            for h in range(2):
                drain(zbuf.at[p, h, :, 0], sendz.at[p, h])
            return carry

        lax.fori_loop(0, PIECES, gone, 0)
        drain(chi.at[0], send.at[1])

    finish_parts(end, last.at[end - kept])
    drain(sent.at[:, :, pl.ds(0, members - 1)], send.at[2])
    store.wait()


def frequency_rows(blocks):
    rows = []
    for pieces in blocks:
        parts = []
        for ref in pieces:
            for part in range(2):
                v = ref[:, part]
                parts.append(v.reshape(v.shape[0] * v.shape[1], v.shape[2]))
        rows.append(jnp.concatenate(parts, axis=0).T)
    return jnp.concatenate(rows, axis=0)


def level_finish(x_hbm, b_hbm, half_hbm, o_hbm, x, b_ref, total, sem):
    points, freqs = total.shape[2:]
    group = x.shape[3]
    spans = [pl.ds(n * group, group) for n in range(PARTS)]
    ahead = [pltpu.make_async_copy(x_hbm.at[0, n], x.at[n], sem.at[0, n]) for n in range(PARTS)]
    halves = [pltpu.make_async_copy(half_hbm.at[:, span], total.at[:, span], sem.at[1, n])
              for n, span in enumerate(spans)]
    stores = [pltpu.make_async_copy(total.at[:, span], o_hbm.at[:, span], sem.at[2, n])
              for n, span in enumerate(spans)]
    tables = pltpu.make_async_copy(b_hbm, b_ref, sem.at[3, 0])
    for copy in [tables] + ahead + halves:
        copy.start()
    tables.wait()
    for n in range(PARTS):
        chosen = slice(n * group, (n + 1) * group)
        ahead[n].wait()
        value = mm3s(frequency_rows([[x.at[n, :, :, c]] for c in range(group)]), b_ref[0], b_ref[1])
        halves[n].wait()
        for part in range(2):
            total[part, chosen] += value[:, part * freqs:(part + 1) * freqs].reshape(group, points, freqs)
        stores[n].start()
    for store in stores:
        store.wait()


def level_local(devices, green, pair_table, mirror_map):
    entries, points, freqs = green.shape[1:]
    side = mirror_map.shape[1]
    plane = side * side
    comps = pair_table.shape[0]
    members = devices // LEVELS
    slots = freqs // (members * PIECES)
    lines = side // LEVELS
    few = entries // HALVES
    f32, bf16 = jnp.float32, jnp.bfloat16
    times = [piece_times(members, freqs, p) for p in range(PIECES)]
    edges = np.cumsum((0,) + STACKS)
    time_table = np.concatenate([stacked_time_table(np.concatenate(times[a:b]), freqs)
                                 for a, b in zip(edges[:-1], edges[1:])])
    plane_tables = np.stack(plane_table(side, 1.0) + plane_table(side, -1.0))
    groups = PIECES // GROUP
    early = np.concatenate([group_table(members, freqs, range(g * GROUP, (g + 1) * GROUP)) for g in range(groups - 1)]
                           + [group_table(members, freqs, [PIECES - 2])], axis=1)
    final = group_table(members, freqs, [PIECES - 1])
    kept = PIECES - 1
    hbm = pl.BlockSpec(memory_space=pl.ANY)
    exchanged = (PARTS, members, 2, comps // PARTS, slots, points)
    result = (2, comps, points, freqs)
    cells = (side, entries, 2, slots, points)
    half, last = pl.pallas_call(
        level_kernel,
        out_shape=[jax.ShapeDtypeStruct(result, f32), jax.ShapeDtypeStruct((1,) + exchanged, f32)],
        in_specs=[hbm] * 6,
        out_specs=[hbm, hbm],
        scratch_shapes=[
            pltpu.SMEM((2, comps), jnp.int32),
            pltpu.SMEM(mirror_map.shape, jnp.int32),
            pltpu.VMEM(green.shape, f32),
            pltpu.VMEM(time_table.shape, bf16),
            pltpu.VMEM(plane_tables.shape, bf16),
            pltpu.VMEM(early.shape, bf16),
            pltpu.VMEM(plane_tables.shape, bf16),
            pltpu.VMEM((PIECES, HALVES, members, 2, few, slots, points), f32),
            pltpu.VMEM((PIECES, HALVES, members, 2, few, slots, points), f32),
            pltpu.VMEM((PIECES, 2, HALVES, LEVELS, 2, lines, few, slots, points), f32),
            pltpu.VMEM(cells, f32),
            pltpu.VMEM(cells, f32),
            pltpu.VMEM((2, PIECES, 2, comps, 2, lines, slots, points), f32),
            pltpu.VMEM((PIECES,) + exchanged, f32),
            pltpu.VMEM((kept,) + exchanged, f32),
            pltpu.VMEM(result, f32),
            pltpu.SemaphoreType.DMA((10,)),
            pltpu.SemaphoreType.DMA((2 * PIECES, HALVES)),
            pltpu.SemaphoreType.DMA((3,)),
            pltpu.SemaphoreType.DMA((PIECES, 2)),
            pltpu.SemaphoreType.DMA((PIECES, HALVES)),
            pltpu.SemaphoreType.DMA((PIECES, 2)),
            pltpu.SemaphoreType.DMA((PIECES, PARTS)),
            pltpu.SemaphoreType.DMA((PIECES,)),
        ],
        compiler_params=pltpu.CompilerParams(
            vmem_limit_bytes=60 * 1024 * 1024, collective_id=0, has_side_effects=True
        ),
        cost_estimate=pl.CostEstimate(flops=18 * 10**9, bytes_accessed=16 * 2**20, transcendentals=0),
    )(pair_table.T, mirror_map, green, time_table, plane_tables, early)
    return pl.pallas_call(
        level_finish,
        out_shape=jax.ShapeDtypeStruct(result, f32),
        in_specs=[hbm, hbm, hbm],
        out_specs=hbm,
        scratch_shapes=[
            pltpu.VMEM(exchanged, f32),
            pltpu.VMEM(final.shape, bf16),
            pltpu.VMEM(result, f32),
            pltpu.SemaphoreType.DMA((4, PARTS)),
        ],
        compiler_params=pltpu.CompilerParams(vmem_limit_bytes=60 * 1024 * 1024),
        cost_estimate=pl.CostEstimate(flops=6 * 10**9, bytes_accessed=16 * 2**20, transcendentals=0),
    )(last, final, half)


def fits_levels(devices):
    return devices == 32


def solution(mesh):
    placed = (P("set", None, "kb", None), P(), P("set", None))
    devices = mesh.shape["kb"]
    return jax.shard_map(
        functools.partial(level_local if fits_levels(devices) else local, devices),
        mesh=mesh,
        in_specs=placed,
        out_specs=P("set", None, "kb", None),
        check_vma=False,
    )
```
